512 devices in a mesh: section: 16 (over x, y_hi, core), tp: 32 (over y_lo, z).
Axes of the slice: x: 4, y: 8 (y_hi: 2, y_lo: 4; y = y_hi * 4 + y_lo), z: 8, core: 2. Of those that a mesh axis runs over, the one named last changes fastest.
Arguments:
- hidden: bfloat16 [208, 4608], P('section', 'tp'), as said below
- head_weight: bfloat16 [4608, 131072], P(None, ('section', 'tp')), as said below
- targets: int32 [208], replicated, may hold values from 0 to 131071
Outputs:
- loss: float32 [], replicated
- head_grad: bfloat16 [4608, 131072], P(None, ('section', 'tp'))
- hidden_grad: bfloat16 [208, 4608], P('section', 'tp')
The draws below stay inside these ranges and needn't reach their ends.
Inputs may be any that keep to these rules, and one draw needn't show every extreme that they name: hidden is drawn as independent normal entries. head_weight has entries of order 3 / sqrt(4608) and may be aligned with rows of hidden.
All inputs are finite; a program needn't handle non-finite values.
Results may differ from the reference program's by a relative error of at most 0.0051.
Values may be sent and summed in bfloat16 or wider, within the bound.
A program may use at most 64 MiB of HBM per device.

```python
import jax
import jax.numpy as jnp
from jax import lax

D = 4608
TOKENS = 208
VOCAB = 131072


def shared_states(key):
    return jax.random.normal(key, (TOKENS, D), jnp.float32)


def draw_hidden(key, part):
    states = shared_states(key)
    return states.astype(jnp.bfloat16)


def draw_head_weight(key, part):
    key = jax.random.fold_in(key, 7)
    weight = jax.random.normal(key, (D, VOCAB), jnp.float32) * (3.0 / jnp.sqrt(jnp.float32(D)))
    return weight.astype(jnp.bfloat16)


def place_ends(entries, key, least, largest):
    spot = [jax.random.randint(jax.random.fold_in(key, axis), (), 0, length) for axis, length in enumerate(entries.shape)]
    widest = entries.shape.index(max(entries.shape))
    beside = spot[:widest] + [(spot[widest] + 1) % entries.shape[widest]] + spot[widest + 1:]
    return entries.at[tuple(spot)].set(least).at[tuple(beside)].set(largest)


def setup_inputs(seed: int = 0) -> dict:
    streams_of = jax.random.split(jax.random.key(seed), 4)
    hidden = draw_hidden(jax.random.fold_in(streams_of[3], 71), 0)
    head_weight = draw_head_weight(jax.random.fold_in(streams_of[3], 71), 0)
    targets = place_ends(jax.random.randint(streams_of[2], (TOKENS,), 0, VOCAB), jax.random.fold_in(streams_of[2], 1), 0, VOCAB - 1).astype(jnp.int32)
    return dict(hidden=hidden, head_weight=head_weight, targets=targets)


def reference(hidden, head_weight, targets):
    logits = jnp.dot(hidden, head_weight, preferred_element_type=jnp.float32)
    top = jnp.max(logits, axis=1)
    shifted = jnp.exp(logits - top[:, None])
    total = jnp.sum(shifted, axis=1)
    columns = jnp.arange(VOCAB, dtype=jnp.int32)
    hit = columns[None, :] == targets[:, None]
    picked = jnp.sum(jnp.where(hit, logits, jnp.float32(0.0)), axis=1)
    loss = jnp.mean(top + jnp.log(total) - picked)
    ratio = shifted / total[:, None]
    probs = ratio.astype(jnp.bfloat16)
    dlogits = (ratio - hit.astype(jnp.float32)).astype(jnp.bfloat16)
    head_grad = lax.dot_general(hidden, probs, (((0,), (0,)), ((), ())), preferred_element_type=jnp.float32).astype(jnp.bfloat16)
    hidden_grad = lax.dot_general(dlogits, head_weight, (((1,), (1,)), ((), ())), preferred_element_type=jnp.float32).astype(jnp.bfloat16)
    return (loss, head_grad, hidden_grad)
```

```python
import functools

import jax
import jax.numpy as jnp
from jax import lax
from jax.experimental import pallas as pl
from jax.experimental.pallas import tpu as pltpu
from jax.sharding import PartitionSpec as P

MESH = pl.DeviceIdType.MESH
F32 = jnp.float32
BF16 = jnp.bfloat16
NX, NY, NZ, NC = 4, 8, 8, 2
YL = 4
ROWS = 13
PAD = 16
FEATS = 144
COLS = NZ * FEATS
BLOCKS = 16
TALL = BLOCKS * PAD
HALF = TALL // 2
D = YL * COLS
VOCAB_DEV = 256
TOKENS = 208
ORDER = (1, 7, 2, 6, 3, 5, 4)
XORDER = (1, 3, 2)


def kernel(shard, weight_hbm, targets, loss, head_grad, hidden_grad,
           weight, hid, pad32, own, zrec, line32, stat, st_x, st_y, st_z, keep, c_out, c_in, x_out, x_in,
           y_out, y_in, z_out, z_in, grad, wsem, gsem, bs, br,
           zs, zr, ys, yr, xs, xr, cs, cr, ss, sr, rcs, rcr, rxs, rxr, rys, ryr, rzs, rzr):
    s = lax.axis_index("section")
    t = lax.axis_index("tp")
    x, yh, c = s // 4, (s // 2) % 2, s % 2
    yl, z = t // NZ, t % NZ
    y = yh * YL + yl

    def at(x_, y_, z_, c_):
        return {"section": x_ * 4 + (y_ // YL) * 2 + c_, "tp": (y_ % YL) * NZ + z_}

    def z_peer(d):
        return at(x, y, (z + d) % NZ, c)

    def y_peer(d):
        return at(x, (y + d) % NY, z, c)

    def x_peer(d, dc=0):
        return at((x + d) % NX, y, z, (c + dc) % 2)

    def remote(src, dst, send, recv, peer):
        return pltpu.make_async_remote_copy(
            src_ref=src, dst_ref=dst, send_sem=send, recv_sem=recv, device_id=peer, device_id_type=MESH)

    sent = []

    def go(copy):
        copy.start()
        sent.append(copy)
        return copy

    fetch = pltpu.make_async_copy(weight_hbm, weight, wsem)
    fetch.start()

    xc = [(d, dc) for d in range(NX) for dc in range(NC) if d or dc]
    peers = [z_peer(d) for d in ORDER] + [y_peer(d) for d in ORDER] + [x_peer(d, dc) for d, dc in xc]
    barrier = pltpu.get_barrier_semaphore()
    for peer in peers:
        pl.semaphore_signal(barrier, inc=1, device_id=peer, device_id_type=MESH)

    pad32[...] = jnp.zeros_like(pad32)
    pad32[0:ROWS, 0:FEATS] = shard[...].astype(F32)
    mine = pad32[...].astype(BF16)
    own[...] = mine
    pl.semaphore_wait(barrier, len(peers))

    copies = [go(remote(own, zrec.at[z], zs.at[d], zr.at[d], z_peer(d))) for d in ORDER]
    zrec[z] = mine
    for copy in copies:
        copy.wait_recv()
    for i in range(NZ):
        line32[:, FEATS * i:FEATS * (i + 1)] = zrec[i][:, 0:FEATS].astype(F32)

    def place(x_, y_, c_):
        rows = pl.ds(pl.multiple_of((c_ * 8 + x_ * 2 + y_ // YL) * PAD, PAD), PAD)
        cols = pl.ds(pl.multiple_of((y_ % YL) * COLS, 128), COLS)
        return hid.at[rows, cols]

    place(x, y, c)[...] = line32[...].astype(BF16)

    ycopies = {d: go(remote(place(x, y, c), place(x, y, c), ys.at[d], yr.at[d], y_peer(d))) for d in ORDER}
    partner = x_peer(0, 1)
    xcopies = []
    ccopies = []
    for d in (0,) + ORDER:
        if d:
            ycopies[d].wait_recv()
        from_y = (y + NY - d) % NY
        block = place(x, from_y, c)
        for dx in XORDER:
            n = d * NX + dx
            xcopies.append((d, dx, go(remote(block, block, xs.at[n], xr.at[n], x_peer(dx)))))
        ccopies.append(go(remote(block, block, cs.at[d * NX], cr.at[d * NX], partner)))
    for d, dx, copy in xcopies:
        copy.wait_recv()
        block = place((x + NX - dx) % NX, (y + NY - d) % NY, c)
        n = d * NX + dx
        ccopies.append(go(remote(block, block, cs.at[n], cr.at[n], partner)))
    for copy in ccopies:
        copy.wait_recv()
    fetch.wait()

    def cols_of(j):
        return pl.ds(pl.multiple_of(j * COLS, 128), COLS)

    logits = lax.fori_loop(
        0, YL, lambda j, acc: acc + jnp.dot(hid[:, cols_of(j)], weight[cols_of(j), :], preferred_element_type=F32),
        jnp.zeros((TALL, VOCAB_DEV), F32))
    top = jnp.max(logits, axis=1, keepdims=True)
    shifted = jnp.exp(logits - top)
    total = jnp.sum(shifted, axis=1, keepdims=True)
    row = lax.broadcasted_iota(jnp.int32, (TALL, TOKENS), 0)
    b = row // PAD
    token = ((b // 2) % 4 * 4 + b % 2 * 2 + b // 8) * ROWS + row % PAD
    match = (token == lax.broadcasted_iota(jnp.int32, (TALL, TOKENS), 1)) & (row % PAD < ROWS)
    goal = jnp.sum(jnp.where(match, targets[...].astype(F32), 0.0), axis=1, keepdims=True).astype(jnp.int32)
    vocab = lax.broadcasted_iota(jnp.int32, (TALL, VOCAB_DEV), 1) + (s * (YL * NZ) + t) * VOCAB_DEV
    hit = vocab == goal
    picked = jnp.sum(jnp.where(hit, logits, 0.0), axis=1, keepdims=True)

    lane = lax.broadcasted_iota(jnp.int32, (TALL, 128), 1)
    wide = jnp.where(lane == 0, top, jnp.where(lane == 1, total, jnp.where(lane == 2, picked, 0.0)))
    stat[0] = wide.T[0:8, :]

    def merge(parts):
        best = functools.reduce(jnp.maximum, [p[0:1, :] for p in parts])
        amount = sum(p[1:2, :] * jnp.exp(p[0:1, :] - best) for p in parts)
        pick = sum(p[2:3, :] for p in parts)
        return jnp.concatenate([best, amount, pick, jnp.zeros((5, TALL), F32)], axis=0)

    k = 0
    for stage, (buf, targets_of) in enumerate((
            (st_x, [x_peer(d, dc) for d, dc in xc]),
            (st_y, [y_peer(d) for d in ORDER]),
            (st_z, [z_peer(d) for d in ORDER]))):
        copies = []
        for i, peer in enumerate(targets_of):
            copies.append(go(remote(stat.at[stage], buf.at[i], ss.at[k], sr.at[k], peer)))
            k += 1
        for copy in copies:
            copy.wait_recv()
        stat[stage + 1] = merge([stat[stage]] + [buf[i] for i in range(len(targets_of))])

    final = stat[3]
    slot = lax.broadcasted_iota(jnp.int32, (1, TALL), 1)
    each = jnp.where(slot % PAD < ROWS, final[0:1, :] + jnp.log(final[1:2, :]) - final[2:3, :], 0.0)
    loss[0, 0] = jnp.sum(each) / TOKENS

    back = jnp.concatenate([final, jnp.zeros((120, TALL), F32)], axis=0).T
    ratio = shifted * jnp.exp(top - back[:, 0:1]) / back[:, 1:2]
    probs = ratio.astype(BF16)
    dlogits = (ratio - hit.astype(F32)).astype(BF16)

    ccopies = []
    for j in range(YL):
        cols = pl.ds(j * COLS, COLS)
        terms = lax.dot_general(dlogits, weight[cols, :], (((1,), (1,)), ((), ())), preferred_element_type=F32)
        first, second = terms[0:HALF], terms[HALF:TALL]
        is0 = c == 0
        keep[:, cols] = jnp.where(is0, first, second)
        c_out[:, cols] = jnp.where(is0, second, first).astype(BF16)
        ccopies.append(go(remote(c_out.at[:, cols], c_in.at[:, cols], rcs.at[j], rcr.at[j], partner)))
    rxcopies = []
    for j in range(YL):
        cols = pl.ds(j * COLS, COLS)
        ccopies[j].wait_recv()
        both = keep[:, cols] + c_in[:, cols].astype(F32)
        keep[:, cols] = both
        x_out[:, cols] = both.astype(BF16)
        for dx in XORDER:
            n = j * NX + dx
            rows = pl.ds(pl.multiple_of((x + dx) % NX * 32, 32), 32)
            rxcopies.append(go(remote(x_out.at[rows, cols], x_in.at[dx, :, cols], rxs.at[n], rxr.at[n], x_peer(dx))))

    writes = []
    for j in range(YL):
        cols = pl.ds(j * COLS, COLS)
        grad[cols, :] = lax.dot_general(
            hid[:, cols], probs, (((0,), (0,)), ((), ())), preferred_element_type=F32).astype(BF16)
        write = pltpu.make_async_copy(grad.at[cols, :], head_grad.at[cols, :], gsem.at[j])
        write.start()
        writes.append(write)

    my_x = pl.ds(pl.multiple_of(x * 32, 32), 32)
    for j in range(YL):
        cols = pl.ds(j * COLS, COLS)
        for copy in rxcopies[j * 3:j * 3 + 3]:
            copy.wait_recv()
        y_out[:, cols] = (keep[my_x, cols] + x_in[1, :, cols].astype(F32) + x_in[2, :, cols].astype(F32)
                          + x_in[3, :, cols].astype(F32)).astype(BF16)

    def y_part(y_):
        rows = pl.ds(pl.multiple_of(y_ // YL * PAD, PAD), PAD)
        cols = pl.ds(pl.multiple_of((y_ % YL) * COLS, 128), COLS)
        return y_out.at[rows, cols]

    copies = [go(remote(y_part((y + d) % NY), y_in.at[d], rys.at[d], ryr.at[d], y_peer(d))) for d in ORDER]
    total_y = y_part(y)[...].astype(F32)
    for d, copy in zip(ORDER, copies):
        copy.wait_recv()
        total_y = total_y + y_in[d].astype(F32)
    for i in range(NZ):
        z_out[i, :, 0:FEATS] = total_y[:, FEATS * i:FEATS * (i + 1)]
    copies = [go(remote(z_out.at[(z + d) % NZ], z_in.at[d], rzs.at[d], rzr.at[d], z_peer(d))) for d in ORDER]
    result = z_out[z][:, 0:FEATS]
    for d, copy in zip(ORDER, copies):
        copy.wait_recv()
        result = result + z_in[d][:, 0:FEATS]
    hidden_grad[...] = result[0:ROWS].astype(BF16)

    for copy in sent:
        copy.wait_send()
    for write in writes:
        write.wait()


def per_device(hidden, head_weight, targets):
    vmem = pl.BlockSpec(memory_space=pltpu.VMEM)
    hbm = pl.BlockSpec(memory_space=pl.ANY)
    dma = pltpu.SemaphoreType.DMA
    loss, head_grad, hidden_grad = pl.pallas_call(
        kernel,
        out_shape=(
            jax.ShapeDtypeStruct((1, 1), F32),
            jax.ShapeDtypeStruct((D, VOCAB_DEV), BF16),
            jax.ShapeDtypeStruct((ROWS, FEATS), BF16),
        ),
        in_specs=[vmem, hbm, vmem],
        out_specs=(pl.BlockSpec(memory_space=pltpu.SMEM), hbm, vmem),
        scratch_shapes=[
            pltpu.VMEM((D, VOCAB_DEV), BF16),
            pltpu.VMEM((TALL, D), BF16),
            pltpu.VMEM((PAD, 256), F32),
            pltpu.VMEM((PAD, 256), BF16),
            pltpu.VMEM((NZ, PAD, 256), BF16),
            pltpu.VMEM((PAD, COLS), F32),
            pltpu.VMEM((4, 8, TALL), F32),
            pltpu.VMEM((7, 8, TALL), F32),
            pltpu.VMEM((7, 8, TALL), F32),
            pltpu.VMEM((7, 8, TALL), F32),
            pltpu.VMEM((HALF, D), F32),
            pltpu.VMEM((HALF, D), BF16),
            pltpu.VMEM((HALF, D), BF16),
            pltpu.VMEM((HALF, D), BF16),
            pltpu.VMEM((NX, 32, D), BF16),
            pltpu.VMEM((32, D), BF16),
            pltpu.VMEM((NY, PAD, COLS), BF16),
            pltpu.VMEM((NZ, PAD, 256), F32),
            pltpu.VMEM((NZ, PAD, 256), F32),
            pltpu.VMEM((D, VOCAB_DEV), BF16),
            dma, dma((YL,)), dma, dma,
            dma((8,)), dma((8,)), dma((8,)), dma((8,)),
            dma((32,)), dma((32,)), dma((32,)), dma((32,)),
            dma((21,)), dma((21,)), dma((YL,)), dma((YL,)),
            dma((16,)), dma((16,)), dma((8,)), dma((8,)), dma((8,)), dma((8,)),
        ],
        compiler_params=pltpu.CompilerParams(
            collective_id=0, has_side_effects=True, vmem_limit_bytes=48 * 2**20),
        name="output_layer",
    )(hidden, head_weight, targets.reshape(1, TOKENS))
    return loss.reshape(()), head_grad, hidden_grad


def solution(mesh):
    placed = (P("section", "tp"), P(None, ("section", "tp")), P())
    return jax.shard_map(
        per_device,
        mesh=mesh,
        in_specs=placed,
        out_specs=(P(), P(None, ("section", "tp")), P("section", "tp")),
        check_vma=False,
    )
```

```python
import functools

import jax
import jax.numpy as jnp
from jax import lax
from jax.experimental import pallas as pl
from jax.experimental.pallas import tpu as pltpu
from jax.sharding import PartitionSpec as P

MESH = pl.DeviceIdType.MESH
F32 = jnp.float32
BF16 = jnp.bfloat16
NX, NY, NZ, NC = 4, 8, 8, 2
YH, YL = 2, 4
ROWS = 13
PAD = 16
FEATS = 144
FA, FB, FC = 80, 32, 32
WA, WB, WC = NZ * FA, NZ * FB, YL * FC
HALF = YH * NX * PAD
TALL = NC * HALF
D = YL * NZ * FEATS
VOCAB_DEV = 256
TOKENS = 208
ORDER = (1, 7, 2, 6, 3, 5, 4)
XORDER = (1, 3, 2)


def kernel(shard_hbm, weight_hbm, targets_hbm, loss, head_grad, hidden_grad,
           shard, targets, w_a, w_b, w_c, hid_a, hid_b, hid_c, pad32, own_ab, own_c, z_rec, y_rec,
           line_a, line_b, line_c, stat, st_x, st_y, st_z,
           keep_a, keep_b, keep_c, out_a, out_b, out_c, in_a, in_b, in_c,
           s1_a, s1_b, s1_c, r1_a, r1_b, r1_c, s2_a, s2_b, s2_c, r2_a, r2_b, r2_c,
           s3_ab, s3_c, r3_ab, r3_c, g_a, g_b, g_c, local, gsem, ssem, rsem):
    s = lax.axis_index("section")
    t = lax.axis_index("tp")
    x, yh, c = s // 4, (s // 2) % 2, s % 2
    yl, z = t // NZ, t % NZ
    y = yh * YL + yl

    def at(x_, y_, z_, c_):
        return {"section": x_ * 4 + (y_ // YL) * 2 + c_, "tp": (y_ % YL) * NZ + z_}

    def z_peer(d):
        return at(x, y, (z + d) % NZ, c)

    def y_peer(d):
        return at(x, (y + d) % NY, z, c)

    def x_peer(d, dc=0):
        return at((x + d) % NX, y, z, (c + dc) % 2)

    sent = []

    def go(src, dst, peer):
        n = len(sent)
        copy = pltpu.make_async_remote_copy(
            src_ref=src, dst_ref=dst, send_sem=ssem.at[n], recv_sem=rsem.at[n], device_id=peer, device_id_type=MESH)
        copy.start()
        sent.append(copy)
        return copy

    fetch_small = [
        pltpu.make_async_copy(shard_hbm, shard, local.at[0]),
        pltpu.make_async_copy(targets_hbm, targets, local.at[1]),
    ]
    fetch = [
        pltpu.make_async_copy(weight_hbm.at[:, :, 0:FA], w_a, local.at[2]),
        pltpu.make_async_copy(weight_hbm.at[:, :, FA:FA + FB], w_b, local.at[3]),
    ] + [
        pltpu.make_async_copy(weight_hbm.at[:, i, FA + FB:FEATS], w_c.at[i], local.at[4 + i]) for i in range(NZ)
    ]
    for copy in fetch_small + fetch:
        copy.start()

    xc = [(d, dc) for d in range(NX) for dc in range(NC) if d or dc]
    peers = [z_peer(d) for d in ORDER] + [y_peer(d) for d in ORDER] + [x_peer(d, dc) for d, dc in xc]
    barrier = pltpu.get_barrier_semaphore()
    for peer in peers:
        pl.semaphore_signal(barrier, inc=1, device_id=peer, device_id_type=MESH)

    for copy in fetch_small:
        copy.wait()
    pad32[...] = jnp.zeros_like(pad32)
    pad32[0, 0:ROWS, 0:FA + FB] = shard[:, 0:FA + FB].astype(F32)
    pad32[1, 0:ROWS, 0:FC] = shard[:, FA + FB:FEATS].astype(F32)
    mine_ab, mine_c = pad32[0].astype(BF16), pad32[1].astype(BF16)
    own_ab[...] = mine_ab
    own_c[...] = mine_c
    pl.semaphore_wait(barrier, len(peers))

    z_copies = [go(own_ab, z_rec.at[z], z_peer(d)) for d in ORDER]
    y_copies = [go(own_c, y_rec.at[y], y_peer(d)) for d in ORDER]
    z_rec[z] = mine_ab
    y_rec[y] = mine_c
    for copy in z_copies:
        copy.wait_recv()
    for i in range(NZ):
        part = z_rec[i].astype(F32)
        line_a[:, FA * i:FA * (i + 1)] = part[:, 0:FA]
        line_b[:, FB * i:FB * (i + 1)] = part[:, FA:FA + FB]
    hid_a[yl, 0, yh, x] = line_a[...].astype(BF16)
    hid_b[yl, 0, yh, x] = line_b[...].astype(BF16)

    partner = x_peer(0, 1)
    block = hid_a.at[yl, 0, yh, x]
    a_y = {d: go(block, block, y_peer(d)) for d in ORDER}
    block = hid_b.at[yl, 0, yh, x]
    b_x = [go(block, block, x_peer(d)) for d in XORDER]
    for copy in y_copies:
        copy.wait_recv()
    for i in range(NY):
        line_c[i // YL, :, FC * (i % YL):FC * (i % YL + 1)] = y_rec[i].astype(F32)[:, 0:FC]
    hid_c[z, 0, :, x] = line_c[...].astype(BF16)
    block = hid_c.at[z, 0, :, x]
    c_x = [go(block, block, x_peer(d)) for d in XORDER]

    across = []
    a_x = []

    def pass_a(d):
        from_y = (y + NY - d) % NY
        block = hid_a.at[from_y % YL, 0, from_y // YL, x]
        for dx in XORDER:
            a_x.append((d, dx, go(block, block, x_peer(dx))))
        across.append(go(block, hid_a.at[from_y % YL, 1, from_y // YL, x], partner))

    pass_a(0)
    for copy in b_x:
        copy.wait_recv()
    block = hid_b.at[yl, 0, yh]
    b_y = [(d, go(block, block, y_peer(d))) for d in ORDER]
    across.append(go(block, hid_b.at[yl, 1, yh], partner))
    for copy in c_x:
        copy.wait_recv()
    block = hid_c.at[z, 0]
    c_z = [(d, go(block, block, z_peer(d))) for d in ORDER]
    across.append(go(block, hid_c.at[z, 1], partner))
    for d in ORDER:
        a_y[d].wait_recv()
        pass_a(d)
    for d, copy in b_y:
        copy.wait_recv()
        from_y = (y + NY - d) % NY
        across.append(go(hid_b.at[from_y % YL, 0, from_y // YL], hid_b.at[from_y % YL, 1, from_y // YL], partner))
    for d, copy in c_z:
        copy.wait_recv()
        from_z = (z + NZ - d) % NZ
        across.append(go(hid_c.at[from_z, 0], hid_c.at[from_z, 1], partner))
    for d, dx, copy in a_x:
        copy.wait_recv()
        from_y, from_x = (y + NY - d) % NY, (x + NX - dx) % NX
        across.append(go(hid_a.at[from_y % YL, 0, from_y // YL, from_x],
                         hid_a.at[from_y % YL, 1, from_y // YL, from_x], partner))
    for copy in across:
        copy.wait_recv()
    for copy in fetch:
        copy.wait()

    def dot(a, b, dims):
        return lax.dot_general(a, b, (dims, ((), ())), preferred_element_type=F32)

    def rows_a(j):
        return hid_a[j].reshape(TALL, WA)

    def rows_b(j):
        return hid_b[j].reshape(TALL, WB)

    def rows_c(j):
        return hid_c[j].reshape(TALL, WC)

    def weight_a(j):
        return w_a[j].reshape(WA, VOCAB_DEV)

    def weight_b(j):
        return w_b[j].reshape(WB, VOCAB_DEV)

    def weight_c(j):
        return w_c[j].reshape(WC, VOCAB_DEV)

    nn, nt, tn = ((1,), (0,)), ((1,), (1,)), ((0,), (0,))
    logits = sum(dot(rows_a(j), weight_a(j), nn) + dot(rows_b(j), weight_b(j), nn) for j in range(YL))
    logits = logits + sum(dot(rows_c(j), weight_c(j), nn) for j in range(NZ))
    top = jnp.max(logits, axis=1, keepdims=True)
    shifted = jnp.exp(logits - top)
    total = jnp.sum(shifted, axis=1, keepdims=True)
    row = lax.broadcasted_iota(jnp.int32, (TALL, TOKENS), 0)
    section = (row // PAD) % NX * 4 + (row // (PAD * NX)) % YH * 2 + (row // HALF + c) % 2
    match = (section * ROWS + row % PAD == lax.broadcasted_iota(jnp.int32, (TALL, TOKENS), 1)) & (row % PAD < ROWS)
    goal = jnp.sum(jnp.where(match, targets[...].astype(F32), 0.0), axis=1, keepdims=True).astype(jnp.int32)
    vocab = lax.broadcasted_iota(jnp.int32, (TALL, VOCAB_DEV), 1) + (s * (YL * NZ) + t) * VOCAB_DEV
    hit = vocab == goal
    picked = jnp.sum(jnp.where(hit, logits, 0.0), axis=1, keepdims=True)

    lane = lax.broadcasted_iota(jnp.int32, (TALL, 128), 1)
    wide = jnp.where(lane == 0, top, jnp.where(lane == 1, total, jnp.where(lane == 2, picked, 0.0)))
    tall = wide.T[0:8, :]
    stat[0] = tall
    stat[3] = jnp.concatenate([tall[:, HALF:TALL], tall[:, 0:HALF]], axis=1)

    def merge(parts):
        best = functools.reduce(jnp.maximum, [p[0:1, :] for p in parts])
        amount = sum(p[1:2, :] * jnp.exp(p[0:1, :] - best) for p in parts)
        pick = sum(p[2:3, :] for p in parts)
        return jnp.concatenate([best, amount, pick, jnp.zeros((5, TALL), F32)], axis=0)

    def exchange(part, buf, sends):
        copies = [go(src, buf.at[i], peer) for i, (src, peer) in enumerate(sends)]
        for copy in copies:
            copy.wait_recv()
        return merge([part] + [buf[i] for i in range(len(sends))])

    part = exchange(tall, st_x, [(stat.at[3 if dc else 0], x_peer(d, dc)) for d, dc in xc])
    stat[1] = part
    part = exchange(part, st_y, [(stat.at[1], y_peer(d)) for d in ORDER])
    stat[2] = part
    part = exchange(part, st_z, [(stat.at[2], z_peer(d)) for d in ORDER])

    slot = lax.broadcasted_iota(jnp.int32, (1, TALL), 1)
    each = jnp.where(slot % PAD < ROWS, part[0:1, :] + jnp.log(part[1:2, :]) - part[2:3, :], 0.0)
    loss[0, 0] = jnp.sum(each) / TOKENS

    back = jnp.concatenate([part, jnp.zeros((120, TALL), F32)], axis=0).T
    ratio = shifted * jnp.exp(top - back[:, 0:1]) / back[:, 1:2]
    probs = ratio.astype(BF16)
    dlogits = (ratio - hit.astype(F32)).astype(BF16)

    def first_half(weight, keep, out, into):
        terms = dot(dlogits, weight, nt)
        shape = (YH, NX, PAD, terms.shape[1])
        keep[...] = terms[0:HALF].reshape(shape)
        out[...] = terms[HALF:TALL].astype(BF16).reshape(shape)
        return go(out, into, partner)

    turn = [(yl + k) % YL for k in range(YL)]
    core_a = [first_half(weight_a(turn[k]), keep_a.at[k], out_a.at[k], in_a.at[k]) for k in range(YL)]
    core_b = [first_half(weight_b(j), keep_b.at[j], out_b.at[j], in_b.at[j]) for j in range(YL)]
    core_c = [first_half(weight_c(j), keep_c.at[j], out_c.at[j], in_c.at[j]) for j in range(NZ)]

    def add_core(copy, keep, into, send):
        copy.wait_recv()
        both = keep[...] + into[...].astype(F32)
        keep[...] = both
        send[...] = both.astype(BF16)

    a_x = []
    for k in range(YL):
        add_core(core_a[k], keep_a.at[k], in_a.at[k], s1_a.at[k])
        a_x.append([go(s1_a.at[k, :, (x + d) % NX], r1_a.at[d, k], x_peer(d)) for d in XORDER])
    for j in range(YL):
        add_core(core_b[j], keep_b.at[j], in_b.at[j], s1_b.at[j])
    b_y = []
    for d in ORDER:
        to_y = (y + d) % NY
        b_y.append(go(s1_b.at[to_y % YL, to_y // YL], r1_b.at[d], y_peer(d)))
    for j in range(NZ):
        add_core(core_c[j], keep_c.at[j], in_c.at[j], s1_c.at[j])
    c_z = [go(s1_c.at[(z + d) % NZ], r1_c.at[d], z_peer(d)) for d in ORDER]

    for j in range(YL):
        g_a[j] = dot(rows_a(j), probs, tn).astype(BF16).reshape(NZ, FA, VOCAB_DEV)
        g_b[j] = dot(rows_b(j), probs, tn).astype(BF16).reshape(NZ, FB, VOCAB_DEV)
    for j in range(NZ):
        g_c[j] = dot(rows_c(j), probs, tn).astype(BF16).reshape(YL, FC, VOCAB_DEV)
    writes = [
        pltpu.make_async_copy(g_a, head_grad.at[:, :, 0:FA], gsem.at[0]),
        pltpu.make_async_copy(g_b, head_grad.at[:, :, FA:FA + FB], gsem.at[1]),
    ] + [
        pltpu.make_async_copy(g_c.at[i], head_grad.at[:, i, FA + FB:FEATS], gsem.at[2 + i]) for i in range(NZ)
    ]
    for write in writes:
        write.start()

    a_y = []
    for k in range(YL):
        for copy in a_x[k]:
            copy.wait_recv()
        chunk = keep_a[k, :, x] + sum(r1_a[d, k].astype(F32) for d in XORDER)
        s2_a[k] = chunk.astype(BF16)
        if k == 0:
            keep_a[0, :, 0] = chunk
        for e in range(YH):
            if k or e:
                to = (yh + e) % YH
                a_y.append(go(s2_a.at[k, to], r2_a.at[e * YL + k], at(x, to * YL + turn[k], z, c)))
    for copy in b_y:
        copy.wait_recv()
    sum_b = keep_b[yl, yh] + sum(r1_b[d].astype(F32) for d in ORDER)
    s2_b[...] = sum_b.astype(BF16)
    keep_b[0, 0] = sum_b
    b_x = [go(s2_b.at[(x + d) % NX], r2_b.at[d], x_peer(d)) for d in XORDER]
    for copy in c_z:
        copy.wait_recv()
    sum_c = keep_c[z] + sum(r1_c[d].astype(F32) for d in ORDER)
    s2_c[...] = sum_c.astype(BF16)
    keep_c[0] = sum_c
    c_x = [go(s2_c.at[:, (x + d) % NX], r2_c.at[d], x_peer(d)) for d in XORDER]

    for copy in c_x:
        copy.wait_recv()
    part_c = keep_c[0, :, x] + sum(r2_c[d].astype(F32) for d in XORDER)
    for i in range(NY):
        s3_c[i, :, 0:FC] = part_c[i // YL, :, FC * (i % YL):FC * (i % YL + 1)]
    c_y = [go(s3_c.at[(y + d) % NY], r3_c.at[d], y_peer(d)) for d in ORDER]
    for copy in b_x:
        copy.wait_recv()
    part_b = keep_b[0, 0, x] + sum(r2_b[d].astype(F32) for d in XORDER)
    for copy in a_y:
        copy.wait_recv()
    part_a = keep_a[0, yh, 0] + sum(r2_a[n].astype(F32) for n in range(1, NY))
    for i in range(NZ):
        s3_ab[i, :, 0:FA] = part_a[:, FA * i:FA * (i + 1)]
        s3_ab[i, :, FA:FA + FB] = part_b[:, FB * i:FB * (i + 1)]
    ab_z = [go(s3_ab.at[(z + d) % NZ], r3_ab.at[d], z_peer(d)) for d in ORDER]
    for copy in c_y:
        copy.wait_recv()
    done_c = s3_c[y][:, 0:FC] + sum(r3_c[d][:, 0:FC] for d in ORDER)
    hidden_grad[:, FA + FB:FEATS] = done_c[0:ROWS].astype(BF16)
    for copy in ab_z:
        copy.wait_recv()
    done_ab = s3_ab[z][:, 0:FA + FB] + sum(r3_ab[d][:, 0:FA + FB] for d in ORDER)
    hidden_grad[:, 0:FA + FB] = done_ab[0:ROWS].astype(BF16)

    for copy in sent:
        copy.wait_send()
    for write in writes:
        write.wait()


def per_device(hidden, head_weight, targets):
    vmem = pl.BlockSpec(memory_space=pltpu.VMEM)
    hbm = pl.BlockSpec(memory_space=pltpu.HBM)
    v = pltpu.VMEM
    dma = pltpu.SemaphoreType.DMA
    halves = (YH, NX, PAD)
    loss, head_grad, hidden_grad = pl.pallas_call(
        kernel,
        out_shape=(
            jax.ShapeDtypeStruct((1, 1), F32),
            jax.ShapeDtypeStruct((YL, NZ, FEATS, VOCAB_DEV), BF16),
            jax.ShapeDtypeStruct((ROWS, FEATS), BF16),
        ),
        in_specs=[hbm, hbm, hbm],
        out_specs=(pl.BlockSpec(memory_space=pltpu.SMEM), pl.BlockSpec(memory_space=pl.ANY), vmem),
        scratch_shapes=[
            v((ROWS, FEATS), BF16), v((1, TOKENS), jnp.int32),
            v((YL, NZ, FA, VOCAB_DEV), BF16), v((YL, NZ, FB, VOCAB_DEV), BF16), v((NZ, YL, FC, VOCAB_DEV), BF16),
            v((YL, NC) + halves + (WA,), BF16), v((YL, NC) + halves + (WB,), BF16), v((NZ, NC) + halves + (WC,), BF16),
            v((2, PAD, 128), F32), v((PAD, 128), BF16), v((PAD, 128), BF16),
            v((NZ, PAD, 128), BF16), v((NY, PAD, 128), BF16),
            v((PAD, WA), F32), v((PAD, WB), F32), v((YH, PAD, WC), F32),
            v((4, 8, TALL), F32), v((7, 8, TALL), F32), v((7, 8, TALL), F32), v((7, 8, TALL), F32),
            v((YL,) + halves + (WA,), F32), v((YL,) + halves + (WB,), F32), v((NZ,) + halves + (WC,), F32),
            v((YL,) + halves + (WA,), BF16), v((YL,) + halves + (WB,), BF16), v((NZ,) + halves + (WC,), BF16),
            v((YL,) + halves + (WA,), BF16), v((YL,) + halves + (WB,), BF16), v((NZ,) + halves + (WC,), BF16),
            v((YL,) + halves + (WA,), BF16), v((YL,) + halves + (WB,), BF16), v((NZ,) + halves + (WC,), BF16),
            v((NX, YL, YH, PAD, WA), BF16), v((NY, NX, PAD, WB), BF16), v((NZ,) + halves + (WC,), BF16),
            v((YL, YH, PAD, WA), BF16), v((NX, PAD, WB), BF16), v(halves + (WC,), BF16),
            v((NY, PAD, WA), BF16), v((NX, PAD, WB), BF16), v((NX, YH, PAD, WC), BF16),
            v((NZ, PAD, 128), F32), v((NY, PAD, 128), F32), v((NZ, PAD, 128), F32), v((NY, PAD, 128), F32),
            v((YL, NZ, FA, VOCAB_DEV), BF16), v((YL, NZ, FB, VOCAB_DEV), BF16), v((NZ, YL, FC, VOCAB_DEV), BF16),
            dma((12,)), dma((10,)), dma((208,)), dma((208,)),
        ],
        compiler_params=pltpu.CompilerParams(
            collective_id=0, has_side_effects=True, vmem_limit_bytes=44 * 2**20),
        name="output_layer",
    )(*[pltpu.with_memory_space_constraint(operand, pltpu.HBM) for operand in (
        hidden, head_weight.reshape(YL, NZ, FEATS, VOCAB_DEV), targets.reshape(1, TOKENS))])
    return loss.reshape(()), head_grad.reshape(D, VOCAB_DEV), hidden_grad


def solution(mesh):
    placed = (P("section", "tp"), P(None, ("section", "tp")), P())
    return jax.shard_map(
        per_device,
        mesh=mesh,
        in_specs=placed,
        out_specs=(P(), P(None, ("section", "tp")), P("section", "tp")),
        check_vma=False,
    )
```

```python
import functools

import jax
import jax.numpy as jnp
from jax import lax
from jax.experimental import pallas as pl
from jax.experimental.pallas import tpu as pltpu
from jax.sharding import PartitionSpec as P

MESH = pl.DeviceIdType.MESH
F32 = jnp.float32
BF16 = jnp.bfloat16
NX, NY, NZ, NC = 4, 8, 8, 2
YH, YL = 2, 4
ROWS = 13
PAD = 16
FEATS = 144
FA, FB, FC = 80, 32, 32
WA, WB, WC = NZ * FA, NZ * FB, YL * FC
HALF = YH * NX * PAD
TALL = NC * HALF
D = YL * NZ * FEATS
VOCAB_DEV = 256
TOKENS = 208
ORDER = (1, 7, 2, 6, 3, 5, 4)
XORDER = (1, 3, 2)
MISS = 2 * len(ORDER) + 1


def kernel(shard_hbm, weight_hbm, targets_hbm, loss, head_grad, hidden_grad,
           shard, targets, w_a, w_b, w_c, wt_a, wt_b, wt_c, hid_a, hid_b, hid_c, pad32, own_ab, own_c,
           z_rec, y_rec, line_a, line_b, line_c, stat, st_x, st_y, st_m, st_z, coef, keep_a, keep_b, keep_c,
           out_a, out_b, out_c, in_a, in_b, in_c, s1_a, s1_b, s1_c, r1_a, r1_b, r1_c, tk_a, tk_b, tk_c,
           to_a, to_b, to_c, ti_a, ti_b, ti_c, tr_a, tr_b, tr_c, s2_a, s2_b, s2_c, r2_a, r2_b, r2_c, s3_ab,
           s3_c, r3_ab, r3_c, g_a, g_b, g_c, local, gsem, ssem, rsem):
    s = lax.axis_index("section")
    t = lax.axis_index("tp")
    x, yh, c = s // 4, (s // 2) % 2, s % 2
    yl, z = t // NZ, t % NZ
    y = yh * YL + yl

    def at(x_, y_, z_, c_):
        return {"section": x_ * 4 + (y_ // YL) * 2 + c_, "tp": (y_ % YL) * NZ + z_}

    def z_peer(d):
        return at(x, y, (z + d) % NZ, c)

    def y_peer(d):
        return at(x, (y + d) % NY, z, c)

    def x_peer(d, dc=0):
        return at((x + d) % NX, y, z, (c + dc) % 2)

    sent = []

    def go(src, dst, peer):
        n = len(sent)
        copy = pltpu.make_async_remote_copy(
            src_ref=src, dst_ref=dst, send_sem=ssem.at[n], recv_sem=rsem.at[n], device_id=peer, device_id_type=MESH)
        copy.start()
        sent.append(copy)
        return copy

    xc = [(d, dc) for d in range(NX) for dc in range(NC) if d or dc]
    peers = [z_peer(d) for d in ORDER] + [y_peer(d) for d in ORDER] + [x_peer(d, dc) for d, dc in xc]
    partner = x_peer(0, 1)
    barrier = pltpu.get_barrier_semaphore()
    for peer in peers:
        pl.semaphore_signal(barrier, inc=1, device_id=peer, device_id_type=MESH)

    fetch_small = [
        pltpu.make_async_copy(shard_hbm, shard, local.at[0]),
        pltpu.make_async_copy(targets_hbm, targets, local.at[1]),
    ]
    fetch = [
        pltpu.make_async_copy(weight_hbm.at[:, :, 0:FA], w_a, local.at[2]),
        pltpu.make_async_copy(weight_hbm.at[:, :, FA:FA + FB], w_b, local.at[3]),
    ] + [
        pltpu.make_async_copy(weight_hbm.at[:, i, FA + FB:FEATS], w_c.at[i], local.at[4 + i]) for i in range(NZ)
    ]
    for copy in fetch_small + fetch:
        copy.start()

    for copy in fetch_small:
        copy.wait()
    pad32[...] = jnp.zeros_like(pad32)
    pad32[0, 0:ROWS, 0:FA + FB] = shard[:, 0:FA + FB].astype(F32)
    pad32[1, 0:ROWS, 0:FC] = shard[:, FA + FB:FEATS].astype(F32)
    mine_ab, mine_c = pad32[0].astype(BF16), pad32[1].astype(BF16)
    own_ab[...] = mine_ab
    own_c[...] = mine_c

    row = lax.broadcasted_iota(jnp.int32, (TALL, TOKENS), 0)
    section = (row // PAD) % NX * 4 + (row // (PAD * NX)) % YH * 2 + (row // HALF + c) % 2
    match = (section * ROWS + row % PAD == lax.broadcasted_iota(jnp.int32, (TALL, TOKENS), 1)) & (row % PAD < ROWS)
    goal = jnp.sum(jnp.where(match, targets[...].astype(F32), 0.0), axis=1, keepdims=True).astype(jnp.int32)
    vocab = lax.broadcasted_iota(jnp.int32, (TALL, VOCAB_DEV), 1) + (s * (YL * NZ) + t) * VOCAB_DEV
    hit = vocab == goal

    def dot(a, b, dims):
        return lax.dot_general(a, b, (dims, ((), ())), preferred_element_type=F32)

    nn, tn = ((1,), (0,)), ((0,), (0,))
    turn = [(yl + k) % YL for k in range(YL)]

    for copy in fetch:
        copy.wait()
    for j in range(YL):
        wt_a[j] = w_a[j].reshape(WA, VOCAB_DEV).T
        wt_b[j] = w_b[j].reshape(WB, VOCAB_DEV).T
    for j in range(NZ):
        wt_c[j] = w_c[j].reshape(WC, VOCAB_DEV).T

    def split(left, weight, keep, out):
        terms = dot(left, weight, nn)
        shape = (YH, NX, PAD, terms.shape[1])
        keep[...] = terms[0:HALF].astype(keep.dtype).reshape(shape)
        out[...] = terms[HALF:TALL].astype(BF16).reshape(shape)

    hot = hit.astype(F32).astype(BF16)
    for k in range(YL):
        split(hot, wt_a[turn[k]], tk_a.at[k], to_a.at[k])
    for j in range(YL):
        split(hot, wt_b[j], tk_b.at[j], to_b.at[j])
    for j in range(NZ):
        split(hot, wt_c[j], tk_c.at[j], to_c.at[j])
    pl.semaphore_wait(barrier, len(peers))

    z_copies = [go(own_ab, z_rec.at[z], z_peer(d)) for d in ORDER]
    y_copies = [go(own_c, y_rec.at[y], y_peer(d)) for d in ORDER]
    z_rec[z] = mine_ab
    y_rec[y] = mine_c
    t_core = [go(to_a.at[k], ti_a.at[k], partner) for k in range(YL)]
    t_core += [go(to_b.at[j], ti_b.at[j], partner) for j in range(YL)]
    t_core += [go(to_c.at[j], ti_c.at[j], partner) for j in range(NZ)]
    for copy in z_copies:
        copy.wait_recv()
    for i in range(NZ):
        part = z_rec[i].astype(F32)
        line_a[:, FA * i:FA * (i + 1)] = part[:, 0:FA]
        line_b[:, FB * i:FB * (i + 1)] = part[:, FA:FA + FB]
    hid_a[yl, 0, yh, x] = line_a[...].astype(BF16)
    hid_b[yl, 0, yh, x] = line_b[...].astype(BF16)

    block = hid_a.at[yl, 0, yh, x]
    a_y = {d: go(block, block, y_peer(d)) for d in ORDER}
    block = hid_b.at[yl, 0, yh, x]
    b_x = [go(block, block, x_peer(d)) for d in XORDER]
    for copy in t_core:
        copy.wait_recv()
    for keep, into in ((tk_a, ti_a), (tk_b, ti_b), (tk_c, ti_c)):
        for j in range(keep.shape[0]):
            keep[j] = keep[j] + into[j]
    for copy in y_copies:
        copy.wait_recv()
    for i in range(NY):
        line_c[i // YL, :, FC * (i % YL):FC * (i % YL + 1)] = y_rec[i].astype(F32)[:, 0:FC]
    hid_c[z, 0, :, x] = line_c[...].astype(BF16)
    block = hid_c.at[z, 0, :, x]
    c_x = [go(block, block, x_peer(d)) for d in XORDER]

    across = []
    a_x = []

    def pass_a(d):
        from_y = (y + NY - d) % NY
        block = hid_a.at[from_y % YL, 0, from_y // YL, x]
        for dx in XORDER:
            a_x.append((d, dx, go(block, block, x_peer(dx))))
        across.append(go(block, hid_a.at[from_y % YL, 1, from_y // YL, x], partner))

    pass_a(0)
    for copy in b_x:
        copy.wait_recv()
    block = hid_b.at[yl, 0, yh]
    b_y = [(d, go(block, block, y_peer(d))) for d in ORDER]
    across.append(go(block, hid_b.at[yl, 1, yh], partner))
    for copy in c_x:
        copy.wait_recv()
    block = hid_c.at[z, 0]
    c_z = [(d, go(block, block, z_peer(d))) for d in ORDER]
    across.append(go(block, hid_c.at[z, 1], partner))
    for d in ORDER:
        a_y[d].wait_recv()
        pass_a(d)
    for d, copy in b_y:
        copy.wait_recv()
        from_y = (y + NY - d) % NY
        across.append(go(hid_b.at[from_y % YL, 0, from_y // YL], hid_b.at[from_y % YL, 1, from_y // YL], partner))
    for d, copy in c_z:
        copy.wait_recv()
        from_z = (z + NZ - d) % NZ
        across.append(go(hid_c.at[from_z, 0], hid_c.at[from_z, 1], partner))
    for d, dx, copy in a_x:
        copy.wait_recv()
        from_y, from_x = (y + NY - d) % NY, (x + NX - dx) % NX
        across.append(go(hid_a.at[from_y % YL, 0, from_y // YL, from_x],
                         hid_a.at[from_y % YL, 1, from_y // YL, from_x], partner))
    def wide_a(src, dst, k):
        return [go(src.at[k, :, (x + d) % NX], dst.at[d, k], x_peer(d)) for d in XORDER]

    def wide_b(src, dst):
        return [go(src.at[(y + d) % NY % YL, (y + d) % NY // YL], dst.at[d], y_peer(d)) for d in ORDER]

    def wide_c(src, dst):
        return [go(src.at[(z + d) % NZ], dst.at[d], z_peer(d)) for d in ORDER]

    ta_x = [wide_a(tk_a, tr_a, k) for k in range(YL)]
    tb_y = wide_b(tk_b, tr_b)
    tc_z = wide_c(tk_c, tr_c)
    for copy in across:
        copy.wait_recv()

    def rows_a(j):
        return hid_a[j].reshape(TALL, WA)

    def rows_b(j):
        return hid_b[j].reshape(TALL, WB)

    def rows_c(j):
        return hid_c[j].reshape(TALL, WC)

    logits = sum(dot(rows_a(j), w_a[j].reshape(WA, VOCAB_DEV), nn) + dot(rows_b(j), w_b[j].reshape(WB, VOCAB_DEV), nn)
                 for j in range(YL))
    logits = logits + sum(dot(rows_c(j), w_c[j].reshape(WC, VOCAB_DEV), nn) for j in range(NZ))
    top = jnp.max(logits, axis=1, keepdims=True)
    shifted = jnp.exp(logits - top)
    rest = jnp.sum(jnp.where(hit, 0.0, shifted), axis=1, keepdims=True)
    aim = jnp.sum(jnp.where(hit, shifted, 0.0), axis=1, keepdims=True)
    picked = jnp.sum(jnp.where(hit, logits, 0.0), axis=1, keepdims=True)

    lane = lax.broadcasted_iota(jnp.int32, (TALL, 128), 1)
    columns = jnp.where(lane == 0, top, jnp.where(lane == 1, rest, jnp.where(lane == 2, picked, jnp.where(
        lane == 3, aim, 0.0))))
    tall = columns.T[0:8, :]
    stat[0] = tall
    stat[3] = jnp.concatenate([tall[:, HALF:TALL], tall[:, 0:HALF]], axis=1)

    def merge(parts):
        best = functools.reduce(jnp.maximum, [p[0:1, :] for p in parts])
        scale = [jnp.exp(p[0:1, :] - best) for p in parts]
        rest_ = sum(p[1:2, :] * f for p, f in zip(parts, scale))
        pick_ = sum(p[2:3, :] for p in parts)
        aim_ = sum(p[3:4, :] * f for p, f in zip(parts, scale))
        return jnp.concatenate([best, rest_, pick_, aim_, jnp.zeros((4, TALL), F32)], axis=0)

    def columns_of(rows):
        full = jnp.concatenate(rows + [jnp.zeros((128 - len(rows), TALL), F32)], axis=0)
        return full.T

    copies = [go(stat.at[3 if dc else 0], st_x.at[i], x_peer(d, dc)) for i, (d, dc) in enumerate(xc)]
    for copy in copies:
        copy.wait_recv()
    group = merge([tall] + [st_x[i] for i in range(len(xc))])
    stat[1] = group
    to_y = [go(stat.at[1], st_y.at[i], y_peer(d)) for i, d in enumerate(ORDER)]
    to_z = [go(stat.at[1], st_m.at[i], z_peer(d)) for i, d in enumerate(ORDER)]

    shifted = jnp.exp(logits - columns_of([group])[:, 0:1])
    others = jnp.where(hit, 0.0, shifted).astype(BF16)
    core_a, core_b, core_c = [], [], []
    for k in range(YL):
        split(others, wt_a[turn[k]], keep_a.at[k], out_a.at[k])
        core_a.append(go(out_a.at[k], in_a.at[k], partner))
    for j in range(YL):
        split(others, wt_b[j], keep_b.at[j], out_b.at[j])
        core_b.append(go(out_b.at[j], in_b.at[j], partner))
    for j in range(NZ):
        split(others, wt_c[j], keep_c.at[j], out_c.at[j])
        core_c.append(go(out_c.at[j], in_c.at[j], partner))

    def add_core(copy, keep, into, send):
        copy.wait_recv()
        both = keep[...] + into[...].astype(F32)
        keep[...] = both
        send[...] = both.astype(BF16)

    a_x = []
    for k in range(YL):
        add_core(core_a[k], keep_a.at[k], in_a.at[k], s1_a.at[k])
        a_x.append(wide_a(s1_a, r1_a, k))
    for copy in to_y:
        copy.wait_recv()
    near = [st_y[i] for i in range(len(ORDER))]
    plane = merge([group] + near)
    stat[2] = plane
    last = [go(stat.at[2], st_z.at[i], z_peer(d)) for i, d in enumerate(ORDER)]
    for j in range(YL):
        add_core(core_b[j], keep_b.at[j], in_b.at[j], s1_b.at[j])
    b_y = wide_b(s1_b, r1_b)
    for j in range(NZ):
        add_core(core_c[j], keep_c.at[j], in_c.at[j], s1_c.at[j])
    c_z = wide_c(s1_c, r1_c)

    for copy in to_z + last:
        copy.wait_recv()
    whole = merge([plane] + [st_z[i] for i in range(len(ORDER))])
    highest, total = whole[0:1, :], whole[1:2, :] + whole[3:4, :]
    slot = lax.broadcasted_iota(jnp.int32, (1, TALL), 1)
    each = jnp.where(slot % PAD < ROWS, highest + jnp.log(total) - whole[2:3, :], 0.0)
    loss[0, 0] = jnp.sum(each) / TOKENS

    def factor(p):
        return jnp.exp(p[0:1, :] - highest) / total

    miss = (whole[1:2, :] / total).astype(BF16).astype(F32)
    factors = columns_of([factor(group)] + [factor(p) for p in near]
                         + [factor(st_m[i]) for i in range(len(ORDER))] + [miss])
    coef[...] = factors[0:HALF].reshape(YH, NX, PAD, 128)
    probs = (shifted * factors[:, 0:1]).astype(BF16)

    a_y = []
    f_x = coef[:, x]
    for k in range(YL):
        for copy in a_x[k] + ta_x[k]:
            copy.wait_recv()
        chunk = keep_a[k, :, x] + sum(r1_a[d, k].astype(F32) for d in XORDER)
        column = tk_a[k, :, x] + sum(tr_a[d, k] for d in XORDER)
        chunk = chunk * f_x[..., 0:1] - column.astype(F32) * f_x[..., MISS:MISS + 1]
        s2_a[k] = chunk.astype(BF16)
        if k == 0:
            keep_a[0, :, 0] = chunk
        for e in range(YH):
            if k or e:
                to = (yh + e) % YH
                a_y.append(go(s2_a.at[k, to], r2_a.at[e * YL + k], at(x, to * YL + turn[k], z, c)))
    for copy in b_y + tb_y:
        copy.wait_recv()
    f_y = coef[yh]
    column = tk_b[yl, yh] + sum(tr_b[d] for d in ORDER)
    sum_b = keep_b[yl, yh] * f_y[..., 0:1] - column.astype(F32) * f_y[..., MISS:MISS + 1]
    sum_b = sum_b + sum(r1_b[d].astype(F32) * f_y[..., 1 + i:2 + i] for i, d in enumerate(ORDER))
    s2_b[...] = sum_b.astype(BF16)
    keep_b[0, 0] = sum_b
    b_x = [go(s2_b.at[(x + d) % NX], r2_b.at[d], x_peer(d)) for d in XORDER]
    for copy in c_z + tc_z:
        copy.wait_recv()
    f_z = coef[...]
    column = tk_c[z] + sum(tr_c[d] for d in ORDER)
    sum_c = keep_c[z] * f_z[..., 0:1] - column.astype(F32) * f_z[..., MISS:MISS + 1]
    sum_c = sum_c + sum(r1_c[d].astype(F32) * f_z[..., 8 + i:9 + i] for i, d in enumerate(ORDER))
    s2_c[...] = sum_c.astype(BF16)
    keep_c[0] = sum_c
    c_x = [go(s2_c.at[:, (x + d) % NX], r2_c.at[d], x_peer(d)) for d in XORDER]

    for j in range(YL):
        g_a[j] = dot(rows_a(j), probs, tn).astype(BF16).reshape(NZ, FA, VOCAB_DEV)
        g_b[j] = dot(rows_b(j), probs, tn).astype(BF16).reshape(NZ, FB, VOCAB_DEV)
    for j in range(NZ):
        g_c[j] = dot(rows_c(j), probs, tn).astype(BF16).reshape(YL, FC, VOCAB_DEV)
    writes = [
        pltpu.make_async_copy(g_a, head_grad.at[:, :, 0:FA], gsem.at[0]),
        pltpu.make_async_copy(g_b, head_grad.at[:, :, FA:FA + FB], gsem.at[1]),
    ] + [
        pltpu.make_async_copy(g_c.at[i], head_grad.at[:, i, FA + FB:FEATS], gsem.at[2 + i]) for i in range(NZ)
    ]
    for write in writes:
        write.start()

    for copy in c_x:
        copy.wait_recv()
    part_c = keep_c[0, :, x] + sum(r2_c[d].astype(F32) for d in XORDER)
    for i in range(NY):
        s3_c[i, :, 0:FC] = part_c[i // YL, :, FC * (i % YL):FC * (i % YL + 1)]
    c_y = [go(s3_c.at[(y + d) % NY], r3_c.at[d], y_peer(d)) for d in ORDER]
    for copy in b_x:
        copy.wait_recv()
    part_b = keep_b[0, 0, x] + sum(r2_b[d].astype(F32) for d in XORDER)
    for copy in a_y:
        copy.wait_recv()
    part_a = keep_a[0, yh, 0] + sum(r2_a[n].astype(F32) for n in range(1, NY))
    for i in range(NZ):
        s3_ab[i, :, 0:FA] = part_a[:, FA * i:FA * (i + 1)]
        s3_ab[i, :, FA:FA + FB] = part_b[:, FB * i:FB * (i + 1)]
    ab_z = [go(s3_ab.at[(z + d) % NZ], r3_ab.at[d], z_peer(d)) for d in ORDER]
    for copy in c_y:
        copy.wait_recv()
    done_c = s3_c[y][:, 0:FC] + sum(r3_c[d][:, 0:FC] for d in ORDER)
    hidden_grad[:, FA + FB:FEATS] = done_c[0:ROWS].astype(BF16)
    for copy in ab_z:
        copy.wait_recv()
    done_ab = s3_ab[z][:, 0:FA + FB] + sum(r3_ab[d][:, 0:FA + FB] for d in ORDER)
    hidden_grad[:, 0:FA + FB] = done_ab[0:ROWS].astype(BF16)

    for copy in sent:
        copy.wait_send()
    for write in writes:
        write.wait()


def per_device(hidden, head_weight, targets):
    vmem = pl.BlockSpec(memory_space=pltpu.VMEM)
    hbm = pl.BlockSpec(memory_space=pltpu.HBM)
    v = pltpu.VMEM
    dma = pltpu.SemaphoreType.DMA
    halves = (YH, NX, PAD)
    loss, head_grad, hidden_grad = pl.pallas_call(
        kernel,
        out_shape=(
            jax.ShapeDtypeStruct((1, 1), F32),
            jax.ShapeDtypeStruct((YL, NZ, FEATS, VOCAB_DEV), BF16),
            jax.ShapeDtypeStruct((ROWS, FEATS), BF16),
        ),
        in_specs=[hbm, hbm, hbm],
        out_specs=(pl.BlockSpec(memory_space=pltpu.SMEM), pl.BlockSpec(memory_space=pl.ANY), vmem),
        scratch_shapes=[
            v((ROWS, FEATS), BF16), v((1, TOKENS), jnp.int32),
            v((YL, NZ, FA, VOCAB_DEV), BF16), v((YL, NZ, FB, VOCAB_DEV), BF16), v((NZ, YL, FC, VOCAB_DEV), BF16),
            v((YL, VOCAB_DEV, WA), BF16), v((YL, VOCAB_DEV, WB), BF16), v((NZ, VOCAB_DEV, WC), BF16),
            v((YL, NC) + halves + (WA,), BF16), v((YL, NC) + halves + (WB,), BF16), v((NZ, NC) + halves + (WC,), BF16),
            v((2, PAD, 128), F32), v((PAD, 128), BF16), v((PAD, 128), BF16),
            v((NZ, PAD, 128), BF16), v((NY, PAD, 128), BF16),
            v((PAD, WA), F32), v((PAD, WB), F32), v((YH, PAD, WC), F32),
            v((4, 8, TALL), F32), v((7, 8, TALL), F32), v((7, 8, TALL), F32), v((7, 8, TALL), F32), v((7, 8, TALL), F32),
            v(halves + (128,), F32),
            v((YL,) + halves + (WA,), F32), v((YL,) + halves + (WB,), F32), v((NZ,) + halves + (WC,), F32),
            v((YL,) + halves + (WA,), BF16), v((YL,) + halves + (WB,), BF16), v((NZ,) + halves + (WC,), BF16),
            v((YL,) + halves + (WA,), BF16), v((YL,) + halves + (WB,), BF16), v((NZ,) + halves + (WC,), BF16),
            v((YL,) + halves + (WA,), BF16), v((YL,) + halves + (WB,), BF16), v((NZ,) + halves + (WC,), BF16),
            v((NX, YL, YH, PAD, WA), BF16), v((NY, NX, PAD, WB), BF16), v((NZ,) + halves + (WC,), BF16),
            v((YL,) + halves + (WA,), BF16), v((YL,) + halves + (WB,), BF16), v((NZ,) + halves + (WC,), BF16),
            v((YL,) + halves + (WA,), BF16), v((YL,) + halves + (WB,), BF16), v((NZ,) + halves + (WC,), BF16),
            v((YL,) + halves + (WA,), BF16), v((YL,) + halves + (WB,), BF16), v((NZ,) + halves + (WC,), BF16),
            v((NX, YL, YH, PAD, WA), BF16), v((NY, NX, PAD, WB), BF16), v((NZ,) + halves + (WC,), BF16),
            v((YL, YH, PAD, WA), BF16), v((NX, PAD, WB), BF16), v(halves + (WC,), BF16),
            v((NY, PAD, WA), BF16), v((NX, PAD, WB), BF16), v((NX, YH, PAD, WC), BF16),
            v((NZ, PAD, 128), F32), v((NY, PAD, 128), F32), v((NZ, PAD, 128), F32), v((NY, PAD, 128), F32),
            v((YL, NZ, FA, VOCAB_DEV), BF16), v((YL, NZ, FB, VOCAB_DEV), BF16), v((NZ, YL, FC, VOCAB_DEV), BF16),
            dma((12,)), dma((10,)), dma((256,)), dma((256,)),
        ],
        compiler_params=pltpu.CompilerParams(
            collective_id=0, has_side_effects=True, vmem_limit_bytes=44 * 2**20),
        name="output_layer",
    )(*[pltpu.with_memory_space_constraint(operand, pltpu.HBM) for operand in (
        hidden, head_weight.reshape(YL, NZ, FEATS, VOCAB_DEV), targets.reshape(1, TOKENS))])
    return loss.reshape(()), head_grad.reshape(D, VOCAB_DEV), hidden_grad


def solution(mesh):
    placed = (P("section", "tp"), P(None, ("section", "tp")), P())
    return jax.shard_map(
        per_device,
        mesh=mesh,
        in_specs=placed,
        out_specs=(P(), P(None, ("section", "tp")), P("section", "tp")),
        check_vma=False,
    )
```

```python
import functools

import jax
import jax.numpy as jnp
from jax import lax
from jax.experimental import pallas as pl
from jax.experimental.pallas import tpu as pltpu
from jax.sharding import PartitionSpec as P

MESH = pl.DeviceIdType.MESH
F32 = jnp.float32
BF16 = jnp.bfloat16
NX, NY, NZ, NC = 4, 8, 8, 2
YH, YL = 2, 4
ROWS = 13
PAD = 16
FEATS = 144
FA, FB, FC = 80, 32, 32
WA, WB, WC = NZ * FA, NZ * FB, YL * FC
HALF = YH * NX * PAD
TALL = NC * HALF
D = YL * NZ * FEATS
VOCAB_DEV = 256
TOKENS = 208
ORDER = (1, 7, 2, 6, 3, 5, 4)
XORDER = (1, 3, 2)
FROM_X, FROM_Y, FROM_Z = 1, 4, 11
MISS = 18


def kernel(shard_hbm, weight_hbm, targets_hbm, loss, head_grad, hidden_grad,
           shard, targets, w_a, w_b, w_c, wt_a, wt_b, wt_c, hid_a, hid_b, hid_c, pad32, own_ab, own_c,
           z_rec, y_rec, line_a, line_b, line_c, stat, st_c, st_x, st_y, st_m, st_n, st_z, coef, keep_a, keep_b, keep_c,
           out_a, out_b, out_c, in_a, in_b, in_c, s1_a, s1_b, s1_c, r1_a, r1_b, r1_c, tk_a, tk_b, tk_c,
           to_a, to_b, to_c, ti_a, ti_b, ti_c, tr_a, tr_b, tr_c, s2_a, s2_b, s2_c, r2_a, r2_b, r2_c, s3_ab,
           s3_c, r3_ab, r3_c, g_a, g_b, g_c, local, gsem, ssem, rsem):
    s = lax.axis_index("section")
    t = lax.axis_index("tp")
    x, yh, c = s // 4, (s // 2) % 2, s % 2
    yl, z = t // NZ, t % NZ
    y = yh * YL + yl

    def at(x_, y_, z_, c_):
        return {"section": x_ * 4 + (y_ // YL) * 2 + c_, "tp": (y_ % YL) * NZ + z_}

    def z_peer(d):
        return at(x, y, (z + d) % NZ, c)

    def y_peer(d):
        return at(x, (y + d) % NY, z, c)

    def x_peer(d):
        return at((x + d) % NX, y, z, c)

    sent = []

    def go(src, dst, peer):
        n = len(sent)
        copy = pltpu.make_async_remote_copy(
            src_ref=src, dst_ref=dst, send_sem=ssem.at[n], recv_sem=rsem.at[n], device_id=peer, device_id_type=MESH)
        copy.start()
        sent.append(copy)
        return copy

    peers = [z_peer(d) for d in ORDER] + [y_peer(d) for d in ORDER] + [x_peer(d) for d in XORDER]
    partner = at(x, y, z, 1 - c)
    peers.append(partner)
    barrier = pltpu.get_barrier_semaphore()
    for peer in peers:
        pl.semaphore_signal(barrier, inc=1, device_id=peer, device_id_type=MESH)

    fetch_small = [
        pltpu.make_async_copy(shard_hbm, shard, local.at[0]),
        pltpu.make_async_copy(targets_hbm, targets, local.at[1]),
    ]
    fetch = [
        pltpu.make_async_copy(weight_hbm.at[:, :, 0:FA], w_a, local.at[2]),
        pltpu.make_async_copy(weight_hbm.at[:, :, FA:FA + FB], w_b, local.at[3]),
    ] + [
        pltpu.make_async_copy(weight_hbm.at[:, i, FA + FB:FEATS], w_c.at[i], local.at[4 + i]) for i in range(NZ)
    ]
    for copy in fetch_small + fetch:
        copy.start()

    for copy in fetch_small:
        copy.wait()
    pad32[...] = jnp.zeros_like(pad32)
    pad32[0, 0:ROWS, 0:FA + FB] = shard[:, 0:FA + FB].astype(F32)
    pad32[1, 0:ROWS, 0:FC] = shard[:, FA + FB:FEATS].astype(F32)
    mine_ab, mine_c = pad32[0].astype(BF16), pad32[1].astype(BF16)
    own_ab[...] = mine_ab
    own_c[...] = mine_c

    row = lax.broadcasted_iota(jnp.int32, (TALL, TOKENS), 0)
    section = (row // PAD) % NX * 4 + (row // (PAD * NX)) % YH * 2 + (row // HALF + c) % 2
    match = (section * ROWS + row % PAD == lax.broadcasted_iota(jnp.int32, (TALL, TOKENS), 1)) & (row % PAD < ROWS)
    goal = jnp.sum(jnp.where(match, targets[...].astype(F32), 0.0), axis=1, keepdims=True).astype(jnp.int32)
    vocab = lax.broadcasted_iota(jnp.int32, (TALL, VOCAB_DEV), 1) + (s * (YL * NZ) + t) * VOCAB_DEV
    hit = vocab == goal

    def dot(a, b, dims):
        return lax.dot_general(a, b, (dims, ((), ())), preferred_element_type=F32)

    nn, tn = ((1,), (0,)), ((0,), (0,))
    turn = [(yl + k) % YL for k in range(YL)]

    pl.semaphore_wait(barrier, len(peers))

    z_copies = [go(own_ab, z_rec.at[z], z_peer(d)) for d in ORDER]
    y_copies = [go(own_c, y_rec.at[y], y_peer(d)) for d in ORDER]
    z_rec[z] = mine_ab
    y_rec[y] = mine_c

    for copy in fetch:
        copy.wait()
    for j in range(YL):
        wt_a[j] = w_a[j].reshape(WA, VOCAB_DEV).T
        wt_b[j] = w_b[j].reshape(WB, VOCAB_DEV).T
    for j in range(NZ):
        wt_c[j] = w_c[j].reshape(WC, VOCAB_DEV).T

    def split(left, weight, keep, out):
        terms = dot(left, weight, nn)
        shape = (YH, NX, PAD, terms.shape[1])
        keep[...] = terms[0:HALF].astype(keep.dtype).reshape(shape)
        out[...] = terms[HALF:TALL].astype(BF16).reshape(shape)

    hot = hit.astype(F32).astype(BF16)
    t_core = []
    for k in range(YL):
        split(hot, wt_a[turn[k]], tk_a.at[k], to_a.at[k])
        t_core.append(go(to_a.at[k], ti_a.at[k], partner))
    for j in range(YL):
        split(hot, wt_b[j], tk_b.at[j], to_b.at[j])
        t_core.append(go(to_b.at[j], ti_b.at[j], partner))
    for j in range(NZ):
        split(hot, wt_c[j], tk_c.at[j], to_c.at[j])
        t_core.append(go(to_c.at[j], ti_c.at[j], partner))

    for copy in z_copies:
        copy.wait_recv()
    for i in range(NZ):
        part = z_rec[i].astype(F32)
        line_a[:, FA * i:FA * (i + 1)] = part[:, 0:FA]
        line_b[:, FB * i:FB * (i + 1)] = part[:, FA:FA + FB]
    hid_a[yl, 0, yh, x] = line_a[...].astype(BF16)
    hid_b[yl, 0, yh, x] = line_b[...].astype(BF16)

    block = hid_a.at[yl, 0, yh, x]
    a_y = {d: go(block, block, y_peer(d)) for d in ORDER}
    block = hid_b.at[yl, 0, yh, x]
    b_x = [go(block, block, x_peer(d)) for d in XORDER]
    for copy in y_copies:
        copy.wait_recv()
    for i in range(NY):
        line_c[i // YL, :, FC * (i % YL):FC * (i % YL + 1)] = y_rec[i].astype(F32)[:, 0:FC]
    hid_c[z, 0, :, x] = line_c[...].astype(BF16)
    block = hid_c.at[z, 0, :, x]
    c_x = [go(block, block, x_peer(d)) for d in XORDER]

    across = []
    a_x = []

    def pass_a(d):
        from_y = (y + NY - d) % NY
        block = hid_a.at[from_y % YL, 0, from_y // YL, x]
        for dx in XORDER:
            a_x.append((d, dx, go(block, block, x_peer(dx))))
        across.append(go(block, hid_a.at[from_y % YL, 1, from_y // YL, x], partner))

    pass_a(0)
    for copy in b_x:
        copy.wait_recv()
    block = hid_b.at[yl, 0, yh]
    b_y = [(d, go(block, block, y_peer(d))) for d in ORDER]
    across.append(go(block, hid_b.at[yl, 1, yh], partner))
    for copy in c_x:
        copy.wait_recv()
    block = hid_c.at[z, 0]
    c_z = [(d, go(block, block, z_peer(d))) for d in ORDER]
    across.append(go(block, hid_c.at[z, 1], partner))
    for d in ORDER:
        a_y[d].wait_recv()
        pass_a(d)

    def wide_a(src, dst, k):
        return [go(src.at[k, :, (x + d) % NX], dst.at[d, k], x_peer(d)) for d in XORDER]

    def wide_b(src, dst):
        return [go(src.at[(y + d) % NY % YL, (y + d) % NY // YL], dst.at[d], y_peer(d)) for d in ORDER]

    def wide_c(src, dst):
        return [go(src.at[(z + d) % NZ], dst.at[d], z_peer(d)) for d in ORDER]

    for copy in t_core:
        copy.wait_recv()
    for keep, into in ((tk_a, ti_a), (tk_b, ti_b), (tk_c, ti_c)):
        for j in range(keep.shape[0]):
            keep[j] = keep[j] + into[j]
    ta_x = [wide_a(tk_a, tr_a, k) for k in range(YL)]

    for d, copy in b_y:
        copy.wait_recv()
        from_y = (y + NY - d) % NY
        across.append(go(hid_b.at[from_y % YL, 0, from_y // YL], hid_b.at[from_y % YL, 1, from_y // YL], partner))
    for d, copy in c_z:
        copy.wait_recv()
        from_z = (z + NZ - d) % NZ
        across.append(go(hid_c.at[from_z, 0], hid_c.at[from_z, 1], partner))
    for d, dx, copy in a_x:
        copy.wait_recv()
        from_y, from_x = (y + NY - d) % NY, (x + NX - dx) % NX
        across.append(go(hid_a.at[from_y % YL, 0, from_y // YL, from_x],
                         hid_a.at[from_y % YL, 1, from_y // YL, from_x], partner))
    tb_y = wide_b(tk_b, tr_b)
    tc_z = wide_c(tk_c, tr_c)
    for copy in across:
        copy.wait_recv()

    def rows_a(j):
        return hid_a[j].reshape(TALL, WA)

    def rows_b(j):
        return hid_b[j].reshape(TALL, WB)

    def rows_c(j):
        return hid_c[j].reshape(TALL, WC)

    logits = sum(dot(rows_a(j), w_a[j].reshape(WA, VOCAB_DEV), nn) + dot(rows_b(j), w_b[j].reshape(WB, VOCAB_DEV), nn)
                 for j in range(YL))
    logits = logits + sum(dot(rows_c(j), w_c[j].reshape(WC, VOCAB_DEV), nn) for j in range(NZ))
    top = jnp.max(logits, axis=1, keepdims=True)
    shifted = jnp.exp(logits - top)
    rest = jnp.sum(jnp.where(hit, 0.0, shifted), axis=1, keepdims=True)
    aim = jnp.sum(jnp.where(hit, shifted, 0.0), axis=1, keepdims=True)
    picked = jnp.sum(jnp.where(hit, logits, 0.0), axis=1, keepdims=True)

    lane = lax.broadcasted_iota(jnp.int32, (TALL, 128), 1)
    columns = jnp.where(lane == 0, top, jnp.where(lane == 1, rest, jnp.where(lane == 2, picked, jnp.where(
        lane == 3, aim, 0.0))))
    tall = columns.T[0:8, :]
    stat[0] = tall
    stat[3] = jnp.concatenate([tall[:, HALF:TALL], tall[:, 0:HALF]], axis=1)

    def merge(parts):
        best = functools.reduce(jnp.maximum, [p[0:1, :] for p in parts])
        scale = [jnp.exp(p[0:1, :] - best) for p in parts]
        rest_ = sum(p[1:2, :] * f for p, f in zip(parts, scale))
        pick_ = sum(p[2:3, :] for p in parts)
        aim_ = sum(p[3:4, :] * f for p, f in zip(parts, scale))
        return jnp.concatenate([best, rest_, pick_, aim_, jnp.zeros((4, TALL), F32)], axis=0)

    def columns_of(rows):
        full = jnp.concatenate(rows + [jnp.zeros((128 - len(rows), TALL), F32)], axis=0)
        return full.T

    mate = go(stat.at[3], st_c, partner)

    others = jnp.where(hit, 0.0, shifted).astype(BF16)
    core_a, core_b, core_c = [], [], []
    for k in range(YL):
        split(others, wt_a[turn[k]], keep_a.at[k], out_a.at[k])
        core_a.append(go(out_a.at[k], in_a.at[k], partner))
    mate.wait_recv()
    theirs = st_c[...]
    pair = merge([tall, theirs])
    stat[1] = pair
    to_x = [go(stat.at[1], st_x.at[i], x_peer(d)) for i, d in enumerate(XORDER)]
    to_y = [go(stat.at[1], st_m.at[i], y_peer(d)) for i, d in enumerate(ORDER)]
    to_z = [go(stat.at[1], st_n.at[i], z_peer(d)) for i, d in enumerate(ORDER)]
    for j in range(YL):
        split(others, wt_b[j], keep_b.at[j], out_b.at[j])
        core_b.append(go(out_b.at[j], in_b.at[j], partner))
    for j in range(NZ):
        split(others, wt_c[j], keep_c.at[j], out_c.at[j])
        core_c.append(go(out_c.at[j], in_c.at[j], partner))
    both = columns_of([jnp.exp(p[0:1, :] - pair[0:1, :]) for p in (tall, theirs)])
    both = both[0:HALF].reshape(YH, NX, PAD, 128)
    f_own, f_in = both[..., 0:1], both[..., 1:2]

    def add_core(copy, keep, into, send):
        copy.wait_recv()
        terms = keep[...] * f_own + into[...].astype(F32) * f_in
        keep[...] = terms
        send[...] = terms.astype(BF16)

    a_x = []
    for k in range(YL):
        add_core(core_a[k], keep_a.at[k], in_a.at[k], s1_a.at[k])
        a_x.append(wide_a(s1_a, r1_a, k))
    for copy in to_x:
        copy.wait_recv()
    near_x = [st_x[i] for i in range(len(XORDER))]
    line = merge([pair] + near_x)
    stat[2] = line
    along_y = [go(stat.at[2], st_y.at[i], y_peer(d)) for i, d in enumerate(ORDER)]
    for j in range(YL):
        add_core(core_b[j], keep_b.at[j], in_b.at[j], s1_b.at[j])
    b_y = wide_b(s1_b, r1_b)
    for j in range(NZ):
        add_core(core_c[j], keep_c.at[j], in_c.at[j], s1_c.at[j])
    c_z = wide_c(s1_c, r1_c)

    for copy in along_y:
        copy.wait_recv()
    plane = merge([line] + [st_y[i] for i in range(len(ORDER))])
    stat[4] = plane
    along_z = [go(stat.at[4], st_z.at[i], z_peer(d)) for i, d in enumerate(ORDER)]
    for copy in to_y + to_z + along_z:
        copy.wait_recv()
    whole = merge([plane] + [st_z[i] for i in range(len(ORDER))])
    highest, total = whole[0:1, :], whole[1:2, :] + whole[3:4, :]
    slot = lax.broadcasted_iota(jnp.int32, (1, TALL), 1)
    each = jnp.where(slot % PAD < ROWS, highest + jnp.log(total) - whole[2:3, :], 0.0)
    loss[0, 0] = jnp.sum(each) / TOKENS

    def factor(p):
        return jnp.exp(p[0:1, :] - highest) / total

    miss = (whole[1:2, :] / total).astype(BF16).astype(F32)
    near = near_x + [st_m[i] for i in range(len(ORDER))] + [st_n[i] for i in range(len(ORDER))]
    factors = columns_of([factor(p) for p in [pair] + near] + [miss, factor(tall)])
    coef[...] = factors[0:HALF].reshape(YH, NX, PAD, 128)
    probs = (shifted * factors[:, MISS + 1:MISS + 2]).astype(BF16)

    a_y = []
    f_x = coef[:, x]
    for k in range(YL):
        for copy in a_x[k] + ta_x[k]:
            copy.wait_recv()
        chunk = keep_a[k, :, x] * f_x[..., 0:1]
        chunk = chunk + sum(r1_a[d, k].astype(F32) * f_x[..., FROM_X + i:FROM_X + i + 1] for i, d in enumerate(XORDER))
        column = tk_a[k, :, x] + sum(tr_a[d, k] for d in XORDER)
        chunk = chunk - column.astype(F32) * f_x[..., MISS:MISS + 1]
        s2_a[k] = chunk.astype(BF16)
        if k == 0:
            keep_a[0, :, 0] = chunk
        for e in range(YH):
            if k or e:
                to = (yh + e) % YH
                a_y.append(go(s2_a.at[k, to], r2_a.at[e * YL + k], at(x, to * YL + turn[k], z, c)))
    for copy in b_y + tb_y:
        copy.wait_recv()
    f_y = coef[yh]
    column = tk_b[yl, yh] + sum(tr_b[d] for d in ORDER)
    sum_b = keep_b[yl, yh] * f_y[..., 0:1] - column.astype(F32) * f_y[..., MISS:MISS + 1]
    sum_b = sum_b + sum(r1_b[d].astype(F32) * f_y[..., FROM_Y + i:FROM_Y + i + 1] for i, d in enumerate(ORDER))
    s2_b[...] = sum_b.astype(BF16)
    keep_b[0, 0] = sum_b
    b_x = [go(s2_b.at[(x + d) % NX], r2_b.at[d], x_peer(d)) for d in XORDER]
    for copy in c_z + tc_z:
        copy.wait_recv()
    f_z = coef[...]
    column = tk_c[z] + sum(tr_c[d] for d in ORDER)
    sum_c = keep_c[z] * f_z[..., 0:1] - column.astype(F32) * f_z[..., MISS:MISS + 1]
    sum_c = sum_c + sum(r1_c[d].astype(F32) * f_z[..., FROM_Z + i:FROM_Z + i + 1] for i, d in enumerate(ORDER))
    s2_c[...] = sum_c.astype(BF16)
    keep_c[0] = sum_c
    c_x = [go(s2_c.at[:, (x + d) % NX], r2_c.at[d], x_peer(d)) for d in XORDER]

    for j in range(YL):
        g_a[j] = dot(rows_a(j), probs, tn).astype(BF16).reshape(NZ, FA, VOCAB_DEV)
        g_b[j] = dot(rows_b(j), probs, tn).astype(BF16).reshape(NZ, FB, VOCAB_DEV)
    for j in range(NZ):
        g_c[j] = dot(rows_c(j), probs, tn).astype(BF16).reshape(YL, FC, VOCAB_DEV)
    writes = [
        pltpu.make_async_copy(g_a, head_grad.at[:, :, 0:FA], gsem.at[0]),
        pltpu.make_async_copy(g_b, head_grad.at[:, :, FA:FA + FB], gsem.at[1]),
    ] + [
        pltpu.make_async_copy(g_c.at[i], head_grad.at[:, i, FA + FB:FEATS], gsem.at[2 + i]) for i in range(NZ)
    ]
    for write in writes:
        write.start()

    for copy in c_x:
        copy.wait_recv()
    part_c = keep_c[0, :, x] + sum(r2_c[d].astype(F32) for d in XORDER)
    for i in range(NY):
        s3_c[i, :, 0:FC] = part_c[i // YL, :, FC * (i % YL):FC * (i % YL + 1)]
    c_y = [go(s3_c.at[(y + d) % NY], r3_c.at[d], y_peer(d)) for d in ORDER]
    for copy in b_x:
        copy.wait_recv()
    part_b = keep_b[0, 0, x] + sum(r2_b[d].astype(F32) for d in XORDER)
    for copy in a_y:
        copy.wait_recv()
    part_a = keep_a[0, yh, 0] + sum(r2_a[n].astype(F32) for n in range(1, NY))
    for i in range(NZ):
        s3_ab[i, :, 0:FA] = part_a[:, FA * i:FA * (i + 1)]
        s3_ab[i, :, FA:FA + FB] = part_b[:, FB * i:FB * (i + 1)]
    ab_z = [go(s3_ab.at[(z + d) % NZ], r3_ab.at[d], z_peer(d)) for d in ORDER]
    for copy in c_y:
        copy.wait_recv()
    done_c = s3_c[y][:, 0:FC] + sum(r3_c[d][:, 0:FC] for d in ORDER)
    hidden_grad[:, FA + FB:FEATS] = done_c[0:ROWS].astype(BF16)
    for copy in ab_z:
        copy.wait_recv()
    done_ab = s3_ab[z][:, 0:FA + FB] + sum(r3_ab[d][:, 0:FA + FB] for d in ORDER)
    hidden_grad[:, 0:FA + FB] = done_ab[0:ROWS].astype(BF16)

    for copy in sent:
        copy.wait_send()
    for write in writes:
        write.wait()


def per_device(hidden, head_weight, targets):
    vmem = pl.BlockSpec(memory_space=pltpu.VMEM)
    hbm = pl.BlockSpec(memory_space=pltpu.HBM)
    v = pltpu.VMEM
    dma = pltpu.SemaphoreType.DMA
    halves = (YH, NX, PAD)
    loss, head_grad, hidden_grad = pl.pallas_call(
        kernel,
        out_shape=(
            jax.ShapeDtypeStruct((1, 1), F32),
            jax.ShapeDtypeStruct((YL, NZ, FEATS, VOCAB_DEV), BF16),
            jax.ShapeDtypeStruct((ROWS, FEATS), BF16),
        ),
        in_specs=[hbm, hbm, hbm],
        out_specs=(pl.BlockSpec(memory_space=pltpu.SMEM), pl.BlockSpec(memory_space=pl.ANY), vmem),
        scratch_shapes=[
            v((ROWS, FEATS), BF16), v((1, TOKENS), jnp.int32),
            v((YL, NZ, FA, VOCAB_DEV), BF16), v((YL, NZ, FB, VOCAB_DEV), BF16), v((NZ, YL, FC, VOCAB_DEV), BF16),
            v((YL, VOCAB_DEV, WA), BF16), v((YL, VOCAB_DEV, WB), BF16), v((NZ, VOCAB_DEV, WC), BF16),
            v((YL, NC) + halves + (WA,), BF16), v((YL, NC) + halves + (WB,), BF16), v((NZ, NC) + halves + (WC,), BF16),
            v((2, PAD, 128), F32), v((PAD, 128), BF16), v((PAD, 128), BF16),
            v((NZ, PAD, 128), BF16), v((NY, PAD, 128), BF16),
            v((PAD, WA), F32), v((PAD, WB), F32), v((YH, PAD, WC), F32),
            v((5, 8, TALL), F32), v((8, TALL), F32), v((3, 8, TALL), F32),
            v((7, 8, TALL), F32), v((7, 8, TALL), F32), v((7, 8, TALL), F32), v((7, 8, TALL), F32),
            v(halves + (128,), F32),
            v((YL,) + halves + (WA,), F32), v((YL,) + halves + (WB,), F32), v((NZ,) + halves + (WC,), F32),
            v((YL,) + halves + (WA,), BF16), v((YL,) + halves + (WB,), BF16), v((NZ,) + halves + (WC,), BF16),
            v((YL,) + halves + (WA,), BF16), v((YL,) + halves + (WB,), BF16), v((NZ,) + halves + (WC,), BF16),
            v((YL,) + halves + (WA,), BF16), v((YL,) + halves + (WB,), BF16), v((NZ,) + halves + (WC,), BF16),
            v((NX, YL, YH, PAD, WA), BF16), v((NY, NX, PAD, WB), BF16), v((NZ,) + halves + (WC,), BF16),
            v((YL,) + halves + (WA,), BF16), v((YL,) + halves + (WB,), BF16), v((NZ,) + halves + (WC,), BF16),
            v((YL,) + halves + (WA,), BF16), v((YL,) + halves + (WB,), BF16), v((NZ,) + halves + (WC,), BF16),
            v((YL,) + halves + (WA,), BF16), v((YL,) + halves + (WB,), BF16), v((NZ,) + halves + (WC,), BF16),
            v((NX, YL, YH, PAD, WA), BF16), v((NY, NX, PAD, WB), BF16), v((NZ,) + halves + (WC,), BF16),
            v((YL, YH, PAD, WA), BF16), v((NX, PAD, WB), BF16), v(halves + (WC,), BF16),
            v((NY, PAD, WA), BF16), v((NX, PAD, WB), BF16), v((NX, YH, PAD, WC), BF16),
            v((NZ, PAD, 128), F32), v((NY, PAD, 128), F32), v((NZ, PAD, 128), F32), v((NY, PAD, 128), F32),
            v((YL, NZ, FA, VOCAB_DEV), BF16), v((YL, NZ, FB, VOCAB_DEV), BF16), v((NZ, YL, FC, VOCAB_DEV), BF16),
            dma((12,)), dma((10,)), dma((260,)), dma((260,)),
        ],
        compiler_params=pltpu.CompilerParams(
            collective_id=0, has_side_effects=True, vmem_limit_bytes=44 * 2**20),
        name="output_layer",
    )(*[pltpu.with_memory_space_constraint(operand, pltpu.HBM) for operand in (
        hidden, head_weight.reshape(YL, NZ, FEATS, VOCAB_DEV), targets.reshape(1, TOKENS))])
    return loss.reshape(()), head_grad.reshape(D, VOCAB_DEV), hidden_grad


def solution(mesh):
    placed = (P("section", "tp"), P(None, ("section", "tp")), P())
    return jax.shard_map(
        per_device,
        mesh=mesh,
        in_specs=placed,
        out_specs=(P(), P(None, ("section", "tp")), P("section", "tp")),
        check_vma=False,
    )
```

```python
import functools

import jax
import jax.numpy as jnp
from jax import lax
from jax.experimental import pallas as pl
from jax.experimental.pallas import tpu as pltpu
from jax.sharding import PartitionSpec as P

MESH = pl.DeviceIdType.MESH
F32 = jnp.float32
BF16 = jnp.bfloat16
NX, NY, NZ, NC = 4, 8, 8, 2
YH, YL = 2, 4
ROWS = 13
PAD = 16
FEATS = 144
FA, FB, FC = 80, 32, 32
WA, WB, WC = NZ * FA, NZ * FB, YL * FC
HALF = YH * NX * PAD
TALL = NC * HALF
D = YL * NZ * FEATS
VOCAB_DEV = 256
VOCAB_CHIP = NC * VOCAB_DEV
TOKENS = 208
ORDER = (1, 7, 2, 6, 3, 5, 4)
XORDER = (1, 3, 2)
FROM_X, FROM_Y, FROM_Z = 1, 4, 11
MISS = 18


def kernel(shard_hbm, weight_hbm, targets_hbm, loss, head_grad, hidden_grad,
           shard, targets, w_a, w_b, w_c, p_a, p_b, p_c, wt_a, wt_b, wt_c, hid_a, hid_b, hid_c, pad32,
           own_ab, own_c, z_rec, y_rec, line_a, line_b, line_c, stat, st_x, st_m, st_n, st_y, st_z, coef,
           keep_a, keep_b, keep_c, s1_a, s1_b, s1_c, r1_a, r1_b, r1_c, tk_a, tk_b, tk_c, tr_a, tr_b, tr_c,
           s2_a, s2_b, s2_c, r2_a, r2_b, r2_c, s3_ab, s3_c, r3_ab, r3_c, g_a, g_b, g_c, p_out, p_in, l_out,
           l_in, local, gsem, ssem, rsem):
    s = lax.axis_index("section")
    t = lax.axis_index("tp")
    x, yh, c = s // 4, (s // 2) % 2, s % 2
    yl, z = t // NZ, t % NZ
    y = yh * YL + yl

    def at(x_, y_, z_, c_):
        return {"section": x_ * 4 + (y_ // YL) * 2 + c_, "tp": (y_ % YL) * NZ + z_}

    def z_peer(d):
        return at(x, y, (z + d) % NZ, c)

    def y_peer(d):
        return at(x, (y + d) % NY, z, c)

    def x_peer(d):
        return at((x + d) % NX, y, z, c)

    sent = []

    def go(src, dst, peer):
        n = len(sent)
        copy = pltpu.make_async_remote_copy(
            src_ref=src, dst_ref=dst, send_sem=ssem.at[n], recv_sem=rsem.at[n], device_id=peer, device_id_type=MESH)
        copy.start()
        sent.append(copy)
        return copy

    peers = [z_peer(d) for d in ORDER] + [y_peer(d) for d in ORDER] + [x_peer(d) for d in XORDER]
    partner = at(x, y, z, 1 - c)
    peers.append(partner)
    barrier = pltpu.get_barrier_semaphore()
    for peer in peers:
        pl.semaphore_signal(barrier, inc=1, device_id=peer, device_id_type=MESH)

    fetch_small = [
        pltpu.make_async_copy(shard_hbm, shard, local.at[0]),
        pltpu.make_async_copy(targets_hbm, targets, local.at[1]),
    ]
    fetch = [
        pltpu.make_async_copy(weight_hbm.at[:, :, 0:FA], w_a, local.at[2]),
        pltpu.make_async_copy(weight_hbm.at[:, :, FA:FA + FB], w_b, local.at[3]),
    ] + [
        pltpu.make_async_copy(weight_hbm.at[:, i, FA + FB:FEATS], w_c.at[i], local.at[4 + i]) for i in range(NZ)
    ]
    for copy in fetch_small + fetch:
        copy.start()

    for copy in fetch_small:
        copy.wait()
    pad32[...] = jnp.zeros_like(pad32)
    pad32[0, 0:ROWS, 0:FA + FB] = shard[:, 0:FA + FB].astype(F32)
    pad32[1, 0:ROWS, 0:FC] = shard[:, FA + FB:FEATS].astype(F32)
    mine_ab, mine_c = pad32[0].astype(BF16), pad32[1].astype(BF16)
    own_ab[...] = mine_ab
    own_c[...] = mine_c

    row = lax.broadcasted_iota(jnp.int32, (HALF, TOKENS), 0)
    section = (row // PAD) % NX * 4 + row // (PAD * NX) * 2 + c
    match = (section * ROWS + row % PAD == lax.broadcasted_iota(jnp.int32, (HALF, TOKENS), 1)) & (row % PAD < ROWS)
    goal = jnp.sum(jnp.where(match, targets[...].astype(F32), 0.0), axis=1, keepdims=True).astype(jnp.int32)
    entry = lax.broadcasted_iota(jnp.int32, (HALF, VOCAB_CHIP), 1)
    mine = (s * (YL * NZ) + t) * VOCAB_DEV
    mate = ((s + 1 - 2 * c) * (YL * NZ) + t) * VOCAB_DEV
    hit = jnp.where(entry < VOCAB_DEV, entry + mine, entry + (mate - VOCAB_DEV)) == goal

    def dot(a, b, dims):
        return lax.dot_general(a, b, (dims, ((), ())), preferred_element_type=F32)

    nn, tn = ((1,), (0,)), ((0,), (0,))
    halves = (YH, NX, PAD)
    turn = [(yl + k) % YL for k in range(YL)]

    pl.semaphore_wait(barrier, len(peers))

    z_copies = [go(own_ab, z_rec.at[z], z_peer(d)) for d in ORDER]
    y_copies = [go(own_c, y_rec.at[y], y_peer(d)) for d in ORDER]
    z_rec[z] = mine_ab
    y_rec[y] = mine_c

    for copy in fetch:
        copy.wait()
    w_core = [go(src, dst, partner) for src, dst in ((w_a, p_a), (w_b, p_b), (w_c, p_c))]

    def transpose(parts, at_row):
        rows = pl.ds(at_row, VOCAB_DEV)
        for part, into in zip(parts, (wt_a, wt_b, wt_c)):
            for j in range(into.shape[0]):
                into[j, rows] = part[j].reshape(into.shape[2], VOCAB_DEV).T

    transpose((w_a, w_b, w_c), 0)
    for copy in z_copies:
        copy.wait_recv()
    for i in range(NZ):
        part = z_rec[i].astype(F32)
        line_a[:, FA * i:FA * (i + 1)] = part[:, 0:FA]
        line_b[:, FB * i:FB * (i + 1)] = part[:, FA:FA + FB]
    hid_a[yl, 0, yh, x] = line_a[...].astype(BF16)
    hid_b[yl, 0, yh, x] = line_b[...].astype(BF16)

    block = hid_a.at[yl, 0, yh, x]
    a_y = {d: go(block, block, y_peer(d)) for d in ORDER}
    block = hid_b.at[yl, 0, yh, x]
    b_x = [go(block, block, x_peer(d)) for d in XORDER]
    for copy in y_copies:
        copy.wait_recv()
    for i in range(NY):
        line_c[i // YL, :, FC * (i % YL):FC * (i % YL + 1)] = y_rec[i].astype(F32)[:, 0:FC]
    hid_c[z, 0, :, x] = line_c[...].astype(BF16)
    block = hid_c.at[z, 0, :, x]
    c_x = [go(block, block, x_peer(d)) for d in XORDER]

    a_x = []

    def pass_a(d):
        from_y = (y + NY - d) % NY
        block = hid_a.at[from_y % YL, 0, from_y // YL, x]
        a_x.extend([go(block, block, x_peer(dx)) for dx in XORDER])

    pass_a(0)
    for copy in b_x:
        copy.wait_recv()
    block = hid_b.at[yl, 0, yh]
    b_y = [go(block, block, y_peer(d)) for d in ORDER]
    for copy in c_x:
        copy.wait_recv()
    block = hid_c.at[z, 0]
    c_z = [go(block, block, z_peer(d)) for d in ORDER]
    for d in ORDER:
        a_y[d].wait_recv()
        pass_a(d)

    def wide_a(src, dst, k):
        return [go(src.at[k, :, (x + d) % NX], dst.at[d, k], x_peer(d)) for d in XORDER]

    def wide_b(src, dst):
        return [go(src.at[(y + d) % NY % YL, (y + d) % NY // YL], dst.at[d], y_peer(d)) for d in ORDER]

    def wide_c(src, dst):
        return [go(src.at[(z + d) % NZ], dst.at[d], z_peer(d)) for d in ORDER]

    for copy in w_core:
        copy.wait_recv()
    transpose((p_a, p_b, p_c), VOCAB_DEV)
    hot = hit.astype(F32).astype(BF16)
    for k in range(YL):
        tk_a[k] = dot(hot, wt_a[turn[k]], nn).astype(BF16).reshape(halves + (WA,))
    ta_x = [wide_a(tk_a, tr_a, k) for k in range(YL)]
    for j in range(YL):
        tk_b[j] = dot(hot, wt_b[j], nn).astype(BF16).reshape(halves + (WB,))
    for j in range(NZ):
        tk_c[j] = dot(hot, wt_c[j], nn).astype(BF16).reshape(halves + (WC,))

    def add_logits(sums, hid, parts):
        for j in range(hid.shape[0]):
            left = hid[j, 0].reshape(HALF, hid.shape[-1])
            sums = [so + dot(left, part[j].reshape(hid.shape[-1], VOCAB_DEV), nn) for so, part in zip(sums, parts)]
        return sums

    for copy in a_x:
        copy.wait_recv()
    sums = add_logits([jnp.zeros((HALF, VOCAB_DEV), F32)] * NC, hid_a, (w_a, p_a))
    for copy in b_y:
        copy.wait_recv()
    sums = add_logits(sums, hid_b, (w_b, p_b))
    for copy in c_z:
        copy.wait_recv()
    tb_y = wide_b(tk_b, tr_b)
    tc_z = wide_c(tk_c, tr_c)
    sums = add_logits(sums, hid_c, (w_c, p_c))
    logits = jnp.concatenate(sums, axis=1)

    top = jnp.max(logits, axis=1, keepdims=True)
    shifted = jnp.exp(logits - top)
    rest = jnp.sum(jnp.where(hit, 0.0, shifted), axis=1, keepdims=True)
    aim = jnp.sum(jnp.where(hit, shifted, 0.0), axis=1, keepdims=True)
    picked = jnp.sum(jnp.where(hit, logits, 0.0), axis=1, keepdims=True)
    others = jnp.where(hit, 0.0, shifted).astype(BF16)

    lane = lax.broadcasted_iota(jnp.int32, (HALF, 128), 1)
    columns = jnp.where(lane == 0, top, jnp.where(lane == 1, rest, jnp.where(lane == 2, picked, jnp.where(
        lane == 3, aim, 0.0))))
    tall = columns.T[0:8, :]
    stat[0] = tall

    def merge(parts):
        best = functools.reduce(jnp.maximum, [p[0:1, :] for p in parts])
        scale = [jnp.exp(p[0:1, :] - best) for p in parts]
        rest_ = sum(p[1:2, :] * f for p, f in zip(parts, scale))
        pick_ = sum(p[2:3, :] for p in parts)
        aim_ = sum(p[3:4, :] * f for p, f in zip(parts, scale))
        return jnp.concatenate([best, rest_, pick_, aim_, jnp.zeros((4, HALF), F32)], axis=0)

    def columns_of(rows):
        full = jnp.concatenate(rows + [jnp.zeros((128 - len(rows), HALF), F32)], axis=0)
        return full.T

    to_x = [go(stat.at[0], st_x.at[i], x_peer(d)) for i, d in enumerate(XORDER)]
    to_y = [go(stat.at[0], st_m.at[i], y_peer(d)) for i, d in enumerate(ORDER)]
    to_z = [go(stat.at[0], st_n.at[i], z_peer(d)) for i, d in enumerate(ORDER)]

    def term(weight, keep, send):
        terms = dot(others, weight, nn).reshape(keep.shape)
        keep[...] = terms
        send[...] = terms.astype(BF16)

    a_x = []
    for k in range(YL):
        term(wt_a[turn[k]], keep_a.at[k], s1_a.at[k])
        a_x.append(wide_a(s1_a, r1_a, k))
    for j in range(YL):
        term(wt_b[j], keep_b.at[j], s1_b.at[j])
    b_y = wide_b(s1_b, r1_b)
    for j in range(NZ):
        term(wt_c[j], keep_c.at[j], s1_c.at[j])
    c_z = wide_c(s1_c, r1_c)
    for copy in to_x:
        copy.wait_recv()
    near_x = [st_x[i] for i in range(len(XORDER))]
    line = merge([tall] + near_x)
    stat[1] = line
    along_y = [go(stat.at[1], st_y.at[i], y_peer(d)) for i, d in enumerate(ORDER)]
    h_core = [go(hid.at[:, 0], hid.at[:, 1], partner) for hid in (hid_a, hid_b, hid_c)]

    for copy in along_y:
        copy.wait_recv()
    plane = merge([line] + [st_y[i] for i in range(len(ORDER))])
    stat[2] = plane
    along_z = [go(stat.at[2], st_z.at[i], z_peer(d)) for i, d in enumerate(ORDER)]
    for copy in to_y + to_z + along_z:
        copy.wait_recv()
    whole = merge([plane] + [st_z[i] for i in range(len(ORDER))])
    highest, total = whole[0:1, :], whole[1:2, :] + whole[3:4, :]
    slot = lax.broadcasted_iota(jnp.int32, (1, HALF), 1)
    each = jnp.where(slot % PAD < ROWS, highest + jnp.log(total) - whole[2:3, :], 0.0)

    def factor(p):
        return jnp.exp(p[0:1, :] - highest) / total

    miss = (whole[1:2, :] / total).astype(BF16).astype(F32)
    near = near_x + [st_m[i] for i in range(len(ORDER))] + [st_n[i] for i in range(len(ORDER))]
    factors = columns_of([factor(p) for p in [tall] + near] + [miss])
    coef[...] = factors.reshape(halves + (128,))

    a_y = []
    f_x = coef[:, x]
    for k in range(YL):
        for copy in a_x[k] + ta_x[k]:
            copy.wait_recv()
        chunk = keep_a[k, :, x] * f_x[..., 0:1]
        chunk = chunk + sum(r1_a[d, k].astype(F32) * f_x[..., FROM_X + i:FROM_X + i + 1] for i, d in enumerate(XORDER))
        column = tk_a[k, :, x] + sum(tr_a[d, k] for d in XORDER)
        chunk = chunk - column.astype(F32) * f_x[..., MISS:MISS + 1]
        s2_a[k] = chunk.astype(BF16)
        if k == 0:
            keep_a[0, :, 0] = chunk
        for e in range(YH):
            if k or e:
                to = (yh + e) % YH
                a_y.append(go(s2_a.at[k, to], r2_a.at[e * YL + k], at(x, to * YL + turn[k], z, c)))
    for copy in b_y + tb_y:
        copy.wait_recv()
    f_y = coef[yh]
    column = tk_b[yl, yh] + sum(tr_b[d] for d in ORDER)
    sum_b = keep_b[yl, yh] * f_y[..., 0:1] - column.astype(F32) * f_y[..., MISS:MISS + 1]
    sum_b = sum_b + sum(r1_b[d].astype(F32) * f_y[..., FROM_Y + i:FROM_Y + i + 1] for i, d in enumerate(ORDER))
    s2_b[...] = sum_b.astype(BF16)
    keep_b[0, 0] = sum_b
    b_x = [go(s2_b.at[(x + d) % NX], r2_b.at[d], x_peer(d)) for d in XORDER]
    for copy in c_z + tc_z:
        copy.wait_recv()
    f_z = coef[...]
    column = tk_c[z] + sum(tr_c[d] for d in ORDER)
    sum_c = keep_c[z] * f_z[..., 0:1] - column.astype(F32) * f_z[..., MISS:MISS + 1]
    sum_c = sum_c + sum(r1_c[d].astype(F32) * f_z[..., FROM_Z + i:FROM_Z + i + 1] for i, d in enumerate(ORDER))
    s2_c[...] = sum_c.astype(BF16)
    keep_c[0] = sum_c
    c_x = [go(s2_c.at[:, (x + d) % NX], r2_c.at[d], x_peer(d)) for d in XORDER]

    probs = (shifted * factors[:, 0:1]).astype(BF16)
    p_out[...] = probs[:, VOCAB_DEV:VOCAB_CHIP]
    l_out[...] = jnp.concatenate([each, jnp.zeros((7, HALF), F32)], axis=0)
    swap = h_core + [go(p_out, p_in, partner), go(l_out, l_in, partner)]
    for copy in swap:
        copy.wait_recv()
    loss[0, 0] = (jnp.sum(each) + jnp.sum(l_in[0:1, :])) / TOKENS
    probs = jnp.concatenate([probs[:, 0:VOCAB_DEV], p_in[...]], axis=0)
    for hid, grad in ((hid_a, g_a), (hid_b, g_b), (hid_c, g_c)):
        for j in range(hid.shape[0]):
            left = hid[j].reshape(TALL, hid.shape[-1])
            grad[j] = dot(left, probs, tn).astype(BF16).reshape(grad.shape[1:])
    writes = [
        pltpu.make_async_copy(g_a, head_grad.at[:, :, 0:FA], gsem.at[0]),
        pltpu.make_async_copy(g_b, head_grad.at[:, :, FA:FA + FB], gsem.at[1]),
    ] + [
        pltpu.make_async_copy(g_c.at[i], head_grad.at[:, i, FA + FB:FEATS], gsem.at[2 + i]) for i in range(NZ)
    ]
    for write in writes:
        write.start()

    for copy in c_x:
        copy.wait_recv()
    part_c = keep_c[0, :, x] + sum(r2_c[d].astype(F32) for d in XORDER)
    for i in range(NY):
        s3_c[i, :, 0:FC] = part_c[i // YL, :, FC * (i % YL):FC * (i % YL + 1)]
    c_y = [go(s3_c.at[(y + d) % NY], r3_c.at[d], y_peer(d)) for d in ORDER]
    for copy in b_x:
        copy.wait_recv()
    part_b = keep_b[0, 0, x] + sum(r2_b[d].astype(F32) for d in XORDER)
    for copy in a_y:
        copy.wait_recv()
    part_a = keep_a[0, yh, 0] + sum(r2_a[n].astype(F32) for n in range(1, NY))
    for i in range(NZ):
        s3_ab[i, :, 0:FA] = part_a[:, FA * i:FA * (i + 1)]
        s3_ab[i, :, FA:FA + FB] = part_b[:, FB * i:FB * (i + 1)]
    ab_z = [go(s3_ab.at[(z + d) % NZ], r3_ab.at[d], z_peer(d)) for d in ORDER]
    for copy in c_y:
        copy.wait_recv()
    done_c = s3_c[y][:, 0:FC] + sum(r3_c[d][:, 0:FC] for d in ORDER)
    hidden_grad[:, FA + FB:FEATS] = done_c[0:ROWS].astype(BF16)
    for copy in ab_z:
        copy.wait_recv()
    done_ab = s3_ab[z][:, 0:FA + FB] + sum(r3_ab[d][:, 0:FA + FB] for d in ORDER)
    hidden_grad[:, 0:FA + FB] = done_ab[0:ROWS].astype(BF16)

    for copy in sent:
        copy.wait_send()
    for write in writes:
        write.wait()


def per_device(hidden, head_weight, targets):
    vmem = pl.BlockSpec(memory_space=pltpu.VMEM)
    hbm = pl.BlockSpec(memory_space=pltpu.HBM)
    v = pltpu.VMEM
    dma = pltpu.SemaphoreType.DMA
    halves = (YH, NX, PAD)
    loss, head_grad, hidden_grad = pl.pallas_call(
        kernel,
        out_shape=(
            jax.ShapeDtypeStruct((1, 1), F32),
            jax.ShapeDtypeStruct((YL, NZ, FEATS, VOCAB_DEV), BF16),
            jax.ShapeDtypeStruct((ROWS, FEATS), BF16),
        ),
        in_specs=[hbm, hbm, hbm],
        out_specs=(pl.BlockSpec(memory_space=pltpu.SMEM), pl.BlockSpec(memory_space=pl.ANY), vmem),
        scratch_shapes=[
            v((ROWS, FEATS), BF16), v((1, TOKENS), jnp.int32),
            v((YL, NZ, FA, VOCAB_DEV), BF16), v((YL, NZ, FB, VOCAB_DEV), BF16), v((NZ, YL, FC, VOCAB_DEV), BF16),
            v((YL, NZ, FA, VOCAB_DEV), BF16), v((YL, NZ, FB, VOCAB_DEV), BF16), v((NZ, YL, FC, VOCAB_DEV), BF16),
            v((YL, VOCAB_CHIP, WA), BF16), v((YL, VOCAB_CHIP, WB), BF16), v((NZ, VOCAB_CHIP, WC), BF16),
            v((YL, NC) + halves + (WA,), BF16), v((YL, NC) + halves + (WB,), BF16), v((NZ, NC) + halves + (WC,), BF16),
            v((2, PAD, 128), F32), v((PAD, 128), BF16), v((PAD, 128), BF16),
            v((NZ, PAD, 128), BF16), v((NY, PAD, 128), BF16),
            v((PAD, WA), F32), v((PAD, WB), F32), v((YH, PAD, WC), F32),
            v((3, 8, HALF), F32), v((3, 8, HALF), F32), v((7, 8, HALF), F32), v((7, 8, HALF), F32),
            v((7, 8, HALF), F32), v((7, 8, HALF), F32),
            v(halves + (128,), F32),
            v((YL,) + halves + (WA,), F32), v((YL,) + halves + (WB,), F32), v((NZ,) + halves + (WC,), F32),
            v((YL,) + halves + (WA,), BF16), v((YL,) + halves + (WB,), BF16), v((NZ,) + halves + (WC,), BF16),
            v((NX, YL, YH, PAD, WA), BF16), v((NY, NX, PAD, WB), BF16), v((NZ,) + halves + (WC,), BF16),
            v((YL,) + halves + (WA,), BF16), v((YL,) + halves + (WB,), BF16), v((NZ,) + halves + (WC,), BF16),
            v((NX, YL, YH, PAD, WA), BF16), v((NY, NX, PAD, WB), BF16), v((NZ,) + halves + (WC,), BF16),
            v((YL, YH, PAD, WA), BF16), v((NX, PAD, WB), BF16), v(halves + (WC,), BF16),
            v((NY, PAD, WA), BF16), v((NX, PAD, WB), BF16), v((NX, YH, PAD, WC), BF16),
            v((NZ, PAD, 128), F32), v((NY, PAD, 128), F32), v((NZ, PAD, 128), F32), v((NY, PAD, 128), F32),
            v((YL, NZ, FA, VOCAB_DEV), BF16), v((YL, NZ, FB, VOCAB_DEV), BF16), v((NZ, YL, FC, VOCAB_DEV), BF16),
            v((HALF, VOCAB_DEV), BF16), v((HALF, VOCAB_DEV), BF16), v((8, HALF), F32), v((8, HALF), F32),
            dma((12,)), dma((10,)), dma((192,)), dma((192,)),
        ],
        compiler_params=pltpu.CompilerParams(
            collective_id=0, has_side_effects=True, vmem_limit_bytes=44 * 2**20),
        name="output_layer",
    )(*[pltpu.with_memory_space_constraint(operand, pltpu.HBM) for operand in (
        hidden, head_weight.reshape(YL, NZ, FEATS, VOCAB_DEV), targets.reshape(1, TOKENS))])
    return loss.reshape(()), head_grad.reshape(D, VOCAB_DEV), hidden_grad


def solution(mesh):
    placed = (P("section", "tp"), P(None, ("section", "tp")), P())
    return jax.shard_map(
        per_device,
        mesh=mesh,
        in_specs=placed,
        out_specs=(P(), P(None, ("section", "tp")), P("section", "tp")),
        check_vma=False,
    )
```

```python
import functools

import jax
import jax.numpy as jnp
from jax import lax
from jax.experimental import pallas as pl
from jax.experimental.pallas import tpu as pltpu
from jax.sharding import PartitionSpec as P

MESH = pl.DeviceIdType.MESH
F32 = jnp.float32
BF16 = jnp.bfloat16
NX, NY, NZ, NC = 4, 8, 8, 2
YH, YL = 2, 4
ROWS = 13
PAD = 16
FEATS = 144
FA, FB, FC = 80, 32, 32
WA, WB, WC = NZ * FA, NZ * FB, YL * FC
HALF = YH * NX * PAD
TALL = NC * HALF
D = YL * NZ * FEATS
VOCAB_DEV = 256
VOCAB_CHIP = NC * VOCAB_DEV
TOKENS = 208
ORDER = (1, 7, 2, 6, 3, 5, 4)
XORDER = (1, 3, 2)
OWN = NY + NX + NX
MISS = OWN + 1


def kernel(shard_hbm, weight_hbm, targets_hbm, loss, head_grad, hidden_grad,
           shard, targets, w_a, w_b, w_c, p_a, p_b, p_c, wt_a, wt_b, wt_c, hid_a, hid_b, hid_c, pad32,
           own_ab, own_c, z_rec, y_rec, line_a, line_b, line_c, stat, st_x, st_m, st_n, st_b, st_c, st_y, st_z, coef,
           keep_a, keep_b, keep_c, s1_a, s1_b, s1_c, r1_a, r1_b, r1_c, tk_a, tk_b, tk_c, tr_a, tr_b, tr_c,
           t2_a, t2_b, t2_c, t3_a, t3_b, t3_c, s2_a, s2_b, s2_c, r2_a, r2_b, r2_c, s3_ab, s3_c, r3_ab, r3_c, g_a, g_b, g_c, p_out, p_in, l_out,
           l_in, local, gsem, ssem, rsem):
    s = lax.axis_index("section")
    t = lax.axis_index("tp")
    x, yh, c = s // 4, (s // 2) % 2, s % 2
    yl, z = t // NZ, t % NZ
    y = yh * YL + yl

    def at(x_, y_, z_, c_):
        return {"section": x_ * 4 + (y_ // YL) * 2 + c_, "tp": (y_ % YL) * NZ + z_}

    def z_peer(d):
        return at(x, y, (z + d) % NZ, c)

    def y_peer(d):
        return at(x, (y + d) % NY, z, c)

    def x_peer(d):
        return at((x + d) % NX, y, z, c)

    sent = []

    def go(src, dst, peer):
        n = len(sent)
        copy = pltpu.make_async_remote_copy(
            src_ref=src, dst_ref=dst, send_sem=ssem.at[n], recv_sem=rsem.at[n], device_id=peer, device_id_type=MESH)
        copy.start()
        sent.append(copy)
        return copy

    peers = [z_peer(d) for d in ORDER] + [y_peer(d) for d in ORDER] + [x_peer(d) for d in XORDER]
    partner = at(x, y, z, 1 - c)
    peers.append(partner)
    barrier = pltpu.get_barrier_semaphore()
    for peer in peers:
        pl.semaphore_signal(barrier, inc=1, device_id=peer, device_id_type=MESH)

    fetch_small = [
        pltpu.make_async_copy(shard_hbm, shard, local.at[0]),
        pltpu.make_async_copy(targets_hbm, targets, local.at[1]),
    ]
    fetch = [
        pltpu.make_async_copy(weight_hbm.at[:, :, 0:FA], w_a, local.at[2]),
        pltpu.make_async_copy(weight_hbm.at[:, :, FA:FA + FB], w_b, local.at[3]),
    ] + [
        pltpu.make_async_copy(weight_hbm.at[:, i, FA + FB:FEATS], w_c.at[i], local.at[4 + i]) for i in range(NZ)
    ]
    for copy in fetch_small + fetch:
        copy.start()

    for copy in fetch_small:
        copy.wait()
    pad32[...] = jnp.zeros_like(pad32)
    pad32[0, 0:ROWS, 0:FA + FB] = shard[:, 0:FA + FB].astype(F32)
    pad32[1, 0:ROWS, 0:FC] = shard[:, FA + FB:FEATS].astype(F32)
    mine_ab, mine_c = pad32[0].astype(BF16), pad32[1].astype(BF16)
    own_ab[...] = mine_ab
    own_c[...] = mine_c

    row = lax.broadcasted_iota(jnp.int32, (HALF, TOKENS), 0)
    section = (row // PAD) % NX * 4 + row // (PAD * NX) * 2 + c
    match = (section * ROWS + row % PAD == lax.broadcasted_iota(jnp.int32, (HALF, TOKENS), 1)) & (row % PAD < ROWS)
    goal = jnp.sum(jnp.where(match, targets[...].astype(F32), 0.0), axis=1, keepdims=True).astype(jnp.int32)
    entry = lax.broadcasted_iota(jnp.int32, (HALF, VOCAB_CHIP), 1)
    mine = (s * (YL * NZ) + t) * VOCAB_DEV
    mate = ((s + 1 - 2 * c) * (YL * NZ) + t) * VOCAB_DEV
    hit = jnp.where(entry < VOCAB_DEV, entry + mine, entry + (mate - VOCAB_DEV)) == goal

    def dot(a, b, dims):
        return lax.dot_general(a, b, (dims, ((), ())), preferred_element_type=F32)

    nn, tn = ((1,), (0,)), ((0,), (0,))
    halves = (YH, NX, PAD)
    turn = [(yl + k) % YL for k in range(YL)]

    pl.semaphore_wait(barrier, len(peers))

    z_copies = [go(own_ab, z_rec.at[z], z_peer(d)) for d in ORDER]
    y_copies = [go(own_c, y_rec.at[y], y_peer(d)) for d in ORDER]
    z_rec[z] = mine_ab
    y_rec[y] = mine_c

    for copy in fetch:
        copy.wait()
    w_core = [go(src, dst, partner) for src, dst in ((w_a, p_a), (w_b, p_b), (w_c, p_c))]

    def transpose(parts, at_row):
        rows = pl.ds(at_row, VOCAB_DEV)
        for part, into in zip(parts, (wt_a, wt_b, wt_c)):
            for j in range(into.shape[0]):
                into[j, rows] = part[j].reshape(into.shape[2], VOCAB_DEV).T

    transpose((w_a, w_b, w_c), 0)

    hot = hit.astype(F32).astype(BF16)

    def columns_at(first):
        rows = pl.ds(first, VOCAB_DEV)
        for into, weight in ((tk_a, wt_a), (tk_b, wt_b), (tk_c, wt_c)):
            for j in range(into.shape[0]):
                chunk = turn[j] if weight is wt_a else j
                column = dot(hot[:, first:first + VOCAB_DEV], weight[chunk, rows], nn).astype(BF16).reshape(into.shape[1:])
                into[j] = into[j] + column if first else column

    columns_at(0)
    for copy in z_copies:
        copy.wait_recv()
    for i in range(NZ):
        part = z_rec[i].astype(F32)
        line_a[:, FA * i:FA * (i + 1)] = part[:, 0:FA]
        line_b[:, FB * i:FB * (i + 1)] = part[:, FA:FA + FB]
    hid_a[yl, 0, yh, x] = line_a[...].astype(BF16)
    hid_b[yl, 0, yh, x] = line_b[...].astype(BF16)

    block = hid_a.at[yl, 0, yh, x]
    a_y = {d: go(block, block, y_peer(d)) for d in ORDER}
    block = hid_b.at[yl, 0, yh, x]
    b_x = [go(block, block, x_peer(d)) for d in XORDER]
    for copy in y_copies:
        copy.wait_recv()
    for i in range(NY):
        line_c[i // YL, :, FC * (i % YL):FC * (i % YL + 1)] = y_rec[i].astype(F32)[:, 0:FC]
    hid_c[z, 0, :, x] = line_c[...].astype(BF16)
    block = hid_c.at[z, 0, :, x]
    c_x = [go(block, block, x_peer(d)) for d in XORDER]

    a_x = []

    def pass_a(d):
        from_y = (y + NY - d) % NY
        block = hid_a.at[from_y % YL, 0, from_y // YL, x]
        a_x.extend([go(block, block, x_peer(dx)) for dx in XORDER])

    pass_a(0)
    for copy in b_x:
        copy.wait_recv()
    block = hid_b.at[yl, 0, yh]
    b_y = [go(block, block, y_peer(d)) for d in ORDER]
    for copy in c_x:
        copy.wait_recv()
    block = hid_c.at[z, 0]
    c_z = [go(block, block, z_peer(d)) for d in ORDER]
    for copy in w_core:
        copy.wait_recv()
    transpose((p_a, p_b, p_c), VOCAB_DEV)
    columns_at(VOCAB_DEV)
    for d in ORDER:
        a_y[d].wait_recv()
        pass_a(d)

    def wide_a(src, dst, k):
        return [go(src.at[k, :, (x + d) % NX], dst.at[d, k], x_peer(d)) for d in XORDER]

    def wide_b(src, dst):
        return [go(src.at[(y + d) % NY % YL, (y + d) % NY // YL], dst.at[d], y_peer(d)) for d in ORDER]

    def wide_c(src, dst):
        return [go(src.at[(z + d) % NZ], dst.at[d], z_peer(d)) for d in ORDER]

    ta_x = [wide_a(tk_a, tr_a, k) for k in range(YL)]

    def add_logits(sums, hid, parts):
        for j in range(hid.shape[0]):
            left = hid[j, 0].reshape(HALF, hid.shape[-1])
            sums = [so + dot(left, part[j].reshape(hid.shape[-1], VOCAB_DEV), nn) for so, part in zip(sums, parts)]
        return sums

    for copy in a_x:
        copy.wait_recv()
    sums = add_logits([jnp.zeros((HALF, VOCAB_DEV), F32)] * NC, hid_a, (w_a, p_a))
    for copy in b_y:
        copy.wait_recv()
    sums = add_logits(sums, hid_b, (w_b, p_b))
    for copy in c_z:
        copy.wait_recv()
    tb_y = wide_b(tk_b, tr_b)
    tc_z = wide_c(tk_c, tr_c)
    sums = add_logits(sums, hid_c, (w_c, p_c))
    logits = jnp.concatenate(sums, axis=1)

    top = jnp.max(logits, axis=1, keepdims=True)
    shifted = jnp.exp(logits - top)
    rest = jnp.sum(jnp.where(hit, 0.0, shifted), axis=1, keepdims=True)
    aim = jnp.sum(jnp.where(hit, shifted, 0.0), axis=1, keepdims=True)
    picked = jnp.sum(jnp.where(hit, logits, 0.0), axis=1, keepdims=True)
    others = jnp.where(hit, 0.0, shifted).astype(BF16)

    lane = lax.broadcasted_iota(jnp.int32, (HALF, 128), 1)
    columns = jnp.where(lane == 0, top, jnp.where(lane == 1, rest, jnp.where(lane == 2, picked, jnp.where(
        lane == 3, aim, 0.0))))
    tall = columns.T[0:8, :]
    stat[0] = tall

    def merge(parts):
        best = functools.reduce(jnp.maximum, [p[0:1, :] for p in parts])
        scale = [jnp.exp(p[0:1, :] - best) for p in parts]
        rest_ = sum(p[1:2, :] * f for p, f in zip(parts, scale))
        pick_ = sum(p[2:3, :] for p in parts)
        aim_ = sum(p[3:4, :] * f for p, f in zip(parts, scale))
        return jnp.concatenate([best, rest_, pick_, aim_, jnp.zeros((4, HALF), F32)], axis=0)

    def columns_of(rows):
        full = jnp.concatenate(rows + [jnp.zeros((128 - len(rows), HALF), F32)], axis=0)
        return full.T

    to_x = [go(stat.at[0], st_x.at[i], x_peer(d)) for i, d in enumerate(XORDER)]
    to_y = [go(stat.at[0], st_m.at[i], y_peer(d)) for i, d in enumerate(ORDER)]
    to_z = [go(stat.at[0], st_n.at[i], z_peer(d)) for i, d in enumerate(ORDER)]

    def term(weight, keep, send):
        terms = dot(others, weight, nn).reshape(keep.shape)
        keep[...] = terms
        send[...] = terms.astype(BF16)

    a_x = []
    for k in range(YL):
        term(wt_a[turn[k]], keep_a.at[k], s1_a.at[k])
        a_x.append(wide_a(s1_a, r1_a, k))
    for j in range(YL):
        term(wt_b[j], keep_b.at[j], s1_b.at[j])
    b_y = wide_b(s1_b, r1_b)
    for j in range(NZ):
        term(wt_c[j], keep_c.at[j], s1_c.at[j])
    c_z = wide_c(s1_c, r1_c)
    for copy in to_x:
        copy.wait_recv()
    line = merge([tall] + [st_x[i] for i in range(len(XORDER))])
    stat[1] = line
    y_turn = [(e, k, at(x, (yh + e) % YH * YL + turn[k], z, c)) for e in range(YH) for k in range(YL) if e or k]
    along_y = [go(stat.at[1], st_y.at[e * YL + k], peer) for e, k, peer in y_turn]
    h_core = [go(hid.at[:, 0], hid.at[:, 1], partner) for hid in (hid_a, hid_b, hid_c)]

    def second_a(src, dst, k):
        return [go(src.at[k, (yh + e) % YH], dst.at[e * YL + k], peer) for e, k_, peer in y_turn if k_ == k]

    def second_b(src, dst):
        return [go(src.at[(x + d) % NX], dst.at[d], x_peer(d)) for d in XORDER]

    def second_c(src, dst):
        return [go(src.at[:, (x + d) % NX], dst.at[d], x_peer(d)) for d in XORDER]

    ta_y = []
    for k in range(YL):
        for copy in ta_x[k]:
            copy.wait_recv()
        t2_a[k] = tk_a[k, :, x] + sum(tr_a[d, k] for d in XORDER)
        ta_y += second_a(t2_a, t3_a, k)
    for copy in tb_y:
        copy.wait_recv()
    t2_b[...] = tk_b[yl, yh] + sum(tr_b[d] for d in ORDER)
    tb_x = second_b(t2_b, t3_b)
    for copy in tc_z:
        copy.wait_recv()
    t2_c[...] = tk_c[z] + sum(tr_c[d] for d in ORDER)
    tc_x = second_c(t2_c, t3_c)

    for copy in to_y + to_z:
        copy.wait_recv()
    near_y, near_z = ([tall] + [st[i] for i in range(len(ORDER))] for st in (st_m, st_n))
    line_y, line_z = merge(near_y), merge(near_z)
    stat[2] = line_y
    stat[3] = line_z
    tiles_x = [go(stat.at[2], st_b.at[i], x_peer(d)) for i, d in enumerate(XORDER)]
    tiles_x += [go(stat.at[3], st_c.at[i], x_peer(d)) for i, d in enumerate(XORDER)]

    def ratios(parts, best):
        return [jnp.exp(p[0:1, :] - best[0:1, :]) for p in parts]

    near_x = [tall] + [st_x[i] for i in range(len(XORDER))]
    scales = ratios(near_x, line) + ratios(near_y, line_y) + ratios(near_z, line_z)
    coef[...] = columns_of(scales).reshape(halves + (128,))

    def scaled(own, others_, f, first):
        parts = [own] + [other.astype(F32) for other in others_]
        return sum(p * f[..., first + i:first + i + 1] for i, p in enumerate(parts))

    a_y = []
    f_x = coef[:, x]
    for k in range(YL):
        for copy in a_x[k]:
            copy.wait_recv()
        chunk = scaled(keep_a[k, :, x], [r1_a[d, k] for d in XORDER], f_x, 0)
        s2_a[k] = chunk.astype(BF16)
        if k == 0:
            keep_a[0, :, 0] = chunk
        a_y += second_a(s2_a, r2_a, k)
    for copy in along_y:
        copy.wait_recv()
    lines = [line] + [st_y[n] for n in range(1, NY)]
    plane = merge(lines)
    stat[4] = plane
    along_z = [go(stat.at[4], st_z.at[i], z_peer(d)) for i, d in enumerate(ORDER)]
    for copy in b_y:
        copy.wait_recv()
    sum_b = scaled(keep_b[yl, yh], [r1_b[d] for d in ORDER], coef[yh], NX)
    s2_b[...] = sum_b.astype(BF16)
    keep_b[0, 0] = sum_b
    b_x = second_b(s2_b, r2_b)
    for copy in c_z:
        copy.wait_recv()
    sum_c = scaled(keep_c[z], [r1_c[d] for d in ORDER], coef[...], NX + NY)
    s2_c[...] = sum_c.astype(BF16)
    keep_c[0] = sum_c
    c_x = second_c(s2_c, r2_c)

    for copy in tiles_x + along_z:
        copy.wait_recv()
    whole = merge([plane] + [st_z[i] for i in range(len(ORDER))])
    highest, total = whole[0:1, :], whole[1:2, :] + whole[3:4, :]
    slot = lax.broadcasted_iota(jnp.int32, (1, HALF), 1)
    each = jnp.where(slot % PAD < ROWS, highest + jnp.log(total) - whole[2:3, :], 0.0)
    miss = (whole[1:2, :] / total).astype(BF16).astype(F32)
    lines_y = [line_y] + [st_b[i] for i in range(len(XORDER))]
    lines_z = [line_z] + [st_c[i] for i in range(len(XORDER))]
    factors = columns_of([f / total for f in ratios(lines + lines_y + lines_z + [tall], whole)] + [miss])
    coef[...] = factors.reshape(halves + (128,))
    probs = (shifted * factors[:, OWN:OWN + 1]).astype(BF16)
    p_out[...] = probs[:, VOCAB_DEV:VOCAB_CHIP]
    l_out[...] = jnp.concatenate([each, jnp.zeros((7, HALF), F32)], axis=0)
    swap = h_core + [go(p_out, p_in, partner), go(l_out, l_in, partner)]

    for copy in c_x + tc_x:
        copy.wait_recv()
    f_c, f_ab = coef[:, x], coef[yh, x]
    part_c = scaled(keep_c[0, :, x], [r2_c[d] for d in XORDER], f_c, NY + NX)
    column = t2_c[:, x] + sum(t3_c[d] for d in XORDER)
    part_c = part_c - column.astype(F32) * f_c[..., MISS:MISS + 1]
    for i in range(NY):
        s3_c[i, :, 0:FC] = part_c[i // YL, :, FC * (i % YL):FC * (i % YL + 1)]
    c_y = [go(s3_c.at[(y + d) % NY], r3_c.at[d], y_peer(d)) for d in ORDER]
    for copy in b_x + tb_x:
        copy.wait_recv()
    part_b = scaled(keep_b[0, 0, x], [r2_b[d] for d in XORDER], f_ab, NY)
    column = t2_b[x] + sum(t3_b[d] for d in XORDER)
    part_b = part_b - column.astype(F32) * f_ab[..., MISS:MISS + 1]
    for copy in a_y + ta_y:
        copy.wait_recv()
    part_a = scaled(keep_a[0, yh, 0], [r2_a[n] for n in range(1, NY)], f_ab, 0)
    column = t2_a[0, yh] + sum(t3_a[n] for n in range(1, NY))
    part_a = part_a - column.astype(F32) * f_ab[..., MISS:MISS + 1]
    for i in range(NZ):
        s3_ab[i, :, 0:FA] = part_a[:, FA * i:FA * (i + 1)]
        s3_ab[i, :, FA:FA + FB] = part_b[:, FB * i:FB * (i + 1)]
    ab_z = [go(s3_ab.at[(z + d) % NZ], r3_ab.at[d], z_peer(d)) for d in ORDER]

    for copy in swap:
        copy.wait_recv()
    loss[0, 0] = (jnp.sum(each) + jnp.sum(l_in[0:1, :])) / TOKENS
    probs = jnp.concatenate([probs[:, 0:VOCAB_DEV], p_in[...]], axis=0)
    for hid, grad in ((hid_a, g_a), (hid_b, g_b), (hid_c, g_c)):
        for j in range(hid.shape[0]):
            left = hid[j].reshape(TALL, hid.shape[-1])
            grad[j] = dot(left, probs, tn).astype(BF16).reshape(grad.shape[1:])
    writes = [
        pltpu.make_async_copy(g_a, head_grad.at[:, :, 0:FA], gsem.at[0]),
        pltpu.make_async_copy(g_b, head_grad.at[:, :, FA:FA + FB], gsem.at[1]),
    ] + [
        pltpu.make_async_copy(g_c.at[i], head_grad.at[:, i, FA + FB:FEATS], gsem.at[2 + i]) for i in range(NZ)
    ]
    for write in writes:
        write.start()

    for copy in c_y:
        copy.wait_recv()
    done_c = s3_c[y][:, 0:FC] + sum(r3_c[d][:, 0:FC] for d in ORDER)
    hidden_grad[:, FA + FB:FEATS] = done_c[0:ROWS].astype(BF16)
    for copy in ab_z:
        copy.wait_recv()
    done_ab = s3_ab[z][:, 0:FA + FB] + sum(r3_ab[d][:, 0:FA + FB] for d in ORDER)
    hidden_grad[:, 0:FA + FB] = done_ab[0:ROWS].astype(BF16)

    for copy in sent:
        copy.wait_send()
    for write in writes:
        write.wait()


def per_device(hidden, head_weight, targets):
    vmem = pl.BlockSpec(memory_space=pltpu.VMEM)
    hbm = pl.BlockSpec(memory_space=pltpu.HBM)
    v = pltpu.VMEM
    dma = pltpu.SemaphoreType.DMA
    halves = (YH, NX, PAD)
    loss, head_grad, hidden_grad = pl.pallas_call(
        kernel,
        out_shape=(
            jax.ShapeDtypeStruct((1, 1), F32),
            jax.ShapeDtypeStruct((YL, NZ, FEATS, VOCAB_DEV), BF16),
            jax.ShapeDtypeStruct((ROWS, FEATS), BF16),
        ),
        in_specs=[hbm, hbm, hbm],
        out_specs=(pl.BlockSpec(memory_space=pltpu.SMEM), pl.BlockSpec(memory_space=pl.ANY), vmem),
        scratch_shapes=[
            v((ROWS, FEATS), BF16), v((1, TOKENS), jnp.int32),
            v((YL, NZ, FA, VOCAB_DEV), BF16), v((YL, NZ, FB, VOCAB_DEV), BF16), v((NZ, YL, FC, VOCAB_DEV), BF16),
            v((YL, NZ, FA, VOCAB_DEV), BF16), v((YL, NZ, FB, VOCAB_DEV), BF16), v((NZ, YL, FC, VOCAB_DEV), BF16),
            v((YL, VOCAB_CHIP, WA), BF16), v((YL, VOCAB_CHIP, WB), BF16), v((NZ, VOCAB_CHIP, WC), BF16),
            v((YL, NC) + halves + (WA,), BF16), v((YL, NC) + halves + (WB,), BF16), v((NZ, NC) + halves + (WC,), BF16),
            v((2, PAD, 128), F32), v((PAD, 128), BF16), v((PAD, 128), BF16),
            v((NZ, PAD, 128), BF16), v((NY, PAD, 128), BF16),
            v((PAD, WA), F32), v((PAD, WB), F32), v((YH, PAD, WC), F32),
            v((5, 8, HALF), F32), v((3, 8, HALF), F32), v((7, 8, HALF), F32), v((7, 8, HALF), F32),
            v((3, 8, HALF), F32), v((3, 8, HALF), F32), v((NY, 8, HALF), F32), v((7, 8, HALF), F32),
            v(halves + (128,), F32),
            v((YL,) + halves + (WA,), F32), v((YL,) + halves + (WB,), F32), v((NZ,) + halves + (WC,), F32),
            v((YL,) + halves + (WA,), BF16), v((YL,) + halves + (WB,), BF16), v((NZ,) + halves + (WC,), BF16),
            v((NX, YL, YH, PAD, WA), BF16), v((NY, NX, PAD, WB), BF16), v((NZ,) + halves + (WC,), BF16),
            v((YL,) + halves + (WA,), BF16), v((YL,) + halves + (WB,), BF16), v((NZ,) + halves + (WC,), BF16),
            v((NX, YL, YH, PAD, WA), BF16), v((NY, NX, PAD, WB), BF16), v((NZ,) + halves + (WC,), BF16),
            v((YL, YH, PAD, WA), BF16), v((NX, PAD, WB), BF16), v(halves + (WC,), BF16),
            v((NY, PAD, WA), BF16), v((NX, PAD, WB), BF16), v((NX, YH, PAD, WC), BF16),
            v((YL, YH, PAD, WA), BF16), v((NX, PAD, WB), BF16), v(halves + (WC,), BF16),
            v((NY, PAD, WA), BF16), v((NX, PAD, WB), BF16), v((NX, YH, PAD, WC), BF16),
            v((NZ, PAD, 128), F32), v((NY, PAD, 128), F32), v((NZ, PAD, 128), F32), v((NY, PAD, 128), F32),
            v((YL, NZ, FA, VOCAB_DEV), BF16), v((YL, NZ, FB, VOCAB_DEV), BF16), v((NZ, YL, FC, VOCAB_DEV), BF16),
            v((HALF, VOCAB_DEV), BF16), v((HALF, VOCAB_DEV), BF16), v((8, HALF), F32), v((8, HALF), F32),
            dma((12,)), dma((10,)), dma((208,)), dma((208,)),
        ],
        compiler_params=pltpu.CompilerParams(
            collective_id=0, has_side_effects=True, vmem_limit_bytes=44 * 2**20),
        name="output_layer",
    )(*[pltpu.with_memory_space_constraint(operand, pltpu.HBM) for operand in (
        hidden, head_weight.reshape(YL, NZ, FEATS, VOCAB_DEV), targets.reshape(1, TOKENS))])
    return loss.reshape(()), head_grad.reshape(D, VOCAB_DEV), hidden_grad


def solution(mesh):
    placed = (P("section", "tp"), P(None, ("section", "tp")), P())
    return jax.shard_map(
        per_device,
        mesh=mesh,
        in_specs=placed,
        out_specs=(P(), P(None, ("section", "tp")), P("section", "tp")),
        check_vma=False,
    )
```

```python
import functools

import jax
import jax.numpy as jnp
from jax import lax
from jax.experimental import pallas as pl
from jax.experimental.pallas import tpu as pltpu
from jax.sharding import PartitionSpec as P

MESH = pl.DeviceIdType.MESH
F32 = jnp.float32
BF16 = jnp.bfloat16
NX, NY, NZ, NC = 4, 8, 8, 2
YH, YL = 2, 4
ROWS = 13
PAD = 16
FEATS = 144
FA, FB, FC = 80, 32, 32
WA, WB, WC = NZ * FA, NZ * FB, YL * FC
HALF = YH * NX * PAD
TALL = NC * HALF
D = YL * NZ * FEATS
VOCAB_DEV = 256
VOCAB_CHIP = NC * VOCAB_DEV
TOKENS = 208
ORDER = (1, 7, 2, 6, 3, 5, 4)
XORDER = (1, 3, 2)
OWN = NY + NX + NX
MISS = OWN + 1


def kernel(shard_hbm, weight_hbm, targets_hbm, loss, head_grad, hidden_grad,
           shard, targets, w_a, w_b, w_c, p_a, p_b, p_c, wt_a, wt_b, wt_c, hid_a, hid_b, hid_c, pad32,
           own_ab, own_c, z_rec, y_rec, line_a, line_b, line_c, stat, st_x, st_m, st_n, st_b, st_c, st_y,
           st_z, coef, keep_a, keep_b, keep_c, s1_a, s1_b, s1_c, r1_a, r1_b, r1_c, tk_a, tk_b, tk_c, to_a,
           to_b, to_c, ti_a, ti_b, ti_c, tr_a, tr_b, tr_c, t2_a, t2_b, t2_c, t3_a, t3_b, t3_c, s2_a, s2_b,
           s2_c, r2_a, r2_b, r2_c, s3_ab, s3_c, r3_ab, r3_c, g_a, g_b, g_c, p_out, p_in, l_out, l_in, local,
           gsem, ssem, rsem):
    s = lax.axis_index("section")
    t = lax.axis_index("tp")
    x, yh, c = s // 4, (s // 2) % 2, s % 2
    yl, z = t // NZ, t % NZ
    y = yh * YL + yl

    def at(x_, y_, z_, c_):
        return {"section": x_ * 4 + (y_ // YL) * 2 + c_, "tp": (y_ % YL) * NZ + z_}

    def z_peer(d):
        return at(x, y, (z + d) % NZ, c)

    def y_peer(d):
        return at(x, (y + d) % NY, z, c)

    def x_peer(d):
        return at((x + d) % NX, y, z, c)

    sent = []

    def go(src, dst, peer):
        n = len(sent)
        copy = pltpu.make_async_remote_copy(
            src_ref=src, dst_ref=dst, send_sem=ssem.at[n], recv_sem=rsem.at[n], device_id=peer, device_id_type=MESH)
        copy.start()
        sent.append(copy)
        return copy

    peers = [z_peer(d) for d in ORDER] + [y_peer(d) for d in ORDER] + [x_peer(d) for d in XORDER]
    partner = at(x, y, z, 1 - c)
    peers.append(partner)
    barrier = pltpu.get_barrier_semaphore()
    for peer in peers:
        pl.semaphore_signal(barrier, inc=1, device_id=peer, device_id_type=MESH)

    fetch_small = [
        pltpu.make_async_copy(shard_hbm, shard, local.at[0]),
        pltpu.make_async_copy(targets_hbm, targets, local.at[1]),
    ]
    fetch = [
        pltpu.make_async_copy(weight_hbm.at[:, :, 0:FA], w_a, local.at[2]),
        pltpu.make_async_copy(weight_hbm.at[:, :, FA:FA + FB], w_b, local.at[3]),
    ] + [
        pltpu.make_async_copy(weight_hbm.at[:, i, FA + FB:FEATS], w_c.at[i], local.at[4 + i]) for i in range(NZ)
    ]
    for copy in fetch_small + fetch:
        copy.start()

    for copy in fetch_small:
        copy.wait()
    pad32[...] = jnp.zeros_like(pad32)
    pad32[0, 0:ROWS, 0:FA + FB] = shard[:, 0:FA + FB].astype(F32)
    pad32[1, 0:ROWS, 0:FC] = shard[:, FA + FB:FEATS].astype(F32)
    mine_ab, mine_c = pad32[0].astype(BF16), pad32[1].astype(BF16)
    own_ab[...] = mine_ab
    own_c[...] = mine_c

    row = lax.broadcasted_iota(jnp.int32, (TALL, TOKENS), 0)
    section = (row // PAD) % NX * 4 + (row // (PAD * NX)) % YH * 2 + (row // HALF + c) % 2
    match = (section * ROWS + row % PAD == lax.broadcasted_iota(jnp.int32, (TALL, TOKENS), 1)) & (row % PAD < ROWS)
    goal = jnp.sum(jnp.where(match, targets[...].astype(F32), 0.0), axis=1, keepdims=True).astype(jnp.int32)
    mine = (s * (YL * NZ) + t) * VOCAB_DEV
    mate = ((s + 1 - 2 * c) * (YL * NZ) + t) * VOCAB_DEV
    hot = lax.broadcasted_iota(jnp.int32, (TALL, VOCAB_DEV), 1) + mine == goal
    entry = lax.broadcasted_iota(jnp.int32, (HALF, VOCAB_CHIP), 1)
    hit = jnp.where(entry < VOCAB_DEV, entry + mine, entry + (mate - VOCAB_DEV)) == goal[0:HALF]

    def dot(a, b, dims):
        return lax.dot_general(a, b, (dims, ((), ())), preferred_element_type=F32)

    nn, tn = ((1,), (0,)), ((0,), (0,))
    halves = (YH, NX, PAD)
    turn = [(yl + k) % YL for k in range(YL)]

    pl.semaphore_wait(barrier, len(peers))

    z_copies = [go(own_ab, z_rec.at[z], z_peer(d)) for d in ORDER]
    y_copies = [go(own_c, y_rec.at[y], y_peer(d)) for d in ORDER]
    z_rec[z] = mine_ab
    y_rec[y] = mine_c

    for copy in fetch:
        copy.wait()
    def transpose(parts, at_row):
        rows = pl.ds(at_row, VOCAB_DEV)
        for part, into in zip(parts, (wt_a, wt_b, wt_c)):
            for j in range(into.shape[0]):
                into[j, rows] = part[j].reshape(into.shape[2], VOCAB_DEV).T

    transpose((w_a, w_b, w_c), 0)

    hot = hot.astype(F32).astype(BF16)
    t_core = []
    for keep, out, into, weight in ((tk_c, to_c, ti_c, wt_c), (tk_a, to_a, ti_a, wt_a), (tk_b, to_b, ti_b, wt_b)):
        for j in range(keep.shape[0]):
            chunk = turn[j] if weight is wt_a else j
            column = dot(hot, weight[chunk, 0:VOCAB_DEV], nn).astype(BF16)
            keep[j] = column[0:HALF].reshape(keep.shape[1:])
            out[j] = column[HALF:TALL].reshape(keep.shape[1:])
        t_core.append(go(out, into, partner))
    w_core = [go(src, dst, partner) for src, dst in ((w_a, p_a), (w_b, p_b), (w_c, p_c))]

    def both_columns(copy, keep, into):
        copy.wait_recv()
        for j in range(keep.shape[0]):
            keep[j] = keep[j] + into[j]

    for copy in z_copies:
        copy.wait_recv()
    for i in range(NZ):
        part = z_rec[i].astype(F32)
        line_a[:, FA * i:FA * (i + 1)] = part[:, 0:FA]
        line_b[:, FB * i:FB * (i + 1)] = part[:, FA:FA + FB]
    hid_a[yl, 0, yh, x] = line_a[...].astype(BF16)
    hid_b[yl, 0, yh, x] = line_b[...].astype(BF16)

    block = hid_a.at[yl, 0, yh, x]
    a_y = {d: go(block, block, y_peer(d)) for d in ORDER}
    block = hid_b.at[yl, 0, yh, x]
    b_x = [go(block, block, x_peer(d)) for d in XORDER]
    for copy in y_copies:
        copy.wait_recv()
    for i in range(NY):
        line_c[i // YL, :, FC * (i % YL):FC * (i % YL + 1)] = y_rec[i].astype(F32)[:, 0:FC]
    hid_c[z, 0, :, x] = line_c[...].astype(BF16)
    block = hid_c.at[z, 0, :, x]
    c_x = [go(block, block, x_peer(d)) for d in XORDER]

    a_x = []

    def pass_a(d):
        from_y = (y + NY - d) % NY
        block = hid_a.at[from_y % YL, 0, from_y // YL, x]
        a_x.extend([go(block, block, x_peer(dx)) for dx in XORDER])

    pass_a(0)

    def wide_a(src, dst, k):
        return [go(src.at[k, :, (x + d) % NX], dst.at[d, k], x_peer(d)) for d in XORDER]

    def wide_b(src, dst):
        return [go(src.at[(y + d) % NY % YL, (y + d) % NY // YL], dst.at[d], y_peer(d)) for d in ORDER]

    def wide_c(src, dst):
        return [go(src.at[(z + d) % NZ], dst.at[d], z_peer(d)) for d in ORDER]

    both_columns(t_core[0], tk_c, ti_c)
    tc_z = wide_c(tk_c, tr_c)
    both_columns(t_core[1], tk_a, ti_a)
    ta_x = [wide_a(tk_a, tr_a, k) for k in range(YL)]

    for copy in b_x:
        copy.wait_recv()
    block = hid_b.at[yl, 0, yh]
    b_y = [go(block, block, y_peer(d)) for d in ORDER]
    for copy in c_x:
        copy.wait_recv()
    block = hid_c.at[z, 0]
    c_z = [go(block, block, z_peer(d)) for d in ORDER]
    both_columns(t_core[2], tk_b, ti_b)
    tb_y = wide_b(tk_b, tr_b)
    for d in ORDER:
        a_y[d].wait_recv()
        pass_a(d)

    for copy in w_core:
        copy.wait_recv()
    transpose((p_a, p_b, p_c), VOCAB_DEV)

    def add_logits(sums, hid, parts):
        for j in range(hid.shape[0]):
            left = hid[j, 0].reshape(HALF, hid.shape[-1])
            sums = [so + dot(left, part[j].reshape(hid.shape[-1], VOCAB_DEV), nn) for so, part in zip(sums, parts)]
        return sums

    for copy in a_x:
        copy.wait_recv()
    sums = add_logits([jnp.zeros((HALF, VOCAB_DEV), F32)] * NC, hid_a, (w_a, p_a))
    for copy in b_y:
        copy.wait_recv()
    sums = add_logits(sums, hid_b, (w_b, p_b))
    for copy in c_z:
        copy.wait_recv()
    sums = add_logits(sums, hid_c, (w_c, p_c))
    logits = jnp.concatenate(sums, axis=1)

    top = jnp.max(logits, axis=1, keepdims=True)
    shifted = jnp.exp(logits - top)
    rest = jnp.sum(jnp.where(hit, 0.0, shifted), axis=1, keepdims=True)
    aim = jnp.sum(jnp.where(hit, shifted, 0.0), axis=1, keepdims=True)
    picked = jnp.sum(jnp.where(hit, logits, 0.0), axis=1, keepdims=True)
    others = jnp.where(hit, 0.0, shifted).astype(BF16)

    lane = lax.broadcasted_iota(jnp.int32, (HALF, 128), 1)
    columns = jnp.where(lane == 0, top, jnp.where(lane == 1, rest, jnp.where(lane == 2, picked, jnp.where(
        lane == 3, aim, 0.0))))
    tall = columns.T[0:8, :]
    stat[0] = tall

    def merge(parts):
        best = functools.reduce(jnp.maximum, [p[0:1, :] for p in parts])
        scale = [jnp.exp(p[0:1, :] - best) for p in parts]
        rest_ = sum(p[1:2, :] * f for p, f in zip(parts, scale))
        pick_ = sum(p[2:3, :] for p in parts)
        aim_ = sum(p[3:4, :] * f for p, f in zip(parts, scale))
        return jnp.concatenate([best, rest_, pick_, aim_, jnp.zeros((4, HALF), F32)], axis=0)

    def columns_of(rows):
        full = jnp.concatenate(rows + [jnp.zeros((128 - len(rows), HALF), F32)], axis=0)
        return full.T

    to_x = [go(stat.at[0], st_x.at[i], x_peer(d)) for i, d in enumerate(XORDER)]
    to_y = [go(stat.at[0], st_m.at[i], y_peer(d)) for i, d in enumerate(ORDER)]
    to_z = [go(stat.at[0], st_n.at[i], z_peer(d)) for i, d in enumerate(ORDER)]

    def term(weight, keep, send):
        terms = dot(others, weight, nn).reshape(keep.shape)
        keep[...] = terms
        send[...] = terms.astype(BF16)

    a_x = []
    for k in range(YL):
        term(wt_a[turn[k]], keep_a.at[k], s1_a.at[k])
        a_x.append(wide_a(s1_a, r1_a, k))
    for j in range(YL):
        term(wt_b[j], keep_b.at[j], s1_b.at[j])
    b_y = wide_b(s1_b, r1_b)
    for j in range(NZ):
        term(wt_c[j], keep_c.at[j], s1_c.at[j])
    c_z = wide_c(s1_c, r1_c)
    for copy in to_x:
        copy.wait_recv()
    line = merge([tall] + [st_x[i] for i in range(len(XORDER))])
    stat[1] = line
    y_turn = [(e, k, at(x, (yh + e) % YH * YL + turn[k], z, c)) for e in range(YH) for k in range(YL) if e or k]
    along_y = [go(stat.at[1], st_y.at[e * YL + k], peer) for e, k, peer in y_turn]
    h_core = [go(hid.at[:, 0], hid.at[:, 1], partner) for hid in (hid_a, hid_b, hid_c)]

    def second_a(src, dst, k):
        return [go(src.at[k, (yh + e) % YH], dst.at[e * YL + k], peer) for e, k_, peer in y_turn if k_ == k]

    def second_b(src, dst):
        return [go(src.at[(x + d) % NX], dst.at[d], x_peer(d)) for d in XORDER]

    def second_c(src, dst):
        return [go(src.at[:, (x + d) % NX], dst.at[d], x_peer(d)) for d in XORDER]

    ta_y = []
    for k in range(YL):
        for copy in ta_x[k]:
            copy.wait_recv()
        t2_a[k] = tk_a[k, :, x] + sum(tr_a[d, k] for d in XORDER)
        ta_y += second_a(t2_a, t3_a, k)
    for copy in tb_y:
        copy.wait_recv()
    t2_b[...] = tk_b[yl, yh] + sum(tr_b[d] for d in ORDER)
    tb_x = second_b(t2_b, t3_b)
    for copy in tc_z:
        copy.wait_recv()
    t2_c[...] = tk_c[z] + sum(tr_c[d] for d in ORDER)
    tc_x = second_c(t2_c, t3_c)

    for copy in to_y + to_z:
        copy.wait_recv()
    near_y, near_z = ([tall] + [st[i] for i in range(len(ORDER))] for st in (st_m, st_n))
    line_y, line_z = merge(near_y), merge(near_z)
    stat[2] = line_y
    stat[3] = line_z
    tiles_x = [go(stat.at[2], st_b.at[i], x_peer(d)) for i, d in enumerate(XORDER)]
    tiles_x += [go(stat.at[3], st_c.at[i], x_peer(d)) for i, d in enumerate(XORDER)]

    def ratios(parts, best):
        return [jnp.exp(p[0:1, :] - best[0:1, :]) for p in parts]

    near_x = [tall] + [st_x[i] for i in range(len(XORDER))]
    scales = ratios(near_x, line) + ratios(near_y, line_y) + ratios(near_z, line_z)
    coef[...] = columns_of(scales).reshape(halves + (128,))

    def scaled(own, others_, f, first):
        parts = [own] + [other.astype(F32) for other in others_]
        return sum(p * f[..., first + i:first + i + 1] for i, p in enumerate(parts))

    a_y = []
    f_x = coef[:, x]
    for k in range(YL):
        for copy in a_x[k]:
            copy.wait_recv()
        chunk = scaled(keep_a[k, :, x], [r1_a[d, k] for d in XORDER], f_x, 0)
        s2_a[k] = chunk.astype(BF16)
        if k == 0:
            keep_a[0, :, 0] = chunk
        a_y += second_a(s2_a, r2_a, k)
    for copy in along_y:
        copy.wait_recv()
    lines = [line] + [st_y[n] for n in range(1, NY)]
    plane = merge(lines)
    stat[4] = plane
    along_z = [go(stat.at[4], st_z.at[i], z_peer(d)) for i, d in enumerate(ORDER)]
    for copy in b_y:
        copy.wait_recv()
    sum_b = scaled(keep_b[yl, yh], [r1_b[d] for d in ORDER], coef[yh], NX)
    s2_b[...] = sum_b.astype(BF16)
    keep_b[0, 0] = sum_b
    b_x = second_b(s2_b, r2_b)
    for copy in c_z:
        copy.wait_recv()
    sum_c = scaled(keep_c[z], [r1_c[d] for d in ORDER], coef[...], NX + NY)
    s2_c[...] = sum_c.astype(BF16)
    keep_c[0] = sum_c
    c_x = second_c(s2_c, r2_c)

    for copy in tiles_x + along_z:
        copy.wait_recv()
    whole = merge([plane] + [st_z[i] for i in range(len(ORDER))])
    highest, total = whole[0:1, :], whole[1:2, :] + whole[3:4, :]
    slot = lax.broadcasted_iota(jnp.int32, (1, HALF), 1)
    each = jnp.where(slot % PAD < ROWS, highest + jnp.log(total) - whole[2:3, :], 0.0)
    miss = (whole[1:2, :] / total).astype(BF16).astype(F32)
    lines_y = [line_y] + [st_b[i] for i in range(len(XORDER))]
    lines_z = [line_z] + [st_c[i] for i in range(len(XORDER))]
    factors = columns_of([f / total for f in ratios(lines + lines_y + lines_z + [tall], whole)] + [miss])
    coef[...] = factors.reshape(halves + (128,))
    probs = (shifted * factors[:, OWN:OWN + 1]).astype(BF16)
    p_out[...] = probs[:, VOCAB_DEV:VOCAB_CHIP]
    l_out[...] = jnp.concatenate([each, jnp.zeros((7, HALF), F32)], axis=0)
    swap = h_core + [go(p_out, p_in, partner), go(l_out, l_in, partner)]

    for copy in c_x + tc_x:
        copy.wait_recv()
    f_c, f_ab = coef[:, x], coef[yh, x]
    part_c = scaled(keep_c[0, :, x], [r2_c[d] for d in XORDER], f_c, NY + NX)
    column = t2_c[:, x] + sum(t3_c[d] for d in XORDER)
    part_c = part_c - column.astype(F32) * f_c[..., MISS:MISS + 1]
    for i in range(NY):
        s3_c[i, :, 0:FC] = part_c[i // YL, :, FC * (i % YL):FC * (i % YL + 1)]
    c_y = [go(s3_c.at[(y + d) % NY], r3_c.at[d], y_peer(d)) for d in ORDER]
    for copy in b_x + tb_x:
        copy.wait_recv()
    part_b = scaled(keep_b[0, 0, x], [r2_b[d] for d in XORDER], f_ab, NY)
    column = t2_b[x] + sum(t3_b[d] for d in XORDER)
    part_b = part_b - column.astype(F32) * f_ab[..., MISS:MISS + 1]
    for copy in a_y + ta_y:
        copy.wait_recv()
    part_a = scaled(keep_a[0, yh, 0], [r2_a[n] for n in range(1, NY)], f_ab, 0)
    column = t2_a[0, yh] + sum(t3_a[n] for n in range(1, NY))
    part_a = part_a - column.astype(F32) * f_ab[..., MISS:MISS + 1]
    for i in range(NZ):
        s3_ab[i, :, 0:FA] = part_a[:, FA * i:FA * (i + 1)]
        s3_ab[i, :, FA:FA + FB] = part_b[:, FB * i:FB * (i + 1)]
    ab_z = [go(s3_ab.at[(z + d) % NZ], r3_ab.at[d], z_peer(d)) for d in ORDER]

    for copy in swap:
        copy.wait_recv()
    loss[0, 0] = (jnp.sum(each) + jnp.sum(l_in[0:1, :])) / TOKENS
    probs = jnp.concatenate([probs[:, 0:VOCAB_DEV], p_in[...]], axis=0)
    for hid, grad in ((hid_a, g_a), (hid_b, g_b), (hid_c, g_c)):
        for j in range(hid.shape[0]):
            left = hid[j].reshape(TALL, hid.shape[-1])
            grad[j] = dot(left, probs, tn).astype(BF16).reshape(grad.shape[1:])
    writes = [
        pltpu.make_async_copy(g_a, head_grad.at[:, :, 0:FA], gsem.at[0]),
        pltpu.make_async_copy(g_b, head_grad.at[:, :, FA:FA + FB], gsem.at[1]),
    ] + [
        pltpu.make_async_copy(g_c.at[i], head_grad.at[:, i, FA + FB:FEATS], gsem.at[2 + i]) for i in range(NZ)
    ]
    for write in writes:
        write.start()

    for copy in c_y:
        copy.wait_recv()
    done_c = s3_c[y][:, 0:FC] + sum(r3_c[d][:, 0:FC] for d in ORDER)
    hidden_grad[:, FA + FB:FEATS] = done_c[0:ROWS].astype(BF16)
    for copy in ab_z:
        copy.wait_recv()
    done_ab = s3_ab[z][:, 0:FA + FB] + sum(r3_ab[d][:, 0:FA + FB] for d in ORDER)
    hidden_grad[:, 0:FA + FB] = done_ab[0:ROWS].astype(BF16)

    for copy in sent:
        copy.wait_send()
    for write in writes:
        write.wait()


def per_device(hidden, head_weight, targets):
    vmem = pl.BlockSpec(memory_space=pltpu.VMEM)
    hbm = pl.BlockSpec(memory_space=pltpu.HBM)
    v = pltpu.VMEM
    dma = pltpu.SemaphoreType.DMA
    halves = (YH, NX, PAD)
    loss, head_grad, hidden_grad = pl.pallas_call(
        kernel,
        out_shape=(
            jax.ShapeDtypeStruct((1, 1), F32),
            jax.ShapeDtypeStruct((YL, NZ, FEATS, VOCAB_DEV), BF16),
            jax.ShapeDtypeStruct((ROWS, FEATS), BF16),
        ),
        in_specs=[hbm, hbm, hbm],
        out_specs=(pl.BlockSpec(memory_space=pltpu.SMEM), pl.BlockSpec(memory_space=pl.ANY), vmem),
        scratch_shapes=[
            v((ROWS, FEATS), BF16), v((1, TOKENS), jnp.int32),
            v((YL, NZ, FA, VOCAB_DEV), BF16), v((YL, NZ, FB, VOCAB_DEV), BF16), v((NZ, YL, FC, VOCAB_DEV), BF16),
            v((YL, NZ, FA, VOCAB_DEV), BF16), v((YL, NZ, FB, VOCAB_DEV), BF16), v((NZ, YL, FC, VOCAB_DEV), BF16),
            v((YL, VOCAB_CHIP, WA), BF16), v((YL, VOCAB_CHIP, WB), BF16), v((NZ, VOCAB_CHIP, WC), BF16),
            v((YL, NC) + halves + (WA,), BF16), v((YL, NC) + halves + (WB,), BF16), v((NZ, NC) + halves + (WC,), BF16),
            v((2, PAD, 128), F32), v((PAD, 128), BF16), v((PAD, 128), BF16),
            v((NZ, PAD, 128), BF16), v((NY, PAD, 128), BF16),
            v((PAD, WA), F32), v((PAD, WB), F32), v((YH, PAD, WC), F32),
            v((5, 8, HALF), F32), v((3, 8, HALF), F32), v((7, 8, HALF), F32), v((7, 8, HALF), F32),
            v((3, 8, HALF), F32), v((3, 8, HALF), F32), v((NY, 8, HALF), F32), v((7, 8, HALF), F32),
            v(halves + (128,), F32),
            v((YL,) + halves + (WA,), F32), v((YL,) + halves + (WB,), F32), v((NZ,) + halves + (WC,), F32),
            v((YL,) + halves + (WA,), BF16), v((YL,) + halves + (WB,), BF16), v((NZ,) + halves + (WC,), BF16),
            v((NX, YL, YH, PAD, WA), BF16), v((NY, NX, PAD, WB), BF16), v((NZ,) + halves + (WC,), BF16),
            v((YL,) + halves + (WA,), BF16), v((YL,) + halves + (WB,), BF16), v((NZ,) + halves + (WC,), BF16),
            v((YL,) + halves + (WA,), BF16), v((YL,) + halves + (WB,), BF16), v((NZ,) + halves + (WC,), BF16),
            v((YL,) + halves + (WA,), BF16), v((YL,) + halves + (WB,), BF16), v((NZ,) + halves + (WC,), BF16),
            v((NX, YL, YH, PAD, WA), BF16), v((NY, NX, PAD, WB), BF16), v((NZ,) + halves + (WC,), BF16),
            v((YL, YH, PAD, WA), BF16), v((NX, PAD, WB), BF16), v(halves + (WC,), BF16),
            v((NY, PAD, WA), BF16), v((NX, PAD, WB), BF16), v((NX, YH, PAD, WC), BF16),
            v((YL, YH, PAD, WA), BF16), v((NX, PAD, WB), BF16), v(halves + (WC,), BF16),
            v((NY, PAD, WA), BF16), v((NX, PAD, WB), BF16), v((NX, YH, PAD, WC), BF16),
            v((NZ, PAD, 128), F32), v((NY, PAD, 128), F32), v((NZ, PAD, 128), F32), v((NY, PAD, 128), F32),
            v((YL, NZ, FA, VOCAB_DEV), BF16), v((YL, NZ, FB, VOCAB_DEV), BF16), v((NZ, YL, FC, VOCAB_DEV), BF16),
            v((HALF, VOCAB_DEV), BF16), v((HALF, VOCAB_DEV), BF16), v((8, HALF), F32), v((8, HALF), F32),
            dma((12,)), dma((10,)), dma((208,)), dma((208,)),
        ],
        compiler_params=pltpu.CompilerParams(
            collective_id=0, has_side_effects=True, vmem_limit_bytes=44 * 2**20),
        name="output_layer",
    )(*[pltpu.with_memory_space_constraint(operand, pltpu.HBM) for operand in (
        hidden, head_weight.reshape(YL, NZ, FEATS, VOCAB_DEV), targets.reshape(1, TOKENS))])
    return loss.reshape(()), head_grad.reshape(D, VOCAB_DEV), hidden_grad


def solution(mesh):
    placed = (P("section", "tp"), P(None, ("section", "tp")), P())
    return jax.shard_map(
        per_device,
        mesh=mesh,
        in_specs=placed,
        out_specs=(P(), P(None, ("section", "tp")), P("section", "tp")),
        check_vma=False,
    )
```

```python
import functools

import jax
import jax.numpy as jnp
from jax import lax
from jax.experimental import pallas as pl
from jax.experimental.pallas import tpu as pltpu
from jax.sharding import PartitionSpec as P

MESH = pl.DeviceIdType.MESH
F32 = jnp.float32
BF16 = jnp.bfloat16
NX, NY, NZ, NC = 4, 8, 8, 2
YH, YL = 2, 4
ROWS = 13
PAD = 16
FEATS = 144
FA, FB, FC = 80, 32, 32
WA, WB, WC = NZ * FA, NZ * FB, YL * FC
HALF = YH * NX * PAD
TALL = NC * HALF
D = YL * NZ * FEATS
VOCAB_DEV = 256
VOCAB_CHIP = NC * VOCAB_DEV
TOKENS = 208
ORDER = (1, 7, 2, 6, 3, 5, 4)
XORDER = (1, 3, 2)
OWN = NY + NX + NX
MISS = OWN + 1


def kernel(shard_hbm, weight_hbm, targets_hbm, loss, head_grad, hidden_grad,
           shard, targets, w_a, w_b, w_c, p_a, p_b, p_c, wt_a, wt_b, wt_c, hid_a, hid_b, hid_c, pad32,
           own_ab, own_c, z_rec, y_rec, line_a, line_b, line_c, stat, st_x, st_m, st_n, st_b, st_c, st_y,
           st_z, coef, keep_a, keep_b, keep_c, s1_a, s1_b, s1_c, r1_a, r1_b, r1_c, tk_a, tk_b, tk_c, to_a,
           to_b, to_c, ti_a, ti_b, ti_c, tr_a, tr_b, tr_c, t2_a, t2_b, t2_c, t3_a, t3_b, t3_c, s2_a, s2_b,
           s2_c, r2_a, r2_b, r2_c, s3_ab, s3_c, r3_ab, r3_c, g_a, g_b, g_c, p_out, p_in, l_out, l_in, local,
           gsem, ssem, rsem):
    s = lax.axis_index("section")
    t = lax.axis_index("tp")
    x, yh, c = s // 4, (s // 2) % 2, s % 2
    yl, z = t // NZ, t % NZ
    y = yh * YL + yl

    def at(x_, y_, z_, c_):
        return {"section": x_ * 4 + (y_ // YL) * 2 + c_, "tp": (y_ % YL) * NZ + z_}

    def z_peer(d):
        return at(x, y, (z + d) % NZ, c)

    def y_peer(d):
        return at(x, (y + d) % NY, z, c)

    def x_peer(d):
        return at((x + d) % NX, y, z, c)

    sent = []

    def go(src, dst, peer):
        n = len(sent)
        copy = pltpu.make_async_remote_copy(
            src_ref=src, dst_ref=dst, send_sem=ssem.at[n], recv_sem=rsem.at[n], device_id=peer, device_id_type=MESH)
        copy.start()
        sent.append(copy)
        return copy

    peers = [z_peer(d) for d in ORDER] + [y_peer(d) for d in ORDER] + [x_peer(d) for d in XORDER]
    partner = at(x, y, z, 1 - c)
    peers.append(partner)
    barrier = pltpu.get_barrier_semaphore()
    for peer in peers:
        pl.semaphore_signal(barrier, inc=1, device_id=peer, device_id_type=MESH)

    fetch_small = [
        pltpu.make_async_copy(shard_hbm, shard, local.at[0]),
        pltpu.make_async_copy(targets_hbm, targets, local.at[1]),
    ]
    fetch = [
        pltpu.make_async_copy(weight_hbm.at[:, :, 0:FA], w_a, local.at[2]),
        pltpu.make_async_copy(weight_hbm.at[:, :, FA:FA + FB], w_b, local.at[3]),
    ] + [
        pltpu.make_async_copy(weight_hbm.at[:, i, FA + FB:FEATS], w_c.at[i], local.at[4 + i]) for i in range(NZ)
    ]
    for copy in fetch_small + fetch:
        copy.start()

    for copy in fetch_small:
        copy.wait()
    pad32[...] = jnp.zeros_like(pad32)
    pad32[0, 0:ROWS, 0:FA + FB] = shard[:, 0:FA + FB].astype(F32)
    pad32[1, 0:ROWS, 0:FC] = shard[:, FA + FB:FEATS].astype(F32)
    mine_ab, mine_c = pad32[0].astype(BF16), pad32[1].astype(BF16)
    own_ab[...] = mine_ab
    own_c[...] = mine_c

    row = lax.broadcasted_iota(jnp.int32, (TALL, TOKENS), 0)
    section = (row // PAD) % NX * 4 + (row // (PAD * NX)) % YH * 2 + (row // HALF + c) % 2
    match = (section * ROWS + row % PAD == lax.broadcasted_iota(jnp.int32, (TALL, TOKENS), 1)) & (row % PAD < ROWS)
    goal = jnp.sum(jnp.where(match, targets[...].astype(F32), 0.0), axis=1, keepdims=True).astype(jnp.int32)
    mine = (s * (YL * NZ) + t) * VOCAB_DEV
    mate = ((s + 1 - 2 * c) * (YL * NZ) + t) * VOCAB_DEV
    hot = lax.broadcasted_iota(jnp.int32, (TALL, VOCAB_DEV), 1) + mine == goal
    entry = lax.broadcasted_iota(jnp.int32, (HALF, VOCAB_CHIP), 1)
    hit = jnp.where(entry < VOCAB_DEV, entry + mine, entry + (mate - VOCAB_DEV)) == goal[0:HALF]

    def dot(a, b, dims):
        return lax.dot_general(a, b, (dims, ((), ())), preferred_element_type=F32)

    nn, tn = ((1,), (0,)), ((0,), (0,))
    halves = (YH, NX, PAD)
    turn = [(yl + k) % YL for k in range(YL)]

    pl.semaphore_wait(barrier, len(peers))

    z_copies = [go(own_ab, z_rec.at[z], z_peer(d)) for d in ORDER]
    y_copies = [go(own_c, y_rec.at[y], y_peer(d)) for d in ORDER]
    z_rec[z] = mine_ab
    y_rec[y] = mine_c

    for copy in fetch:
        copy.wait()
    def transpose(parts, at_row):
        rows = pl.ds(at_row, VOCAB_DEV)
        for part, into in zip(parts, (wt_a, wt_b, wt_c)):
            for j in range(into.shape[0]):
                into[j, rows] = part[j].reshape(into.shape[2], VOCAB_DEV).T

    transpose((w_a, w_b, w_c), 0)

    hot = hot.astype(F32).astype(BF16)
    t_core = []
    for keep, out, into, weight in ((tk_c, to_c, ti_c, wt_c), (tk_a, to_a, ti_a, wt_a), (tk_b, to_b, ti_b, wt_b)):
        for j in range(keep.shape[0]):
            chunk = turn[j] if weight is wt_a else j
            column = dot(hot, weight[chunk, 0:VOCAB_DEV], nn).astype(BF16)
            keep[j] = column[0:HALF].reshape(keep.shape[1:])
            out[j] = column[HALF:TALL].reshape(keep.shape[1:])
        t_core.append(go(out, into, partner))
    w_core = [go(src, dst, partner) for src, dst in ((w_a, p_a), (w_b, p_b), (w_c, p_c))]

    def both_columns(copy, keep, into):
        copy.wait_recv()
        for j in range(keep.shape[0]):
            keep[j] = keep[j] + into[j]

    for copy in z_copies:
        copy.wait_recv()
    for i in range(NZ):
        part = z_rec[i].astype(F32)
        line_a[:, FA * i:FA * (i + 1)] = part[:, 0:FA]
        line_b[:, FB * i:FB * (i + 1)] = part[:, FA:FA + FB]
    hid_a[yl, 0, yh, x] = line_a[...].astype(BF16)
    hid_b[yl, 0, yh, x] = line_b[...].astype(BF16)

    block = hid_a.at[yl, 0, yh, x]
    a_y = {d: go(block, block, y_peer(d)) for d in ORDER}
    block = hid_b.at[yl, 0, yh, x]
    b_x = [go(block, block, x_peer(d)) for d in XORDER]
    for copy in y_copies:
        copy.wait_recv()
    for i in range(NY):
        line_c[i // YL, :, FC * (i % YL):FC * (i % YL + 1)] = y_rec[i].astype(F32)[:, 0:FC]
    hid_c[z, 0, :, x] = line_c[...].astype(BF16)
    block = hid_c.at[z, 0, :, x]
    c_x = [go(block, block, x_peer(d)) for d in XORDER]

    a_x = []

    def pass_a(d):
        from_y = (y + NY - d) % NY
        block = hid_a.at[from_y % YL, 0, from_y // YL, x]
        a_x.extend([go(block, block, x_peer(dx)) for dx in XORDER])

    pass_a(0)

    def wide_a(src, dst, k):
        return [go(src.at[k, :, (x + d) % NX], dst.at[d, k], x_peer(d)) for d in XORDER]

    def wide_b(src, dst):
        return [go(src.at[(y + d) % NY % YL, (y + d) % NY // YL], dst.at[d], y_peer(d)) for d in ORDER]

    def wide_c(src, dst):
        return [go(src.at[(z + d) % NZ], dst.at[d], z_peer(d)) for d in ORDER]


    for copy in b_x:
        copy.wait_recv()
    block = hid_b.at[yl, 0, yh]
    b_y = [go(block, block, y_peer(d)) for d in ORDER]
    for copy in c_x:
        copy.wait_recv()
    block = hid_c.at[z, 0]
    c_z = [go(block, block, z_peer(d)) for d in ORDER]
    for d in ORDER:
        a_y[d].wait_recv()
        pass_a(d)

    both_columns(t_core[0], tk_c, ti_c)
    tc_z = wide_c(tk_c, tr_c)
    both_columns(t_core[1], tk_a, ti_a)
    ta_x = [wide_a(tk_a, tr_a, k) for k in range(YL)]
    both_columns(t_core[2], tk_b, ti_b)
    tb_y = wide_b(tk_b, tr_b)
    for copy in w_core:
        copy.wait_recv()
    transpose((p_a, p_b, p_c), VOCAB_DEV)

    def add_logits(sums, hid, parts):
        for j in range(hid.shape[0]):
            left = hid[j, 0].reshape(HALF, hid.shape[-1])
            sums = [so + dot(left, part[j].reshape(hid.shape[-1], VOCAB_DEV), nn) for so, part in zip(sums, parts)]
        return sums

    for copy in a_x:
        copy.wait_recv()
    sums = add_logits([jnp.zeros((HALF, VOCAB_DEV), F32)] * NC, hid_a, (w_a, p_a))
    for copy in b_y:
        copy.wait_recv()
    sums = add_logits(sums, hid_b, (w_b, p_b))
    for copy in c_z:
        copy.wait_recv()
    sums = add_logits(sums, hid_c, (w_c, p_c))
    logits = jnp.concatenate(sums, axis=1)

    top = jnp.max(logits, axis=1, keepdims=True)
    shifted = jnp.exp(logits - top)
    rest = jnp.sum(jnp.where(hit, 0.0, shifted), axis=1, keepdims=True)
    aim = jnp.sum(jnp.where(hit, shifted, 0.0), axis=1, keepdims=True)
    picked = jnp.sum(jnp.where(hit, logits, 0.0), axis=1, keepdims=True)
    others = jnp.where(hit, 0.0, shifted).astype(BF16)

    lane = lax.broadcasted_iota(jnp.int32, (HALF, 128), 1)
    columns = jnp.where(lane == 0, top, jnp.where(lane == 1, rest, jnp.where(lane == 2, picked, jnp.where(
        lane == 3, aim, 0.0))))
    tall = columns.T[0:8, :]
    stat[0] = tall

    def merge(parts):
        best = functools.reduce(jnp.maximum, [p[0:1, :] for p in parts])
        scale = [jnp.exp(p[0:1, :] - best) for p in parts]
        rest_ = sum(p[1:2, :] * f for p, f in zip(parts, scale))
        pick_ = sum(p[2:3, :] for p in parts)
        aim_ = sum(p[3:4, :] * f for p, f in zip(parts, scale))
        return jnp.concatenate([best, rest_, pick_, aim_, jnp.zeros((4, HALF), F32)], axis=0)

    def columns_of(rows):
        full = jnp.concatenate(rows + [jnp.zeros((128 - len(rows), HALF), F32)], axis=0)
        return full.T

    to_x = [go(stat.at[0], st_x.at[i], x_peer(d)) for i, d in enumerate(XORDER)]
    to_y = [go(stat.at[0], st_m.at[i], y_peer(d)) for i, d in enumerate(ORDER)]
    to_z = [go(stat.at[0], st_n.at[i], z_peer(d)) for i, d in enumerate(ORDER)]

    def term(weight, keep, send):
        terms = dot(others, weight, nn).reshape(keep.shape)
        keep[...] = terms
        send[...] = terms.astype(BF16)

    a_x = []
    for k in range(YL):
        term(wt_a[turn[k]], keep_a.at[k], s1_a.at[k])
        a_x.append(wide_a(s1_a, r1_a, k))
    for j in range(YL):
        term(wt_b[j], keep_b.at[j], s1_b.at[j])
    b_y = wide_b(s1_b, r1_b)
    for j in range(NZ):
        term(wt_c[j], keep_c.at[j], s1_c.at[j])
    c_z = wide_c(s1_c, r1_c)
    for copy in to_x:
        copy.wait_recv()
    line = merge([tall] + [st_x[i] for i in range(len(XORDER))])
    stat[1] = line
    y_turn = [(e, k, at(x, (yh + e) % YH * YL + turn[k], z, c)) for e in range(YH) for k in range(YL) if e or k]
    along_y = [go(stat.at[1], st_y.at[e * YL + k], peer) for e, k, peer in y_turn]
    h_core = [go(hid.at[:, 0], hid.at[:, 1], partner) for hid in (hid_a, hid_b, hid_c)]

    def second_a(src, dst, k):
        return [go(src.at[k, (yh + e) % YH], dst.at[e * YL + k], peer) for e, k_, peer in y_turn if k_ == k]

    def second_b(src, dst):
        return [go(src.at[(x + d) % NX], dst.at[d], x_peer(d)) for d in XORDER]

    def second_c(src, dst):
        return [go(src.at[:, (x + d) % NX], dst.at[d], x_peer(d)) for d in XORDER]

    ta_y = []
    for k in range(YL):
        for copy in ta_x[k]:
            copy.wait_recv()
        t2_a[k] = tk_a[k, :, x] + sum(tr_a[d, k] for d in XORDER)
        ta_y += second_a(t2_a, t3_a, k)
    for copy in tb_y:
        copy.wait_recv()
    t2_b[...] = tk_b[yl, yh] + sum(tr_b[d] for d in ORDER)
    tb_x = second_b(t2_b, t3_b)
    for copy in tc_z:
        copy.wait_recv()
    t2_c[...] = tk_c[z] + sum(tr_c[d] for d in ORDER)
    tc_x = second_c(t2_c, t3_c)

    for copy in to_y + to_z:
        copy.wait_recv()
    near_y, near_z = ([tall] + [st[i] for i in range(len(ORDER))] for st in (st_m, st_n))
    line_y, line_z = merge(near_y), merge(near_z)
    stat[2] = line_y
    stat[3] = line_z
    tiles_x = [go(stat.at[2], st_b.at[i], x_peer(d)) for i, d in enumerate(XORDER)]
    tiles_x += [go(stat.at[3], st_c.at[i], x_peer(d)) for i, d in enumerate(XORDER)]

    def ratios(parts, best):
        return [jnp.exp(p[0:1, :] - best[0:1, :]) for p in parts]

    near_x = [tall] + [st_x[i] for i in range(len(XORDER))]
    scales = ratios(near_x, line) + ratios(near_y, line_y) + ratios(near_z, line_z)
    coef[...] = columns_of(scales).reshape(halves + (128,))

    def scaled(own, others_, f, first):
        parts = [own] + [other.astype(F32) for other in others_]
        return sum(p * f[..., first + i:first + i + 1] for i, p in enumerate(parts))

    a_y = []
    f_x = coef[:, x]
    for k in range(YL):
        for copy in a_x[k]:
            copy.wait_recv()
        chunk = scaled(keep_a[k, :, x], [r1_a[d, k] for d in XORDER], f_x, 0)
        s2_a[k] = chunk.astype(BF16)
        if k == 0:
            keep_a[0, :, 0] = chunk
        a_y += second_a(s2_a, r2_a, k)
    for copy in along_y:
        copy.wait_recv()
    lines = [line] + [st_y[n] for n in range(1, NY)]
    plane = merge(lines)
    stat[4] = plane
    along_z = [go(stat.at[4], st_z.at[i], z_peer(d)) for i, d in enumerate(ORDER)]
    for copy in b_y:
        copy.wait_recv()
    sum_b = scaled(keep_b[yl, yh], [r1_b[d] for d in ORDER], coef[yh], NX)
    s2_b[...] = sum_b.astype(BF16)
    keep_b[0, 0] = sum_b
    b_x = second_b(s2_b, r2_b)
    for copy in c_z:
        copy.wait_recv()
    sum_c = scaled(keep_c[z], [r1_c[d] for d in ORDER], coef[...], NX + NY)
    s2_c[...] = sum_c.astype(BF16)
    keep_c[0] = sum_c
    c_x = second_c(s2_c, r2_c)

    for copy in tiles_x + along_z:
        copy.wait_recv()
    whole = merge([plane] + [st_z[i] for i in range(len(ORDER))])
    highest, total = whole[0:1, :], whole[1:2, :] + whole[3:4, :]
    slot = lax.broadcasted_iota(jnp.int32, (1, HALF), 1)
    each = jnp.where(slot % PAD < ROWS, highest + jnp.log(total) - whole[2:3, :], 0.0)
    miss = (whole[1:2, :] / total).astype(BF16).astype(F32)
    lines_y = [line_y] + [st_b[i] for i in range(len(XORDER))]
    lines_z = [line_z] + [st_c[i] for i in range(len(XORDER))]
    factors = columns_of([f / total for f in ratios(lines + lines_y + lines_z + [tall], whole)] + [miss])
    coef[...] = factors.reshape(halves + (128,))
    probs = (shifted * factors[:, OWN:OWN + 1]).astype(BF16)
    p_out[...] = probs[:, VOCAB_DEV:VOCAB_CHIP]
    l_out[...] = jnp.concatenate([each, jnp.zeros((7, HALF), F32)], axis=0)
    swap = h_core + [go(p_out, p_in, partner), go(l_out, l_in, partner)]

    for copy in c_x + tc_x:
        copy.wait_recv()
    f_c, f_ab = coef[:, x], coef[yh, x]
    part_c = scaled(keep_c[0, :, x], [r2_c[d] for d in XORDER], f_c, NY + NX)
    column = t2_c[:, x] + sum(t3_c[d] for d in XORDER)
    part_c = part_c - column.astype(F32) * f_c[..., MISS:MISS + 1]
    for i in range(NY):
        s3_c[i, :, 0:FC] = part_c[i // YL, :, FC * (i % YL):FC * (i % YL + 1)]
    c_y = [go(s3_c.at[(y + d) % NY], r3_c.at[d], y_peer(d)) for d in ORDER]
    for copy in b_x + tb_x:
        copy.wait_recv()
    part_b = scaled(keep_b[0, 0, x], [r2_b[d] for d in XORDER], f_ab, NY)
    column = t2_b[x] + sum(t3_b[d] for d in XORDER)
    part_b = part_b - column.astype(F32) * f_ab[..., MISS:MISS + 1]
    for copy in a_y + ta_y:
        copy.wait_recv()
    part_a = scaled(keep_a[0, yh, 0], [r2_a[n] for n in range(1, NY)], f_ab, 0)
    column = t2_a[0, yh] + sum(t3_a[n] for n in range(1, NY))
    part_a = part_a - column.astype(F32) * f_ab[..., MISS:MISS + 1]
    for i in range(NZ):
        s3_ab[i, :, 0:FA] = part_a[:, FA * i:FA * (i + 1)]
        s3_ab[i, :, FA:FA + FB] = part_b[:, FB * i:FB * (i + 1)]
    ab_z = [go(s3_ab.at[(z + d) % NZ], r3_ab.at[d], z_peer(d)) for d in ORDER]

    for copy in swap:
        copy.wait_recv()
    loss[0, 0] = (jnp.sum(each) + jnp.sum(l_in[0:1, :])) / TOKENS
    probs = jnp.concatenate([probs[:, 0:VOCAB_DEV], p_in[...]], axis=0)
    for hid, grad in ((hid_a, g_a), (hid_b, g_b), (hid_c, g_c)):
        for j in range(hid.shape[0]):
            left = hid[j].reshape(TALL, hid.shape[-1])
            grad[j] = dot(left, probs, tn).astype(BF16).reshape(grad.shape[1:])
    writes = [
        pltpu.make_async_copy(g_a, head_grad.at[:, :, 0:FA], gsem.at[0]),
        pltpu.make_async_copy(g_b, head_grad.at[:, :, FA:FA + FB], gsem.at[1]),
    ] + [
        pltpu.make_async_copy(g_c.at[i], head_grad.at[:, i, FA + FB:FEATS], gsem.at[2 + i]) for i in range(NZ)
    ]
    for write in writes:
        write.start()

    for copy in c_y:
        copy.wait_recv()
    done_c = s3_c[y][:, 0:FC] + sum(r3_c[d][:, 0:FC] for d in ORDER)
    hidden_grad[:, FA + FB:FEATS] = done_c[0:ROWS].astype(BF16)
    for copy in ab_z:
        copy.wait_recv()
    done_ab = s3_ab[z][:, 0:FA + FB] + sum(r3_ab[d][:, 0:FA + FB] for d in ORDER)
    hidden_grad[:, 0:FA + FB] = done_ab[0:ROWS].astype(BF16)

    for copy in sent:
        copy.wait_send()
    for write in writes:
        write.wait()


def per_device(hidden, head_weight, targets):
    vmem = pl.BlockSpec(memory_space=pltpu.VMEM)
    hbm = pl.BlockSpec(memory_space=pltpu.HBM)
    v = pltpu.VMEM
    dma = pltpu.SemaphoreType.DMA
    halves = (YH, NX, PAD)
    loss, head_grad, hidden_grad = pl.pallas_call(
        kernel,
        out_shape=(
            jax.ShapeDtypeStruct((1, 1), F32),
            jax.ShapeDtypeStruct((YL, NZ, FEATS, VOCAB_DEV), BF16),
            jax.ShapeDtypeStruct((ROWS, FEATS), BF16),
        ),
        in_specs=[hbm, hbm, hbm],
        out_specs=(pl.BlockSpec(memory_space=pltpu.SMEM), pl.BlockSpec(memory_space=pl.ANY), vmem),
        scratch_shapes=[
            v((ROWS, FEATS), BF16), v((1, TOKENS), jnp.int32),
            v((YL, NZ, FA, VOCAB_DEV), BF16), v((YL, NZ, FB, VOCAB_DEV), BF16), v((NZ, YL, FC, VOCAB_DEV), BF16),
            v((YL, NZ, FA, VOCAB_DEV), BF16), v((YL, NZ, FB, VOCAB_DEV), BF16), v((NZ, YL, FC, VOCAB_DEV), BF16),
            v((YL, VOCAB_CHIP, WA), BF16), v((YL, VOCAB_CHIP, WB), BF16), v((NZ, VOCAB_CHIP, WC), BF16),
            v((YL, NC) + halves + (WA,), BF16), v((YL, NC) + halves + (WB,), BF16), v((NZ, NC) + halves + (WC,), BF16),
            v((2, PAD, 128), F32), v((PAD, 128), BF16), v((PAD, 128), BF16),
            v((NZ, PAD, 128), BF16), v((NY, PAD, 128), BF16),
            v((PAD, WA), F32), v((PAD, WB), F32), v((YH, PAD, WC), F32),
            v((5, 8, HALF), F32), v((3, 8, HALF), F32), v((7, 8, HALF), F32), v((7, 8, HALF), F32),
            v((3, 8, HALF), F32), v((3, 8, HALF), F32), v((NY, 8, HALF), F32), v((7, 8, HALF), F32),
            v(halves + (128,), F32),
            v((YL,) + halves + (WA,), F32), v((YL,) + halves + (WB,), F32), v((NZ,) + halves + (WC,), F32),
            v((YL,) + halves + (WA,), BF16), v((YL,) + halves + (WB,), BF16), v((NZ,) + halves + (WC,), BF16),
            v((NX, YL, YH, PAD, WA), BF16), v((NY, NX, PAD, WB), BF16), v((NZ,) + halves + (WC,), BF16),
            v((YL,) + halves + (WA,), BF16), v((YL,) + halves + (WB,), BF16), v((NZ,) + halves + (WC,), BF16),
            v((YL,) + halves + (WA,), BF16), v((YL,) + halves + (WB,), BF16), v((NZ,) + halves + (WC,), BF16),
            v((YL,) + halves + (WA,), BF16), v((YL,) + halves + (WB,), BF16), v((NZ,) + halves + (WC,), BF16),
            v((NX, YL, YH, PAD, WA), BF16), v((NY, NX, PAD, WB), BF16), v((NZ,) + halves + (WC,), BF16),
            v((YL, YH, PAD, WA), BF16), v((NX, PAD, WB), BF16), v(halves + (WC,), BF16),
            v((NY, PAD, WA), BF16), v((NX, PAD, WB), BF16), v((NX, YH, PAD, WC), BF16),
            v((YL, YH, PAD, WA), BF16), v((NX, PAD, WB), BF16), v(halves + (WC,), BF16),
            v((NY, PAD, WA), BF16), v((NX, PAD, WB), BF16), v((NX, YH, PAD, WC), BF16),
            v((NZ, PAD, 128), F32), v((NY, PAD, 128), F32), v((NZ, PAD, 128), F32), v((NY, PAD, 128), F32),
            v((YL, NZ, FA, VOCAB_DEV), BF16), v((YL, NZ, FB, VOCAB_DEV), BF16), v((NZ, YL, FC, VOCAB_DEV), BF16),
            v((HALF, VOCAB_DEV), BF16), v((HALF, VOCAB_DEV), BF16), v((8, HALF), F32), v((8, HALF), F32),
            dma((12,)), dma((10,)), dma((208,)), dma((208,)),
        ],
        compiler_params=pltpu.CompilerParams(
            collective_id=0, has_side_effects=True, vmem_limit_bytes=44 * 2**20),
        name="output_layer",
    )(*[pltpu.with_memory_space_constraint(operand, pltpu.HBM) for operand in (
        hidden, head_weight.reshape(YL, NZ, FEATS, VOCAB_DEV), targets.reshape(1, TOKENS))])
    return loss.reshape(()), head_grad.reshape(D, VOCAB_DEV), hidden_grad


def solution(mesh):
    placed = (P("section", "tp"), P(None, ("section", "tp")), P())
    return jax.shard_map(
        per_device,
        mesh=mesh,
        in_specs=placed,
        out_specs=(P(), P(None, ("section", "tp")), P("section", "tp")),
        check_vma=False,
    )
```

```python
import functools

import jax
import jax.numpy as jnp
from jax import lax
from jax.experimental import pallas as pl
from jax.experimental.pallas import tpu as pltpu
from jax.sharding import PartitionSpec as P

MESH = pl.DeviceIdType.MESH
F32 = jnp.float32
BF16 = jnp.bfloat16
NX, NY, NZ, NC = 4, 8, 8, 2
YH, YL = 2, 4
ROWS = 13
PAD = 16
FEATS = 144
FA, FB, FC = 80, 32, 32
WA, WB, WC = NZ * FA, NZ * FB, YL * FC
HALF = YH * NX * PAD
TALL = NC * HALF
D = YL * NZ * FEATS
VOCAB_DEV = 256
VOCAB_CHIP = NC * VOCAB_DEV
TOKENS = 208
ORDER = (1, 7, 2, 6, 3, 5, 4)
XORDER = (1, 3, 2)
OWN = NY + NX + NX
MISS = OWN + 1


def kernel(shard_hbm, weight_hbm, targets_hbm, loss, head_grad, hidden_grad,
           shard, targets, w_a, w_b, w_c, p_a, p_b, p_c, wt_a, wt_b, wt_c, hid_a, hid_b, hid_c, pad32,
           own_ab, own_c, z_rec, y_rec, line_a, line_b, line_c, stat, st_x, st_m, st_n, st_b, st_c, st_y,
           st_z, coef, keep_a, keep_b, keep_c, s1_a, s1_b, s1_c, r1_a, r1_b, r1_c, tk_a, tk_b, tk_c, to_a,
           to_b, to_c, ti_a, ti_b, ti_c, tr_a, tr_b, tr_c, t2_a, t2_b, t2_c, t3_a, t3_b, t3_c, s2_a, s2_b,
           s2_c, r2_a, r2_b, r2_c, s3_ab, s3_c, r3_ab, r3_c, g_a, g_b, g_c, p_out, p_in, l_out, l_in, local,
           gsem, ssem, rsem):
    s = lax.axis_index("section")
    t = lax.axis_index("tp")
    x, yh, c = s // 4, (s // 2) % 2, s % 2
    yl, z = t // NZ, t % NZ
    y = yh * YL + yl

    def at(x_, y_, z_, c_):
        return {"section": x_ * 4 + (y_ // YL) * 2 + c_, "tp": (y_ % YL) * NZ + z_}

    def z_peer(d):
        return at(x, y, (z + d) % NZ, c)

    def y_peer(d):
        return at(x, (y + d) % NY, z, c)

    def x_peer(d):
        return at((x + d) % NX, y, z, c)

    sent = []

    def go(src, dst, peer):
        n = len(sent)
        copy = pltpu.make_async_remote_copy(
            src_ref=src, dst_ref=dst, send_sem=ssem.at[n], recv_sem=rsem.at[n], device_id=peer, device_id_type=MESH)
        copy.start()
        sent.append(copy)
        return copy

    peers = [z_peer(d) for d in ORDER] + [y_peer(d) for d in ORDER] + [x_peer(d) for d in XORDER]
    partner = at(x, y, z, 1 - c)
    peers.append(partner)
    barrier = pltpu.get_barrier_semaphore()
    for peer in peers:
        pl.semaphore_signal(barrier, inc=1, device_id=peer, device_id_type=MESH)

    fetch_small = [
        pltpu.make_async_copy(shard_hbm, shard, local.at[0]),
        pltpu.make_async_copy(targets_hbm, targets, local.at[1]),
    ]
    fetch = [
        pltpu.make_async_copy(weight_hbm.at[:, :, 0:FA], w_a, local.at[2]),
        pltpu.make_async_copy(weight_hbm.at[:, :, FA:FA + FB], w_b, local.at[3]),
    ] + [
        pltpu.make_async_copy(weight_hbm.at[:, i, FA + FB:FEATS], w_c.at[i], local.at[4 + i]) for i in range(NZ)
    ]
    for copy in fetch_small + fetch:
        copy.start()

    for copy in fetch_small:
        copy.wait()
    pad32[...] = jnp.zeros_like(pad32)
    pad32[0, 0:ROWS, 0:FA + FB] = shard[:, 0:FA + FB].astype(F32)
    pad32[1, 0:ROWS, 0:FC] = shard[:, FA + FB:FEATS].astype(F32)
    mine_ab, mine_c = pad32[0].astype(BF16), pad32[1].astype(BF16)
    own_ab[...] = mine_ab
    own_c[...] = mine_c

    row = lax.broadcasted_iota(jnp.int32, (TALL, TOKENS), 0)
    section = (row // PAD) % NX * 4 + (row // (PAD * NX)) % YH * 2 + (row // HALF + c) % 2
    match = (section * ROWS + row % PAD == lax.broadcasted_iota(jnp.int32, (TALL, TOKENS), 1)) & (row % PAD < ROWS)
    goal = jnp.sum(jnp.where(match, targets[...].astype(F32), 0.0), axis=1, keepdims=True).astype(jnp.int32)
    mine = (s * (YL * NZ) + t) * VOCAB_DEV
    mate = ((s + 1 - 2 * c) * (YL * NZ) + t) * VOCAB_DEV
    hot = lax.broadcasted_iota(jnp.int32, (TALL, VOCAB_DEV), 1) + mine == goal
    entry = lax.broadcasted_iota(jnp.int32, (HALF, VOCAB_CHIP), 1)
    hit = jnp.where(entry < VOCAB_DEV, entry + mine, entry + (mate - VOCAB_DEV)) == goal[0:HALF]

    def dot(a, b, dims):
        return lax.dot_general(a, b, (dims, ((), ())), preferred_element_type=F32)

    nn, tn = ((1,), (0,)), ((0,), (0,))
    halves = (YH, NX, PAD)
    turn = [(yl + k) % YL for k in range(YL)]

    pl.semaphore_wait(barrier, len(peers))

    z_copies = [go(own_ab, z_rec.at[z], z_peer(d)) for d in ORDER]
    y_copies = [go(own_c, y_rec.at[y], y_peer(d)) for d in ORDER]
    z_rec[z] = mine_ab
    y_rec[y] = mine_c

    for copy in fetch:
        copy.wait()
    def transpose(parts, at_row):
        rows = pl.ds(at_row, VOCAB_DEV)
        for part, into in zip(parts, (wt_a, wt_b, wt_c)):
            for j in range(into.shape[0]):
                into[j, rows] = part[j].reshape(into.shape[2], VOCAB_DEV).T

    transpose((w_a, w_b, w_c), 0)

    hot = hot.astype(F32).astype(BF16)
    t_core = []
    for keep, out, into, weight in ((tk_c, to_c, ti_c, wt_c), (tk_a, to_a, ti_a, wt_a), (tk_b, to_b, ti_b, wt_b)):
        for j in range(keep.shape[0]):
            chunk = turn[j] if weight is wt_a else j
            column = dot(hot, weight[chunk, 0:VOCAB_DEV], nn).astype(BF16)
            keep[j] = column[0:HALF].reshape(keep.shape[1:])
            out[j] = column[HALF:TALL].reshape(keep.shape[1:])
        t_core.append(go(out, into, partner))
    w_core = [go(src, dst, partner) for src, dst in ((w_a, p_a), (w_b, p_b), (w_c, p_c))]

    def both_columns(copy, keep, into):
        copy.wait_recv()
        for j in range(keep.shape[0]):
            keep[j] = keep[j] + into[j]

    for copy in z_copies:
        copy.wait_recv()
    for i in range(NZ):
        part = z_rec[i].astype(F32)
        line_a[:, FA * i:FA * (i + 1)] = part[:, 0:FA]
        line_b[:, FB * i:FB * (i + 1)] = part[:, FA:FA + FB]
    hid_a[yl, 0, yh, x] = line_a[...].astype(BF16)
    hid_b[yl, 0, yh, x] = line_b[...].astype(BF16)

    block = hid_a.at[yl, 0, yh, x]
    a_y = {d: go(block, block, y_peer(d)) for d in ORDER}
    block = hid_b.at[yl, 0, yh, x]
    b_x = [go(block, block, x_peer(d)) for d in XORDER]
    for copy in y_copies:
        copy.wait_recv()
    for i in range(NY):
        line_c[i // YL, :, FC * (i % YL):FC * (i % YL + 1)] = y_rec[i].astype(F32)[:, 0:FC]
    hid_c[z, 0, :, x] = line_c[...].astype(BF16)
    block = hid_c.at[z, 0, :, x]
    c_x = [go(block, block, x_peer(d)) for d in XORDER]

    a_x = []

    def pass_a(d):
        from_y = (y + NY - d) % NY
        block = hid_a.at[from_y % YL, 0, from_y // YL, x]
        a_x.extend([go(block, block, x_peer(dx)) for dx in XORDER])

    pass_a(0)

    def wide_a(src, dst, k):
        return [go(src.at[k, :, (x + d) % NX], dst.at[d, k], x_peer(d)) for d in XORDER]

    def wide_b(src, dst):
        return [go(src.at[(y + d) % NY % YL, (y + d) % NY // YL], dst.at[d], y_peer(d)) for d in ORDER]

    def wide_c(src, dst):
        return [go(src.at[(z + d) % NZ], dst.at[d], z_peer(d)) for d in ORDER]


    for copy in b_x:
        copy.wait_recv()
    block = hid_b.at[yl, 0, yh]
    b_y = [go(block, block, y_peer(d)) for d in ORDER]
    for copy in c_x:
        copy.wait_recv()
    block = hid_c.at[z, 0]
    c_z = [go(block, block, z_peer(d)) for d in ORDER]
    for d in ORDER:
        a_y[d].wait_recv()
        pass_a(d)

    both_columns(t_core[0], tk_c, ti_c)
    tc_z = wide_c(tk_c, tr_c)
    both_columns(t_core[1], tk_a, ti_a)
    ta_x = [wide_a(tk_a, tr_a, k) for k in range(YL)]
    both_columns(t_core[2], tk_b, ti_b)
    tb_y = wide_b(tk_b, tr_b)
    for copy in w_core:
        copy.wait_recv()
    transpose((p_a, p_b, p_c), VOCAB_DEV)

    def add_logits(sums, hid, parts):
        for j in range(hid.shape[0]):
            left = hid[j, 0].reshape(HALF, hid.shape[-1])
            sums = [so + dot(left, part[j].reshape(hid.shape[-1], VOCAB_DEV), nn) for so, part in zip(sums, parts)]
        return sums

    for copy in a_x:
        copy.wait_recv()
    sums = add_logits([jnp.zeros((HALF, VOCAB_DEV), F32)] * NC, hid_a, (w_a, p_a))
    for copy in b_y:
        copy.wait_recv()
    sums = add_logits(sums, hid_b, (w_b, p_b))
    for copy in c_z:
        copy.wait_recv()
    sums = add_logits(sums, hid_c, (w_c, p_c))
    logits = jnp.concatenate(sums, axis=1)

    top = jnp.max(logits, axis=1, keepdims=True)
    shifted = jnp.exp(logits - top)
    rest = jnp.sum(jnp.where(hit, 0.0, shifted), axis=1, keepdims=True)
    aim = jnp.sum(jnp.where(hit, shifted, 0.0), axis=1, keepdims=True)
    picked = jnp.sum(jnp.where(hit, logits, 0.0), axis=1, keepdims=True)
    others = jnp.where(hit, 0.0, shifted).astype(BF16)

    lane = lax.broadcasted_iota(jnp.int32, (HALF, 128), 1)
    columns = jnp.where(lane == 0, top, jnp.where(lane == 1, rest, jnp.where(lane == 2, picked, jnp.where(
        lane == 3, aim, 0.0))))
    tall = columns.T[0:8, :]
    stat[0] = tall

    def merge(parts):
        best = functools.reduce(jnp.maximum, [p[0:1, :] for p in parts])
        scale = [jnp.exp(p[0:1, :] - best) for p in parts]
        rest_ = sum(p[1:2, :] * f for p, f in zip(parts, scale))
        pick_ = sum(p[2:3, :] for p in parts)
        aim_ = sum(p[3:4, :] * f for p, f in zip(parts, scale))
        return jnp.concatenate([best, rest_, pick_, aim_, jnp.zeros((4, HALF), F32)], axis=0)

    def columns_of(rows):
        full = jnp.concatenate(rows + [jnp.zeros((128 - len(rows), HALF), F32)], axis=0)
        return full.T

    to_x = [go(stat.at[0], st_x.at[i], x_peer(d)) for i, d in enumerate(XORDER)]
    to_y = [go(stat.at[0], st_m.at[i], y_peer(d)) for i, d in enumerate(ORDER)]
    to_z = [go(stat.at[0], st_n.at[i], z_peer(d)) for i, d in enumerate(ORDER)]

    def term(weight, keep, send):
        terms = dot(others, weight, nn).reshape(keep.shape)
        keep[...] = terms
        send[...] = terms.astype(BF16)

    a_x = []
    for k in range(YL):
        term(wt_a[turn[k]], keep_a.at[k], s1_a.at[k])
        a_x.append(wide_a(s1_a, r1_a, k))
    for j in range(YL):
        term(wt_b[j], keep_b.at[j], s1_b.at[j])
    b_y = wide_b(s1_b, r1_b)
    for j in range(NZ):
        term(wt_c[j], keep_c.at[j], s1_c.at[j])
    c_z = wide_c(s1_c, r1_c)
    for copy in to_x:
        copy.wait_recv()
    line = merge([tall] + [st_x[i] for i in range(len(XORDER))])
    stat[1] = line
    y_turn = [(e, k, at(x, (yh + e) % YH * YL + turn[k], z, c)) for e in range(YH) for k in range(YL) if e or k]
    along_y = [go(stat.at[1], st_y.at[e * YL + k], peer) for e, k, peer in y_turn]
    h_core = [go(hid.at[:, 0], hid.at[:, 1], partner) for hid in (hid_a, hid_b, hid_c)]

    def second_a(src, dst, k):
        return [go(src.at[k, (yh + e) % YH], dst.at[e * YL + k], peer) for e, k_, peer in y_turn if k_ == k]

    def second_b(src, dst):
        return [go(src.at[(x + d) % NX], dst.at[d], x_peer(d)) for d in XORDER]

    def second_c(src, dst):
        return [go(src.at[:, (x + d) % NX], dst.at[d], x_peer(d)) for d in XORDER]

    ta_y = []
    for k in range(YL):
        for copy in ta_x[k]:
            copy.wait_recv()
        t2_a[k] = tk_a[k, :, x] + sum(tr_a[d, k] for d in XORDER)
        ta_y += second_a(t2_a, t3_a, k)
    for copy in tb_y:
        copy.wait_recv()
    t2_b[...] = tk_b[yl, yh] + sum(tr_b[d] for d in ORDER)
    tb_x = second_b(t2_b, t3_b)
    for copy in tc_z:
        copy.wait_recv()
    t2_c[...] = tk_c[z] + sum(tr_c[d] for d in ORDER)
    tc_x = second_c(t2_c, t3_c)

    for copy in to_y + to_z:
        copy.wait_recv()
    near_y, near_z = ([tall] + [st[i] for i in range(len(ORDER))] for st in (st_m, st_n))
    line_y, line_z = merge(near_y), merge(near_z)
    stat[2] = line_y
    stat[3] = line_z
    tiles_x = [go(stat.at[2], st_b.at[i], x_peer(d)) for i, d in enumerate(XORDER)]
    tiles_x += [go(stat.at[3], st_c.at[i], x_peer(d)) for i, d in enumerate(XORDER)]

    def ratios(parts, best):
        return [jnp.exp(p[0:1, :] - best[0:1, :]) for p in parts]

    near_x = [tall] + [st_x[i] for i in range(len(XORDER))]
    scales = ratios(near_x, line) + ratios(near_y, line_y) + ratios(near_z, line_z)
    coef[...] = columns_of(scales).reshape(halves + (128,))

    def scaled(own, others_, f, first):
        parts = [own] + [other.astype(F32) for other in others_]
        return sum(p * f[..., first + i:first + i + 1] for i, p in enumerate(parts))

    a_y = []
    f_x = coef[:, x]
    for k in range(YL):
        for copy in a_x[k]:
            copy.wait_recv()
        chunk = scaled(keep_a[k, :, x], [r1_a[d, k] for d in XORDER], f_x, 0)
        s2_a[k] = chunk.astype(BF16)
        if k == 0:
            keep_a[0, :, 0] = chunk
        a_y += second_a(s2_a, r2_a, k)
    for copy in along_y:
        copy.wait_recv()
    lines = [line] + [st_y[n] for n in range(1, NY)]
    plane = merge(lines)
    stat[4] = plane
    along_z = [go(stat.at[4], st_z.at[i], z_peer(d)) for i, d in enumerate(ORDER)]
    for copy in b_y:
        copy.wait_recv()
    sum_b = scaled(keep_b[yl, yh], [r1_b[d] for d in ORDER], coef[yh], NX)
    s2_b[...] = sum_b.astype(BF16)
    keep_b[0, 0] = sum_b
    b_x = second_b(s2_b, r2_b)
    for copy in c_z:
        copy.wait_recv()
    sum_c = scaled(keep_c[z], [r1_c[d] for d in ORDER], coef[...], NX + NY)
    s2_c[...] = sum_c.astype(BF16)
    keep_c[0] = sum_c
    c_x = second_c(s2_c, r2_c)

    for copy in tiles_x + along_z:
        copy.wait_recv()
    whole = merge([plane] + [st_z[i] for i in range(len(ORDER))])
    highest, total = whole[0:1, :], whole[1:2, :] + whole[3:4, :]
    slot = lax.broadcasted_iota(jnp.int32, (1, HALF), 1)
    each = jnp.where(slot % PAD < ROWS, highest + jnp.log(total) - whole[2:3, :], 0.0)
    miss = (whole[1:2, :] / total).astype(BF16).astype(F32)
    lines_y = [line_y] + [st_b[i] for i in range(len(XORDER))]
    lines_z = [line_z] + [st_c[i] for i in range(len(XORDER))]
    factors = columns_of([f / total for f in ratios(lines + lines_y + lines_z + [tall], whole)] + [miss])
    coef[...] = factors.reshape(halves + (128,))

    for copy in c_x + tc_x:
        copy.wait_recv()
    f_c, f_ab = coef[:, x], coef[yh, x]
    part_c = scaled(keep_c[0, :, x], [r2_c[d] for d in XORDER], f_c, NY + NX)
    column = t2_c[:, x] + sum(t3_c[d] for d in XORDER)
    part_c = part_c - column.astype(F32) * f_c[..., MISS:MISS + 1]
    for i in range(NY):
        s3_c[i, :, 0:FC] = part_c[i // YL, :, FC * (i % YL):FC * (i % YL + 1)]
    c_y = [go(s3_c.at[(y + d) % NY], r3_c.at[d], y_peer(d)) for d in ORDER]
    for copy in b_x + tb_x:
        copy.wait_recv()
    part_b = scaled(keep_b[0, 0, x], [r2_b[d] for d in XORDER], f_ab, NY)
    column = t2_b[x] + sum(t3_b[d] for d in XORDER)
    part_b = part_b - column.astype(F32) * f_ab[..., MISS:MISS + 1]
    for copy in a_y + ta_y:
        copy.wait_recv()
    part_a = scaled(keep_a[0, yh, 0], [r2_a[n] for n in range(1, NY)], f_ab, 0)
    column = t2_a[0, yh] + sum(t3_a[n] for n in range(1, NY))
    part_a = part_a - column.astype(F32) * f_ab[..., MISS:MISS + 1]
    for i in range(NZ):
        s3_ab[i, :, 0:FA] = part_a[:, FA * i:FA * (i + 1)]
        s3_ab[i, :, FA:FA + FB] = part_b[:, FB * i:FB * (i + 1)]
    ab_z = [go(s3_ab.at[(z + d) % NZ], r3_ab.at[d], z_peer(d)) for d in ORDER]

    probs = (shifted * factors[:, OWN:OWN + 1]).astype(BF16)
    p_out[...] = probs[:, VOCAB_DEV:VOCAB_CHIP]
    l_out[...] = jnp.concatenate([each, jnp.zeros((7, HALF), F32)], axis=0)
    swap = h_core + [go(p_out, p_in, partner), go(l_out, l_in, partner)]
    for copy in swap:
        copy.wait_recv()
    loss[0, 0] = (jnp.sum(each) + jnp.sum(l_in[0:1, :])) / TOKENS
    probs = jnp.concatenate([probs[:, 0:VOCAB_DEV], p_in[...]], axis=0)
    for hid, grad in ((hid_a, g_a), (hid_b, g_b), (hid_c, g_c)):
        for j in range(hid.shape[0]):
            left = hid[j].reshape(TALL, hid.shape[-1])
            grad[j] = dot(left, probs, tn).astype(BF16).reshape(grad.shape[1:])
    writes = [
        pltpu.make_async_copy(g_a, head_grad.at[:, :, 0:FA], gsem.at[0]),
        pltpu.make_async_copy(g_b, head_grad.at[:, :, FA:FA + FB], gsem.at[1]),
    ] + [
        pltpu.make_async_copy(g_c.at[i], head_grad.at[:, i, FA + FB:FEATS], gsem.at[2 + i]) for i in range(NZ)
    ]
    for write in writes:
        write.start()

    for copy in c_y:
        copy.wait_recv()
    done_c = s3_c[y][:, 0:FC] + sum(r3_c[d][:, 0:FC] for d in ORDER)
    hidden_grad[:, FA + FB:FEATS] = done_c[0:ROWS].astype(BF16)
    for copy in ab_z:
        copy.wait_recv()
    done_ab = s3_ab[z][:, 0:FA + FB] + sum(r3_ab[d][:, 0:FA + FB] for d in ORDER)
    hidden_grad[:, 0:FA + FB] = done_ab[0:ROWS].astype(BF16)

    for copy in sent:
        copy.wait_send()
    for write in writes:
        write.wait()


def per_device(hidden, head_weight, targets):
    vmem = pl.BlockSpec(memory_space=pltpu.VMEM)
    hbm = pl.BlockSpec(memory_space=pltpu.HBM)
    v = pltpu.VMEM
    dma = pltpu.SemaphoreType.DMA
    halves = (YH, NX, PAD)
    loss, head_grad, hidden_grad = pl.pallas_call(
        kernel,
        out_shape=(
            jax.ShapeDtypeStruct((1, 1), F32),
            jax.ShapeDtypeStruct((YL, NZ, FEATS, VOCAB_DEV), BF16),
            jax.ShapeDtypeStruct((ROWS, FEATS), BF16),
        ),
        in_specs=[hbm, hbm, hbm],
        out_specs=(pl.BlockSpec(memory_space=pltpu.SMEM), pl.BlockSpec(memory_space=pl.ANY), vmem),
        scratch_shapes=[
            v((ROWS, FEATS), BF16), v((1, TOKENS), jnp.int32),
            v((YL, NZ, FA, VOCAB_DEV), BF16), v((YL, NZ, FB, VOCAB_DEV), BF16), v((NZ, YL, FC, VOCAB_DEV), BF16),
            v((YL, NZ, FA, VOCAB_DEV), BF16), v((YL, NZ, FB, VOCAB_DEV), BF16), v((NZ, YL, FC, VOCAB_DEV), BF16),
            v((YL, VOCAB_CHIP, WA), BF16), v((YL, VOCAB_CHIP, WB), BF16), v((NZ, VOCAB_CHIP, WC), BF16),
            v((YL, NC) + halves + (WA,), BF16), v((YL, NC) + halves + (WB,), BF16), v((NZ, NC) + halves + (WC,), BF16),
            v((2, PAD, 128), F32), v((PAD, 128), BF16), v((PAD, 128), BF16),
            v((NZ, PAD, 128), BF16), v((NY, PAD, 128), BF16),
            v((PAD, WA), F32), v((PAD, WB), F32), v((YH, PAD, WC), F32),
            v((5, 8, HALF), F32), v((3, 8, HALF), F32), v((7, 8, HALF), F32), v((7, 8, HALF), F32),
            v((3, 8, HALF), F32), v((3, 8, HALF), F32), v((NY, 8, HALF), F32), v((7, 8, HALF), F32),
            v(halves + (128,), F32),
            v((YL,) + halves + (WA,), F32), v((YL,) + halves + (WB,), F32), v((NZ,) + halves + (WC,), F32),
            v((YL,) + halves + (WA,), BF16), v((YL,) + halves + (WB,), BF16), v((NZ,) + halves + (WC,), BF16),
            v((NX, YL, YH, PAD, WA), BF16), v((NY, NX, PAD, WB), BF16), v((NZ,) + halves + (WC,), BF16),
            v((YL,) + halves + (WA,), BF16), v((YL,) + halves + (WB,), BF16), v((NZ,) + halves + (WC,), BF16),
            v((YL,) + halves + (WA,), BF16), v((YL,) + halves + (WB,), BF16), v((NZ,) + halves + (WC,), BF16),
            v((YL,) + halves + (WA,), BF16), v((YL,) + halves + (WB,), BF16), v((NZ,) + halves + (WC,), BF16),
            v((NX, YL, YH, PAD, WA), BF16), v((NY, NX, PAD, WB), BF16), v((NZ,) + halves + (WC,), BF16),
            v((YL, YH, PAD, WA), BF16), v((NX, PAD, WB), BF16), v(halves + (WC,), BF16),
            v((NY, PAD, WA), BF16), v((NX, PAD, WB), BF16), v((NX, YH, PAD, WC), BF16),
            v((YL, YH, PAD, WA), BF16), v((NX, PAD, WB), BF16), v(halves + (WC,), BF16),
            v((NY, PAD, WA), BF16), v((NX, PAD, WB), BF16), v((NX, YH, PAD, WC), BF16),
            v((NZ, PAD, 128), F32), v((NY, PAD, 128), F32), v((NZ, PAD, 128), F32), v((NY, PAD, 128), F32),
            v((YL, NZ, FA, VOCAB_DEV), BF16), v((YL, NZ, FB, VOCAB_DEV), BF16), v((NZ, YL, FC, VOCAB_DEV), BF16),
            v((HALF, VOCAB_DEV), BF16), v((HALF, VOCAB_DEV), BF16), v((8, HALF), F32), v((8, HALF), F32),
            dma((12,)), dma((10,)), dma((208,)), dma((208,)),
        ],
        compiler_params=pltpu.CompilerParams(
            collective_id=0, has_side_effects=True, vmem_limit_bytes=44 * 2**20),
        name="output_layer",
    )(*[pltpu.with_memory_space_constraint(operand, pltpu.HBM) for operand in (
        hidden, head_weight.reshape(YL, NZ, FEATS, VOCAB_DEV), targets.reshape(1, TOKENS))])
    return loss.reshape(()), head_grad.reshape(D, VOCAB_DEV), hidden_grad


def solution(mesh):
    placed = (P("section", "tp"), P(None, ("section", "tp")), P())
    return jax.shard_map(
        per_device,
        mesh=mesh,
        in_specs=placed,
        out_specs=(P(), P(None, ("section", "tp")), P("section", "tp")),
        check_vma=False,
    )
```
